32 devices in a mesh: dp: 8 (over z, y), sp: 4 (over x, core).
Axes of the slice: x: 2, y: 2, z: 4, core: 2. Of those that a mesh axis runs over, the one named last changes fastest.
Arguments:
- hidden_in: bfloat16 [16, 1024, 1024], P('dp', 'sp'), may hold values from -6 to 6
- time_embed: bfloat16 [16, 1024], P('dp'), may hold values from -6 to 6
- seg_lengths: int32 [16, 4], P('dp'), may hold values from 1 to 1021, as said below
- ada_weight: bfloat16 [1024, 6144], P('dp', 'sp'), may hold values from -0.1875 to 0.1875
- query_weight: bfloat16 [1024, 1024], P('dp', 'sp'), may hold values from -0.1875 to 0.1875
- key_weight: bfloat16 [1024, 1024], P('dp', 'sp'), may hold values from -0.1875 to 0.1875
- value_weight: bfloat16 [1024, 1024], P('dp', 'sp'), may hold values from -0.1875 to 0.1875
- out_weight: bfloat16 [1024, 1024], P('dp', 'sp'), may hold values from -2 to 2
- up_weight: bfloat16 [1024, 2048], P('dp', 'sp'), may hold values from -0.1875 to 0.1875
- down_weight: bfloat16 [2048, 1024], P('dp', 'sp'), may hold values from -0.125 to 0.125
- out_cotangent: bfloat16 [16, 1024, 1024], P('dp', 'sp'), may hold values from -6 to 6
Outputs:
- hidden_out: bfloat16 [16, 1024, 1024], P('dp', 'sp')
- hidden_grad: bfloat16 [16, 1024, 1024], P('dp', 'sp')
- time_grad: float32 [16, 1024], P('dp')
- ada_grad: float32 [1024, 6144], P('dp', 'sp')
- query_grad: float32 [1024, 1024], P('dp', 'sp')
- key_grad: float32 [1024, 1024], P('dp', 'sp')
- value_grad: float32 [1024, 1024], P('dp', 'sp')
- out_weight_grad: float32 [1024, 1024], P('dp', 'sp')
- up_grad: float32 [1024, 2048], P('dp', 'sp')
- down_grad: float32 [2048, 1024], P('dp', 'sp')
The draws below stay inside these ranges and needn't reach their ends.
Inputs may be any that keep to these rules, and one draw needn't show every extreme that they name: `seg_lengths`: in every row the 4 lengths sum to 1024, and one segment, at a place drawn for each row, is longer than 768 frames.
All inputs are finite; a program needn't handle non-finite values.
Results may differ from the reference program's by a relative error of at most 0.019.
Values may be sent and summed in bfloat16 or wider, within the bound.
No kernel may reach another device: no remote copies, remote signals or barrier semaphores. Data moves between devices by JAX's collectives and lax.ppermute only.
A program may use at most 192 MiB of HBM per device.

```python
import jax
import jax.numpy as jnp
from jax import lax

D = 1024
HEADS = 16
HEAD_DIM = 64
FF = 2048
SEGS = 4
ROWS = 16
FRAMES = 1024
FR_LOC = 256


def draw_seg_lengths(key, part):
    key = jax.random.fold_in(key, 11)
    subkeys = jax.random.split(key, 4)
    least_long = FRAMES - FR_LOC + 1
    most_long = FRAMES - SEGS + 1
    longest = jax.random.randint(subkeys[0], (ROWS,), least_long, most_long + 1)
    chosen = jax.random.randint(subkeys[1], (), 0, ROWS)
    longest = jnp.where(jnp.arange(ROWS) == chosen, most_long, longest)
    extra = FRAMES - longest - (SEGS - 1)
    cuts = jax.random.randint(subkeys[2], (ROWS, SEGS - 2), 0, extra[:, None] + 1)
    cuts = jnp.sort(cuts, axis=1)
    edges = jnp.concatenate([jnp.zeros((ROWS, 1), jnp.int32), cuts, extra[:, None]], axis=1)
    others = edges[:, 1:] - edges[:, :-1] + 1
    place = jax.random.randint(subkeys[3], (ROWS, 1), 0, SEGS)
    slots = jnp.arange(SEGS, dtype=jnp.int32)[None, :]
    left_side = jnp.concatenate([others, jnp.zeros((ROWS, 1), jnp.int32)], axis=1)
    right_side = jnp.concatenate([jnp.zeros((ROWS, 1), jnp.int32), others], axis=1)
    lengths = jnp.where(slots < place, left_side, jnp.where(slots == place, longest[:, None], right_side))
    return lengths.astype(jnp.int32)


def level_of(rng, dims, pieces, low, top_value):
    level, own = 1.0, jax.random.fold_in(rng, 6)
    for position, blocks in pieces:
        draws = jnp.exp(jax.random.uniform(jax.random.fold_in(own, position), (blocks,), jnp.float32, low / len(pieces), top_value / len(pieces)))
        level = level * jnp.repeat(draws, dims[position] // blocks).reshape([-1 if axis == position else 1 for axis in range(len(dims))])
    return level


def centred(stream_key, shape, width, limit, cuts=(), kind=jnp.bfloat16):
    factor_of = level_of(stream_key, shape, cuts, -0.22, 0.18) if cuts else 1.0
    entries = jax.random.normal(stream_key, shape, jnp.float32) * width * factor_of
    return jnp.minimum(jnp.maximum(entries, -limit), limit).astype(kind)


def setup_inputs(seed: int = 0) -> dict:
    seeds = jax.random.split(jax.random.key(seed), 12)
    hidden_in = centred(seeds[0], (ROWS, FRAMES, D), 1.0, 6.0, ((0, 8), (1, 4)))
    time_embed = centred(seeds[1], (ROWS, D), 1.0, 6.0, ((0, 8),))
    seg_lengths = draw_seg_lengths(jax.random.fold_in(seeds[11], 71), 0)
    ada_weight = centred(seeds[3], (D, 6 * D), D ** -0.5, 0.1875, ((0, 8), (1, 4)))
    query_weight = centred(seeds[4], (D, D), D ** -0.5, 0.1875, ((0, 8), (1, 4)))
    key_weight = centred(seeds[5], (D, D), D ** -0.5, 0.1875, ((0, 8), (1, 4)))
    value_weight = centred(seeds[6], (D, D), D ** -0.5, 0.1875, ((0, 8), (1, 4)))
    out_weight = centred(seeds[7], (D, D), (max(D // 128, 1)) ** -0.5, 2.0, ((0, 8), (1, 4)))
    up_weight = centred(seeds[8], (D, FF), D ** -0.5, 0.1875, ((0, 8), (1, 4)))
    down_weight = centred(seeds[9], (FF, D), FF ** -0.5, 0.125, ((0, 8), (1, 4)))
    out_cotangent = centred(seeds[10], (ROWS, FRAMES, D), 1.0, 6.0, ((0, 8), (1, 4)))
    return dict(hidden_in=hidden_in, time_embed=time_embed, seg_lengths=seg_lengths, ada_weight=ada_weight, query_weight=query_weight, key_weight=key_weight, value_weight=value_weight, out_weight=out_weight, up_weight=up_weight, down_weight=down_weight, out_cotangent=out_cotangent)


HIGH = lax.Precision.HIGHEST

@jax.custom_vjp
def low(v):
    return lax.optimization_barrier(v.astype(jnp.bfloat16)).astype(jnp.float32)

@jax.custom_vjp
def low_back(v):
    return v

def low_keep(v):
    return (low(v), None)

def low_pass(kept, grad):
    return (grad,)

def back_keep(v):
    return (v, None)

def back_low(kept, grad):
    return (low(grad),)
low.defvjp(low_keep, low_pass)
low_back.defvjp(back_keep, back_low)

def segment_info(frame_ids, lengths):
    seg_ends = jnp.cumsum(lengths).astype(jnp.int32)
    passed = frame_ids[:, None] >= seg_ends[None, :]
    seg_ids = lax.optimization_barrier(jnp.sum(passed.astype(jnp.int32), axis=1)).astype(jnp.int32)
    positions = frame_ids - lax.optimization_barrier(jnp.sum(jnp.where(passed, lengths[None, :], 0), axis=1)).astype(jnp.int32)
    return (seg_ids, positions)

def rotary(positions):
    half_dim = HEAD_DIM // 2
    inverse = 10000.0 ** (-jnp.arange(half_dim, dtype=jnp.float32) / half_dim)
    angles = positions.astype(jnp.float32)[:, None] * inverse[None, :]
    return (jnp.cos(angles), jnp.sin(angles))

def rotate(values, cosine, sine):
    frames = values.shape[0]
    split = values.reshape(frames, HEADS, HEAD_DIM)
    half_dim = HEAD_DIM // 2
    first_half = split[..., :half_dim]
    second_half = split[..., half_dim:]
    cos_part = cosine[:, None, :]
    sin_part = sine[:, None, :]
    turned = jnp.concatenate([first_half * cos_part - second_half * sin_part, second_half * cos_part + first_half * sin_part], axis=-1)
    return turned.reshape(frames, HEADS * HEAD_DIM)

def layer_norm(values):
    centre = values - lax.optimization_barrier(jnp.mean(values, axis=-1, keepdims=True))
    spread = lax.optimization_barrier(jnp.mean(centre * centre, axis=-1, keepdims=True))
    return centre * lax.rsqrt(spread + 1e-06)

def attention(query, key, value, seg_ids):
    frames = query.shape[0]
    block_rows = min(512, frames)
    block_count = frames // block_rows
    query_blocks = query.reshape(block_count, block_rows, HEADS, HEAD_DIM)
    key_split = key.reshape(frames, HEADS, HEAD_DIM)
    value_split = value.reshape(frames, HEADS, HEAD_DIM)
    seg_blocks = seg_ids.reshape(block_count, block_rows)

    def one_block(block_pair):
        query_block, seg_block = block_pair
        scores = jnp.einsum('qhd,khd->hqk', query_block, key_split, precision=HIGH) * HEAD_DIM ** (-0.5)
        scores = low_back(scores)
        same_segment = seg_block[:, None] == seg_ids[None, :]
        scores = jnp.where(same_segment[None], scores, -1e+30)
        soft_low = low(jax.nn.softmax(scores, axis=-1))
        return jnp.einsum('hqk,khd->qhd', soft_low, value_split, precision=HIGH)
    attended = lax.map(jax.checkpoint(one_block), (query_blocks, seg_blocks))
    return attended.reshape(frames, HEADS * HEAD_DIM)

def row_forward(params, hidden, time_vec, lengths):
    ada_full, query_full, key_full, value_full, out_full, up_full, down_full = params
    frames = hidden.shape[0]
    frame_ids = jnp.arange(frames, dtype=jnp.int32)
    seg_ids, positions = segment_info(frame_ids, lengths)
    cosine, sine = rotary(positions)
    time_low = low(jax.nn.silu(time_vec))
    modulation = jnp.dot(time_low, ada_full, precision=HIGH)
    attn_shift, attn_scale, attn_gate, ffn_shift, ffn_scale, ffn_gate = jnp.split(modulation, 6)
    attn_input = low(layer_norm(hidden) * (1.0 + attn_scale) + attn_shift)
    query_rot = low(low_back(rotate(low_back(jnp.dot(attn_input, query_full, precision=HIGH)), cosine, sine)))
    key_rot = low(low_back(rotate(low_back(jnp.dot(attn_input, key_full, precision=HIGH)), cosine, sine)))
    value_low = low(low_back(jnp.dot(attn_input, value_full, precision=HIGH)))
    attended = low(low_back(attention(query_rot, key_rot, value_low, seg_ids)))
    branch_attn = low_back(jnp.dot(attended, out_full, precision=HIGH))
    mid = hidden + attn_gate * branch_attn
    ffn_input = low(layer_norm(mid) * (1.0 + ffn_scale) + ffn_shift)
    up_proj = low_back(jnp.dot(ffn_input, up_full, precision=HIGH))
    gelu_low = low(jax.nn.gelu(up_proj, approximate=True))
    branch_ffn = low_back(jnp.dot(gelu_low, down_full, precision=HIGH))
    return mid + ffn_gate * branch_ffn

def reference(hidden_in, time_embed, seg_lengths, ada_weight, query_weight, key_weight, value_weight, out_weight, up_weight, down_weight, out_cotangent):
    params = (ada_weight.astype(jnp.float32), query_weight.astype(jnp.float32), key_weight.astype(jnp.float32), value_weight.astype(jnp.float32), out_weight.astype(jnp.float32), up_weight.astype(jnp.float32), down_weight.astype(jnp.float32))
    row_function = jax.checkpoint(row_forward)

    def forward(hidden, time_vecs, weights):

        def row_step(carry, row_args):
            hidden_row, time_row, length_row = row_args
            return (carry, row_function(weights, hidden_row, time_row, length_row))
        _, rows_out = lax.scan(row_step, None, (hidden, time_vecs, seg_lengths))
        return rows_out
    result, pullback = jax.vjp(forward, hidden_in.astype(jnp.float32), time_embed.astype(jnp.float32), params)
    d_hidden, d_time, d_params = pullback(out_cotangent.astype(jnp.float32))
    return (result.astype(jnp.bfloat16), d_hidden.astype(jnp.bfloat16), d_time, d_params[0], d_params[1], d_params[2], d_params[3], d_params[4], d_params[5], d_params[6])
```

```python
import functools

import jax
import jax.numpy as jnp
from jax import lax
from jax.experimental import pallas as pl
from jax.experimental.pallas import tpu as pltpu
from jax.sharding import Mesh
from jax.sharding import PartitionSpec as P

HEAD_DIM = 64
PAIR = 2 * HEAD_DIM
LOG2E = 1.4426950408889634
LN2 = 0.6931471805599453
HIGH = lax.Precision.HIGHEST
F32 = jnp.float32
BF = jnp.bfloat16
NN = (((1,), (0,)), ((), ()))
NT = (((1,), (1,)), ((), ()))
TN = (((0,), (0,)), ((), ()))
ANY = pl.BlockSpec(memory_space=pl.ANY)
VM = pl.BlockSpec(memory_space=pltpu.VMEM)
MIB = 1 << 20


def dot(left, right, dims=NN):
    return lax.dot_general(left, right, dims, preferred_element_type=F32)


def sds(shape, dtype):
    return jax.ShapeDtypeStruct(shape, dtype)


def call(kernel, name, outs, in_specs, out_specs, args, grid=(), scratch=(), flops=0, vmem=40):
    moved = sum(x.size * x.dtype.itemsize for x in args)
    moved += sum(x.size * x.dtype.itemsize for x in outs)
    return pl.pallas_call(
        kernel,
        name=name,
        grid=grid,
        in_specs=in_specs,
        out_specs=out_specs,
        out_shape=outs,
        scratch_shapes=scratch,
        compiler_params=pltpu.CompilerParams(vmem_limit_bytes=vmem * MIB),
        cost_estimate=pl.CostEstimate(flops=flops, bytes_accessed=moved, transcendentals=0),
    )(*args)


def rows_of(block, width):
    return pl.BlockSpec((block, width), lambda i: (i, 0))


def fixed(*shape):
    return pl.BlockSpec(shape, lambda *_: (0,) * len(shape))


def swap(value, axis, offset=1):
    count = lax.axis_size(axis)
    return lax.ppermute(value, axis, [(i, i ^ offset) for i in range(count)])


def doubled(value, axes):
    for axis in axes:
        step = 1
        while step < lax.axis_size(axis):
            value = jnp.concatenate([value, swap(value, axis, step)], axis=0)
            step *= 2
    return value


def halved(value, axes):
    for axis in reversed(axes):
        step = lax.axis_size(axis) // 2
        while step:
            half = value.shape[0] // 2
            value = value[:half] + swap(value[half:], axis, step)
            step //= 2
    return value


def gather_blocks(shard):
    line = lax.axis_size("a")
    half = line // 2
    first = jnp.stack([shard] + [swap(shard, "a", d) for d in range(1, line)])
    blocks = {(0, 0): [(0, first)], (0, 1): [(0, swap(first, "r"))]}
    for dy in range(1, lax.axis_size("b")):
        blocks[(dy, 0)] = [(0, swap(first, "b", dy))]
    for dy in range(1, lax.axis_size("b")):
        blocks[(dy, 1)] = [
            (0, swap(blocks[(dy, 0)][0][1][:half], "r")),
            (half, swap(blocks[(0, 1)][0][1][half:], "b", dy)),
        ]
    return blocks


def scatter_blocks(parts):
    line = lax.axis_size("a")
    half = line // 2
    count_b = lax.axis_size("b")
    get = lambda dy, dr: sum(part[dy, dr].astype(F32) for part in parts)
    first_r = {}
    first_b = {}
    for dy in range(1, count_b):
        corner = get(dy, 1).astype(BF)
        first_r[dy] = swap(corner[:half], "r")
        first_b[dy] = swap(corner[half:], "b", dy)
    side = get(0, 1)
    extra = sum(part.astype(F32) for part in first_b.values())
    side = jnp.concatenate([side[:half], side[half:] + extra]).astype(BF)
    total = get(0, 0) + swap(side, "r").astype(F32)
    for dy in range(1, count_b):
        side = get(dy, 0)
        side = jnp.concatenate([side[:half] + first_r[dy].astype(F32), side[half:]]).astype(BF)
        total = total + swap(side, "b", dy).astype(F32)
    final = total[0]
    sent = total.astype(BF)
    for dz in range(1, line):
        final = final + swap(sent[dz], "a", dz).astype(F32)
    return final


def assemble_kernel(meta, keep_r, count_b, *refs):
    ins, out, sems = refs[: len(meta)], refs[len(meta)], refs[len(meta) + 1]
    at_a, at_b, at_r = (lax.axis_index(name) for name in ("a", "b", "r"))
    copies = []
    for ref, (dy, dr, dz0) in zip(ins, meta):
        depth = ref.shape[1]
        for t in range(ref.shape[0]):
            row = pl.multiple_of(((at_a ^ (dz0 + t)) * count_b + (at_b ^ dy)) * depth, depth)
            place = out.at[at_r ^ dr] if keep_r else out
            copy = pltpu.make_async_copy(
                ref.at[t], place.at[pl.ds(row, depth), :], sems.at[len(copies)]
            )
            copy.start()
            copies.append(copy)
    for copy in copies:
        copy.wait()


def assemble(blocks, rights, name):
    count_a, count_b = lax.axis_size("a"), lax.axis_size("b")
    arrays, meta = [], []
    for (dy, dr), pieces in blocks.items():
        if dr in rights:
            for dz0, piece in pieces:
                arrays.append(piece)
                meta.append((dy, dr, dz0))
    _, depth, width = arrays[0].shape
    keep_r = len(rights) > 1
    shape = (count_a * count_b * depth, width)
    if keep_r:
        shape = (len(rights),) + shape
    total = sum(x.shape[0] for x in arrays)
    return call(
        functools.partial(assemble_kernel, tuple(meta), keep_r, count_b),
        name,
        [sds(shape, BF)],
        [ANY] * len(arrays),
        [ANY],
        arrays,
        scratch=[pltpu.SemaphoreType.DMA((total,))],
    )[0]


def normed(values):
    centre = values - jnp.mean(values, axis=-1, keepdims=True)
    spread = lax.rsqrt(jnp.mean(centre * centre, axis=-1, keepdims=True) + 1e-06)
    return centre * spread, spread


def norm_back(grad, norm, spread):
    return spread * (
        grad
        - jnp.mean(grad, axis=-1, keepdims=True)
        - norm * jnp.mean(grad * norm, axis=-1, keepdims=True)
    )


def attn_input_kernel(x_ref, mod_ref, out_ref):
    norm, _ = normed(x_ref[...].astype(F32))
    out_ref[...] = (norm * (1.0 + mod_ref[1:2, :]) + mod_ref[0:1, :]).astype(BF)


def lane_ids(width=PAIR):
    return lax.broadcasted_iota(jnp.int32, (1, width), 1)


def turn(values, cosine, sine):
    early = lane_ids() % HEAD_DIM < HEAD_DIM // 2
    step = HEAD_DIM // 2
    other = jnp.where(early, pltpu.roll(values, PAIR - step, 1), pltpu.roll(values, step, 1))
    return values * cosine + other * sine


def qkv_kernel(x_ref, w_ref, cos_ref, sin_ref, q_ref, k_ref, v_ref):
    width = q_ref.shape[1]
    both = dot(x_ref[...], w_ref[...])
    cosine, sine = cos_ref[...], sin_ref[...]
    for lane in range(0, width, PAIR):
        q_ref[:, lane : lane + PAIR] = (
            turn(both[:, lane : lane + PAIR], cosine, sine) * (HEAD_DIM**-0.5 * LOG2E)
        ).astype(BF)
        at = width + lane
        k_ref[:, lane : lane + PAIR] = turn(both[:, at : at + PAIR], cosine, sine).astype(BF)
    v_ref[...] = both[:, 2 * width :].astype(BF)


def attend_kernel(block, q_ref, k_ref, v_ref, aq_ref, ak_ref, o_ref, lse_ref):
    frames = q_ref.shape[0]
    keys = jnp.concatenate([k_ref[...], ak_ref[...]], axis=1)
    values = v_ref[...]
    low = lane_ids() < HEAD_DIM
    zero, one = jnp.zeros((), BF), jnp.ones((), BF)

    def attend(with_max):
        for start in range(0, frames, block):
            rows = pl.ds(start, block)
            query, extra = q_ref[rows, :], aq_ref[rows, :]
            outs, logs = [], []
            for head in range(2):
                mine = low if head == 0 else jnp.logical_not(low)
                left = jnp.concatenate([jnp.where(mine, query, zero), extra], axis=1)
                scores = dot(left, keys, NT)
                if with_max:
                    top = jnp.max(scores, axis=1, keepdims=True)
                    scores = scores - top
                weights = jnp.exp2(scores).astype(BF)
                mixed = dot(weights, jnp.where(mine, values, one))
                outs.append(mixed / pltpu.roll(mixed, HEAD_DIM, 1))
                log = jnp.log2(jnp.maximum(mixed, 1e-30))
                logs.append(log + top if with_max else log)
            o_ref[rows, :] = jnp.where(low, outs[0], outs[1]).astype(BF)
            lse_ref[rows, :] = jnp.where(low, logs[1], logs[0])

    query_all, key_all = q_ref[...].astype(F32), k_ref[...].astype(F32)
    bound = jnp.max(jnp.sum(query_all * query_all, axis=1)) * jnp.max(
        jnp.sum(key_all * key_all, axis=1)
    )
    small = bound < 3600.0

    @pl.when(small)
    def _():
        attend(False)

    @pl.when(jnp.logical_not(small))
    def _():
        attend(True)


def split3(values):
    first = values.astype(BF)
    rest = values - first.astype(F32)
    second = rest.astype(BF)
    return first, second, (rest - second.astype(F32)).astype(BF)


def placed(parts, start, base):
    lanes = lane_ids()
    for i, part in enumerate(parts):
        base = jnp.where(lanes == start + i, part, base)
    return base


def attend_back_kernel(block, parts, q_ref, k_ref, v_ref, aq_ref, ak_ref, o_ref, lse_ref, cos_ref, sin_ref, *refs):
    do_refs, (dq_ref, dk_ref, dv_ref) = refs[:parts], refs[parts:]
    frames = q_ref.shape[0]
    lanes = lane_ids()
    low = lanes < HEAD_DIM
    zero = jnp.zeros((), BF)
    query, extra, lse = q_ref[...], aq_ref[...], lse_ref[...]
    grad = jnp.concatenate([ref[...] for ref in do_refs], axis=0)
    product = grad.astype(F32) * o_ref[...].astype(F32)
    queries, grads, lefts, rights = [], [], [], []
    for head in range(2):
        mine = low if head == 0 else jnp.logical_not(low)
        log = lse[:, HEAD_DIM : HEAD_DIM + 1] if head == 0 else lse[:, 0:1]
        queries.append(jnp.where(mine, query, zero))
        lefts.append(jnp.concatenate([queries[-1], placed(split3(-log), 8, extra)], axis=1))
        inner = -jnp.sum(jnp.where(mine, product, 0.0), axis=1, keepdims=True)
        grads.append(jnp.where(mine, grad, zero))
        tail = placed(split3(inner), 0, jnp.zeros((frames, PAIR), BF))
        rights.append(jnp.concatenate([grads[-1], tail], axis=1))
    ones = jnp.where(lanes < 3, 1.0, 0.0).astype(BF)
    dq_turned = jnp.zeros((PAIR, frames), F32)
    for start in range(0, frames, block):
        rows = pl.ds(start, block)
        key, value = k_ref[rows, :], v_ref[rows, :]
        keys = jnp.concatenate([key, ak_ref[rows, :]], axis=1)
        values = jnp.concatenate([value, jnp.broadcast_to(ones, value.shape)], axis=1)
        dv, dk = 0.0, 0.0
        for head in range(2):
            mine = low if head == 0 else jnp.logical_not(low)
            soft = jnp.exp2(dot(keys, lefts[head], NT))
            d_scores = (soft * dot(values, rights[head], NT)).astype(BF)
            dv = dv + dot(soft.astype(BF), grads[head])
            dk = dk + dot(d_scores, queries[head])
            dq_turned = dq_turned + dot(jnp.where(mine, key, zero), d_scores, TN)
        dv_ref[rows, :] = dv.astype(BF)
        dk_ref[rows, :] = turn(dk * LN2, cos_ref[rows, :], -sin_ref[rows, :]).astype(BF)
    dq = dq_turned.T * HEAD_DIM**-0.5
    dq_ref[...] = turn(dq, cos_ref[...], -sin_ref[...]).astype(BF)


def column(dr, dp):
    at_r, at_p = lax.axis_index("r"), lax.axis_index("p")
    return (at_r ^ dr) * lax.axis_size("p") + (at_p ^ dp)


def lanes_of(index, width):
    return pl.ds(pl.multiple_of(index * width, width), width)


def column_blocks(weight_refs):
    count_r = lax.axis_size("r")
    count_p = lax.axis_size("p")
    at_p = lax.axis_index("p")
    for dp, ref in enumerate(weight_refs):
        for r in range(count_r):
            yield r * count_p + (at_p ^ dp), ref, r


def out_kernel(count_p, x_ref, mod_ref, *refs):
    att_refs = refs[: 2 * count_p]
    w_refs = refs[2 * count_p : 3 * count_p]
    branch_ref, mid_ref, ffn_ref, att_ref, sum_ref = refs[3 * count_p :]
    width = att_refs[0].shape[1]
    for dp in range(count_p):
        for dr in range(2):
            att_ref[:, lanes_of(column(dr, dp), width)] = att_refs[2 * dp + dr][...]
    att = att_ref[...]
    for j, ref, r in column_blocks(w_refs):
        sum_ref[:, lanes_of(j, ref.shape[2])] = dot(att, ref[r])
    branch = sum_ref[...]
    branch_ref[...] = branch.astype(BF)
    mid = x_ref[...].astype(F32) + mod_ref[2:3, :] * branch
    mid_ref[...] = mid
    norm, _ = normed(mid)
    ffn_ref[...] = (norm * (1.0 + mod_ref[4:5, :]) + mod_ref[3:4, :]).astype(BF)


def up_kernel(count_p, x_ref, *refs):
    w_refs, (gelu_ref, slope_ref) = refs[:count_p], refs[count_p:]
    x = x_ref[...]
    root = 0.7978845608028654
    for j, ref, r in column_blocks(w_refs):
        up = dot(x, ref[r])
        square = up * up
        tanh = jnp.tanh(root * (up + 0.044715 * up * square))
        half = 0.5 * (1.0 + tanh)
        at = lanes_of(j, ref.shape[2])
        gelu_ref[:, at] = (up * half).astype(BF)
        slope = half + 0.5 * up * (1.0 - tanh * tanh) * (root * (1.0 + 0.134145 * square))
        slope_ref[:, at] = slope.astype(BF)


def down_kernel(count_p, gelu_ref, mid_ref, cot_ref, mod_ref, *refs):
    w_refs = refs[:count_p]
    out_ref, dbf_ref, dgate_ref, sum_ref = refs[count_p:]
    gelu = gelu_ref[...]
    for j, ref, r in column_blocks(w_refs):
        sum_ref[:, lanes_of(j, ref.shape[2])] = dot(gelu, ref[r])
    branch = sum_ref[...]
    gate = mod_ref[5:6, :]
    out_ref[...] = (mid_ref[...] + gate * branch).astype(BF)
    cot = cot_ref[...].astype(F32)
    dbf_ref[...] = (cot * gate).astype(BF)

    @pl.when(pl.program_id(0) == 0)
    def _():
        dgate_ref[...] = jnp.zeros_like(dgate_ref)

    dgate_ref[...] += jnp.sum(cot * branch, axis=0, keepdims=True)


def turned_dot(x_ref, w_refs):
    total = 0.0
    for j, ref, r in column_blocks(w_refs):
        total = total + dot(x_ref[:, lanes_of(j, ref.shape[2])], ref[r], NT)
    return total


def d_up_kernel(count_p, dbf_ref, slope_ref, *refs):
    w_refs, (out_ref,) = refs[:count_p], refs[count_p:]
    out_ref[...] = (turned_dot(dbf_ref, w_refs) * slope_ref[...].astype(F32)).astype(BF)


def mid_back_kernel(count_p, d_up_ref, mid_ref, cot_ref, branch_ref, mod_ref, *refs):
    up_refs, o_refs = refs[:count_p], refs[count_p : 2 * count_p]
    d_mid_ref, dba_ref, sums_ref = refs[2 * count_p : 2 * count_p + 3]
    att_refs, att_all = refs[2 * count_p + 3 : -1], refs[-1]
    d_in = turned_dot(d_up_ref, up_refs)
    norm, spread = normed(mid_ref[...])

    @pl.when(pl.program_id(0) == 0)
    def _():
        sums_ref[...] = jnp.zeros_like(sums_ref)

    sums_ref[1:2, :] += jnp.sum(d_in, axis=0, keepdims=True)
    sums_ref[2:3, :] += jnp.sum(d_in * norm, axis=0, keepdims=True)
    d_mid = cot_ref[...].astype(F32) + norm_back(d_in * (1.0 + mod_ref[4:5, :]), norm, spread)
    d_mid_ref[...] = d_mid
    sums_ref[0:1, :] += jnp.sum(d_mid * branch_ref[...].astype(F32), axis=0, keepdims=True)
    dba_ref[...] = (d_mid * mod_ref[2:3, :]).astype(BF)
    att_all[...] = turned_dot(dba_ref, o_refs)
    for dp in range(count_p):
        for dr in range(2):
            ref = att_refs[2 * dp + dr]
            ref[...] = att_all[:, lanes_of(column(dr, dp), ref.shape[1])].astype(BF)


def weight_grad_kernel(count_x, places, sizes, count_y, *refs):
    x_refs, y_refs = refs[:count_x], refs[count_x : count_x + count_y]
    out_refs = refs[count_x + count_y : -2]
    held, sems = refs[-2:]
    count_a, count_b = sizes
    at_a, at_b = lax.axis_index("a"), lax.axis_index("b")
    depth, width = out_refs[0].shape[-2:]
    x = x_refs[0][...] if count_x == 1 else jnp.concatenate([ref[...] for ref in x_refs], axis=1)
    copies = []
    for slot, (dp, dr) in enumerate(places):
        if dr is None:
            for t, ref in enumerate(y_refs):
                part = ref.shape[1]
                held[slot, :, t * part : (t + 1) * part] = dot(x, ref[...], TN).astype(BF)
        else:
            held[slot] = dot(x, y_refs[0][:, lanes_of(column(dr, dp), width)], TN).astype(BF)
        for dy in range(count_b):
            for dz in range(count_a):
                row = pl.multiple_of(((at_a ^ dz) * count_b + (at_b ^ dy)) * depth, depth)
                place = out_refs[dp].at[dy, dz] if dr is None else out_refs[dp].at[dy, dr, dz]
                copy = pltpu.make_async_copy(
                    held.at[slot, pl.ds(row, depth), :], place, sems.at[len(copies)]
                )
                copy.start()
                copies.append(copy)
    for copy in copies:
        copy.wait()


def weight_grad(name, x, ys, split):
    count_a, count_b = lax.axis_size("a"), lax.axis_size("b")
    count_p = lax.axis_size("p") if split else 1
    depth = x.shape[1] // (count_a * count_b)
    width = sum(y.shape[1] for y in ys)
    if split:
        width //= 2 * count_p
        places = [(dp, dr) for dp in reversed(range(count_p)) for dr in reversed(range(2))]
        outs = [sds((count_b, 2, count_a, depth, width), BF)] * count_p
    else:
        places = [(0, None)]
        outs = [sds((count_b, count_a, depth, width), BF)]
    return call(
        functools.partial(weight_grad_kernel, 1, tuple(places), (count_a, count_b), len(ys)),
        name,
        outs,
        [VM] * (1 + len(ys)),
        [ANY] * count_p,
        [x, *ys],
        scratch=[
            pltpu.VMEM((len(places), x.shape[1], width), BF),
            pltpu.SemaphoreType.DMA((len(places) * count_a * count_b,)),
        ],
        flops=2 * x.size * sum(y.shape[1] for y in ys),
    )


def qkv_turned(refs, ws):
    total = 0.0
    for t, ref in enumerate(refs):
        width = ref.shape[1]
        at = (t % 3) * width
        total = total + dot(ref[...], ws[t // 3][:, at : at + width], NT)
    return total


def d_attn_send_kernel(*refs):
    refs[-1][...] = qkv_turned(refs[:6], refs[6:8]).astype(BF)


def hidden_back_kernel(count_recv, *refs):
    d_refs, ws = refs[:6], refs[6:8]
    recv = refs[8 : 8 + count_recv]
    x_ref, d_mid_ref, mod_ref, out_ref, sums_ref = refs[8 + count_recv :]
    d_in = qkv_turned(d_refs, ws)
    for ref in recv:
        d_in = d_in + ref[...].astype(F32)
    norm, spread = normed(x_ref[...].astype(F32))

    @pl.when(pl.program_id(0) == 0)
    def _():
        sums_ref[...] = jnp.zeros_like(sums_ref)

    sums_ref[0:1, :] += jnp.sum(d_in, axis=0, keepdims=True)
    sums_ref[1:2, :] += jnp.sum(d_in * norm, axis=0, keepdims=True)
    back = norm_back(d_in * (1.0 + mod_ref[1:2, :]), norm, spread)
    out_ref[...] = (d_mid_ref[...] + back).astype(BF)


def exchange_rows(rows):
    at_r = lax.axis_index("r")
    own = lax.dynamic_index_in_dim(rows, at_r, keepdims=False)
    other = swap(lax.dynamic_index_in_dim(rows, 1 - at_r, keepdims=False), "r")
    return jnp.concatenate([own, other], axis=0)


def restore_rows(frames):
    half = frames.shape[0] // 2
    own, other = frames[:half], swap(frames[half:], "r")
    return jnp.where(lax.axis_index("r") == 0, jnp.stack([own, other]), jnp.stack([other, own]))


def by_columns(parts):
    count = parts.shape[0]
    me = lax.axis_index("r") * lax.axis_size("p") + lax.axis_index("p")
    step = 1
    while step < count:
        shape = (count // (2 * step), 2, step) + parts.shape[1:]
        grouped = parts.reshape(shape)
        flipped = jnp.flip(grouped, axis=1)
        parts = jnp.where((me & step) != 0, flipped, grouped).reshape(parts.shape)
        step *= 2
    return parts


def local(
    hidden_in,
    time_embed,
    seg_lengths,
    ada_weight,
    query_weight,
    key_weight,
    value_weight,
    out_weight,
    up_weight,
    down_weight,
    out_cotangent,
):
    count_a, count_b, count_p = (lax.axis_size(name) for name in ("a", "b", "p"))
    at_a, at_b, at_r, at_p = (lax.axis_index(name) for name in ("a", "b", "r", "p"))
    width = hidden_in.shape[2]
    block = hidden_in.shape[1]
    mine = 2 * block
    frames = mine * count_p
    heads_wide = query_weight.shape[1]
    ffn = up_weight.shape[1] * 2 * count_p
    others = range(1, count_p)

    qkv_blocks = gather_blocks(jnp.concatenate([query_weight, key_weight, value_weight], axis=1))
    hidden = exchange_rows(hidden_in)
    hidden_all = jnp.concatenate([hidden] + [swap(hidden, "p", dp) for dp in others], axis=0)

    time_vecs = time_embed.astype(F32)
    time_low = jax.nn.silu(time_vecs).astype(BF)
    low_all = doubled(time_low, ("b", "a"))
    ada_rows = ada_weight.shape[0]
    low_mine = lax.dynamic_slice_in_dim(
        low_all, (at_a * count_b + at_b) * ada_rows, ada_rows, axis=1
    )
    part = jnp.dot(low_mine, ada_weight, preferred_element_type=F32)
    part = halved(part, ("b", "a"))
    part = jnp.stack(
        [
            lax.dynamic_index_in_dim(part, at_r, keepdims=False),
            swap(lax.dynamic_index_in_dim(part, 1 - at_r, keepdims=False), "r"),
        ]
    )
    parts = [part] + [swap(part, "p", dp) for dp in others]
    parts = jnp.stack(parts, axis=1).reshape(2 * count_p, -1)
    modulation = by_columns(parts).reshape(6, width)

    lengths = lax.dynamic_index_in_dim(seg_lengths, at_r, keepdims=False)
    frame_ids = jnp.concatenate(
        [
            ((at_r ^ dr) * count_p + (at_p ^ dp)) * block + jnp.arange(block, dtype=jnp.int32)
            for dp in range(count_p)
            for dr in range(2)
        ]
    )
    passed = frame_ids[:, None] >= jnp.cumsum(lengths)[None, :]
    seg_ids = jnp.sum(passed.astype(jnp.int32), axis=1)
    positions = frame_ids - jnp.sum(jnp.where(passed, lengths[None, :], 0), axis=1)
    half_dim = HEAD_DIM // 2
    lane = jnp.arange(PAIR, dtype=jnp.int32)
    inverse = 10000.0 ** (-(lane % half_dim).astype(F32) / half_dim)
    angles = positions.astype(F32)[:, None] * inverse[None, :]
    cosine = jnp.cos(angles)
    sine = jnp.where(lane % HEAD_DIM < half_dim, -1.0, 1.0)[None, :] * jnp.sin(angles)
    segs = seg_lengths.shape[1]
    same = seg_ids[:, None] == lane[None, :]
    real = (lane < segs)[None, :]
    extra_q = jnp.where(real & ~same, -1e30, 0.0).astype(BF)
    extra_k = jnp.where((real & same) | ((lane >= 8) & (lane < 11))[None, :], 1.0, 0.0).astype(BF)

    tile = 256
    grid = (frames // tile,)
    attn_input = call(
        attn_input_kernel,
        "attn_input",
        [sds((frames, width), BF)],
        [rows_of(tile, width), fixed(6, width)],
        [rows_of(tile, width)],
        [hidden_all, modulation],
        grid=grid,
    )[0]

    q_w = [assemble(qkv_blocks, (dr,), "assemble_qkv") for dr in range(2)]
    pair_block = pl.BlockSpec((frames, PAIR), lambda i: (0, i))
    pair_fixed = fixed(frames, PAIR)
    qkv, attended = [], []
    for dr in range(2):
        heads = sds((frames, heads_wide), BF)
        qkv.append(
            call(
                qkv_kernel,
                "qkv",
                [heads] * 3,
                [rows_of(tile, width), fixed(width, 3 * heads_wide)] + [rows_of(tile, PAIR)] * 2,
                [rows_of(tile, heads_wide)] * 3,
                [attn_input, q_w[dr], cosine, sine],
                grid=grid,
                flops=6 * frames * width * heads_wide,
            )
        )
        attended.append(
            call(
                functools.partial(attend_kernel, min(256, frames)),
                "attend",
                [heads, sds((frames, heads_wide), F32)],
                [pair_block] * 3 + [pair_fixed] * 2,
                [pair_block] * 2,
                [*qkv[dr], extra_q, extra_k],
                grid=(heads_wide // PAIR,),
                flops=frames * frames * heads_wide * 16,
            )
        )

    def with_others(blocks, name):
        whole = assemble(blocks, (0, 1), name)
        return [whole] + [swap(whole, "p", dp) for dp in others]

    out_w = with_others(gather_blocks(out_weight), "assemble_out")
    up_w = with_others(gather_blocks(up_weight), "assemble_up")
    down_w = with_others(gather_blocks(down_weight), "assemble_down")
    cotangent = exchange_rows(out_cotangent)

    att = [attended[dr][0][:mine] for dr in range(2)]
    for dp in others:
        att += [swap(attended[dr][0][dp * mine : (dp + 1) * mine], "p", dp) for dr in range(2)]
    tile = min(256, mine)
    grid = (mine // tile,)
    full = rows_of(tile, width)
    wide = rows_of(tile, ffn)
    mod_spec = fixed(6, width)
    out_specs = [fixed(*w.shape) for w in out_w]
    up_specs = [fixed(*w.shape) for w in up_w]
    down_specs = [fixed(*w.shape) for w in down_w]
    branch_attn, mid, ffn_input = call(
        functools.partial(out_kernel, count_p),
        "attn_out",
        [sds((mine, width), BF), sds((mine, width), F32), sds((mine, width), BF)],
        [full, mod_spec] + [rows_of(tile, heads_wide)] * (2 * count_p) + out_specs,
        [full] * 3,
        [hidden, modulation, *att, *out_w],
        grid=grid,
        scratch=[pltpu.VMEM((tile, width), BF), pltpu.VMEM((tile, width), F32)],
        flops=2 * mine * width * width,
    )
    gelu_low, slope = call(
        functools.partial(up_kernel, count_p),
        "ffn_up",
        [sds((mine, ffn), BF)] * 2,
        [full] + up_specs,
        [wide] * 2,
        [ffn_input, *up_w],
        grid=grid,
        flops=2 * mine * width * ffn,
    )
    hidden_out, d_branch_ffn, d_ffn_gate = call(
        functools.partial(down_kernel, count_p),
        "ffn_down",
        [sds((mine, width), BF), sds((mine, width), BF), sds((1, width), F32)],
        [wide, full, full, mod_spec] + down_specs,
        [full, full, fixed(1, width)],
        [gelu_low, mid, cotangent, modulation, *down_w],
        grid=grid,
        scratch=[pltpu.VMEM((tile, width), F32)],
        flops=2 * mine * width * ffn,
    )
    hidden_out = restore_rows(hidden_out)

    def reduce_split(parts):
        own = [parts[0]] + [swap(parts[dp], "p", dp) for dp in others]
        return scatter_blocks(own)

    down_grad = reduce_split(weight_grad("down_grad", gelu_low, [d_branch_ffn], True))
    d_up = call(
        functools.partial(d_up_kernel, count_p),
        "d_up",
        [sds((mine, ffn), BF)],
        [full, wide] + down_specs,
        [wide],
        [d_branch_ffn, slope, *down_w],
        grid=grid,
        flops=2 * mine * width * ffn,
    )[0]
    up_grad = reduce_split(weight_grad("up_grad", ffn_input, [d_up], True))
    d_mid, d_branch_attn, sums_mid, *d_att = call(
        functools.partial(mid_back_kernel, count_p),
        "mid_back",
        [sds((mine, width), F32), sds((mine, width), BF), sds((3, width), F32)]
        + [sds((mine, heads_wide), BF)] * (2 * count_p),
        [wide, full, full, full, mod_spec] + up_specs + out_specs,
        [full, full, fixed(3, width)] + [rows_of(tile, heads_wide)] * (2 * count_p),
        [d_up, mid, cotangent, branch_attn, modulation, *up_w, *out_w],
        grid=grid,
        scratch=[pltpu.VMEM((tile, width), F32)],
        flops=2 * mine * width * (ffn + width),
    )
    att_all = [att[2 * dp + dr] for dp in range(count_p) for dr in range(2)]
    att_cols = by_columns(jnp.stack([att_all[2 * dp + dr] for dr in range(2) for dp in range(count_p)]))
    att_full = jnp.moveaxis(att_cols, 0, 1).reshape(mine, width)
    out_grad = reduce_split(weight_grad("out_grad", att_full, [d_branch_attn], True))

    d_qkv = [None, None]
    qkv_final = [None, None]
    grad_parts = [None, None]
    for dr in (1, 0):
        d_heads = [d_att[dr]] + [swap(d_att[2 * dp + dr], "p", dp) for dp in others]
        d_qkv[dr] = call(
            functools.partial(attend_back_kernel, min(512, frames), count_p),
            "attend_back",
            [sds((frames, heads_wide), BF)] * 3,
            [pair_block] * 3
            + [pair_fixed] * 2
            + [pair_block] * 2
            + [pair_fixed] * 2
            + [pl.BlockSpec((mine, PAIR), lambda i: (0, i))] * count_p,
            [pair_block] * 3,
            [*qkv[dr], extra_q, extra_k, *attended[dr], cosine, sine, *d_heads],
            grid=(heads_wide // PAIR,),
            flops=frames * frames * heads_wide * 40,
            vmem=56,
        )
        grad_parts[dr] = weight_grad("qkv_grad", attn_input, d_qkv[dr], False)[0]
    both = jnp.stack(grad_parts, axis=1)
    qkv_grad = scatter_blocks([both])

    six = [*d_qkv[0], *d_qkv[1]]
    w_specs = [fixed(width, 3 * heads_wide)] * 2
    received = []
    for dp in others:
        first = dp * mine // tile
        part_spec = pl.BlockSpec((tile, heads_wide), lambda i, first=first: (i + first, 0))
        sent = call(
            d_attn_send_kernel,
            "d_attn_send",
            [sds((mine, width), BF)],
            [part_spec] * 6 + w_specs,
            [full],
            [*six, *q_w],
            grid=grid,
            flops=12 * mine * width * heads_wide,
        )[0]
        received.append(swap(sent, "p", dp))
    hidden_grad, sums_in = call(
        functools.partial(hidden_back_kernel, len(received)),
        "hidden_back",
        [sds((mine, width), BF), sds((2, width), F32)],
        [rows_of(tile, heads_wide)] * 6 + w_specs + [full] * len(received) + [full, full, mod_spec],
        [full, fixed(2, width)],
        [*six, *q_w, *received, hidden, d_mid, modulation],
        grid=grid,
        flops=12 * mine * width * heads_wide,
    )
    hidden_grad = restore_rows(hidden_grad)

    d_mod = jnp.concatenate([sums_in, sums_mid, d_ffn_gate], axis=0).reshape(2, count_p, -1)
    d_cols = lax.dynamic_index_in_dim(d_mod, at_p, axis=1, keepdims=False)
    for dp in others:
        d_cols = d_cols + swap(
            lax.dynamic_index_in_dim(d_mod, at_p ^ dp, axis=1, keepdims=False), "p", dp
        )
    own = lax.dynamic_index_in_dim(d_cols, at_r, keepdims=False)
    other = swap(lax.dynamic_index_in_dim(d_cols, 1 - at_r, keepdims=False), "r")
    d_rows = jnp.where(at_r == 0, jnp.stack([own, other]), jnp.stack([other, own]))
    d_rows = doubled(d_rows, ("b", "a"))
    ada_grad = jnp.dot(low_mine.astype(F32).T, d_rows, precision=HIGH)
    d_low = jnp.dot(d_rows, ada_weight.astype(F32).T, precision=HIGH)
    d_low = d_low + swap(d_low, "r")
    step = 1
    while step < count_p:
        d_low = d_low + swap(d_low, "p", step)
        step *= 2
    spread = jnp.zeros((d_low.shape[0], width), F32)
    spread = lax.dynamic_update_slice_in_dim(
        spread, d_low, (at_a * count_b + at_b) * ada_rows, axis=1
    )
    d_time_low = halved(spread, ("b", "a"))
    _, silu_pullback = jax.vjp(jax.nn.silu, time_vecs)
    time_grad = silu_pullback(d_time_low)[0]

    return (
        hidden_out,
        hidden_grad,
        time_grad,
        ada_grad,
        qkv_grad[:, :heads_wide],
        qkv_grad[:, heads_wide : 2 * heads_wide],
        qkv_grad[:, 2 * heads_wide :],
        out_grad,
        up_grad,
        down_grad,
    )


def solution(mesh):
    count_dp, count_sp = mesh.shape["dp"], mesh.shape["sp"]
    fine = Mesh(mesh.devices.reshape(4, count_dp // 4, 2, count_sp // 2), ("a", "b", "r", "p"))
    dp, sp = ("a", "b"), ("r", "p")
    in_specs = (
        (P(dp, sp, None), P(dp, None), P(dp, None)) + (P(dp, sp),) * 7 + (P(dp, sp, None),)
    )
    out_specs = (P(dp, sp, None), P(dp, sp, None), P(dp, None)) + (P(dp, sp),) * 7
    return jax.shard_map(local, mesh=fine, in_specs=in_specs, out_specs=out_specs, check_vma=False)
```

```python
import functools

import jax
import jax.numpy as jnp
from jax import lax
from jax.experimental import pallas as pl
from jax.experimental.pallas import tpu as pltpu
from jax.sharding import Mesh
from jax.sharding import PartitionSpec as P

HEAD_DIM = 64
PAIR = 2 * HEAD_DIM
LOG2E = 1.4426950408889634
LN2 = 0.6931471805599453
HIGH = lax.Precision.HIGHEST
F32 = jnp.float32
BF = jnp.bfloat16
NN = (((1,), (0,)), ((), ()))
NT = (((1,), (1,)), ((), ()))
TN = (((0,), (0,)), ((), ()))
ANY = pl.BlockSpec(memory_space=pl.ANY)
VM = pl.BlockSpec(memory_space=pltpu.VMEM)
MIB = 1 << 20


def dot(left, right, dims=NN):
    return lax.dot_general(left, right, dims, preferred_element_type=F32)


def sds(shape, dtype):
    return jax.ShapeDtypeStruct(shape, dtype)


def call(kernel, name, outs, in_specs, out_specs, args, grid=(), scratch=(), vmem=24, after=()):
    taken = len(args)

    def body(*refs):
        kernel(*refs[:taken], *refs[taken + len(after) :])

    args = [*args, *after]
    in_specs = [*in_specs] + [ANY] * len(after)
    return pl.pallas_call(
        body,
        name=name,
        grid=grid,
        in_specs=in_specs,
        out_specs=out_specs,
        out_shape=outs,
        scratch_shapes=scratch,
        compiler_params=pltpu.CompilerParams(vmem_limit_bytes=vmem * MIB),
        cost_estimate=pl.CostEstimate(flops=1, bytes_accessed=1, transcendentals=0),
    )(*args)


def rows_of(block, width):
    return pl.BlockSpec((block, width), lambda i: (i, 0))


def fixed(*shape):
    return pl.BlockSpec(shape, lambda *_: (0,) * len(shape))


def swap(value, axis, offset=1):
    count = lax.axis_size(axis)
    return lax.ppermute(value, axis, [(i, i ^ offset) for i in range(count)])


def stage_kernel(plan, *refs):
    count = sum(len(pieces) for pieces in plan)
    ins, outs, sems = refs[:count], refs[count:-1], refs[-1]
    copies = []
    ins = iter(ins)
    for pieces, out in zip(plan, outs):
        at = 0
        for start, size in pieces:
            ref = next(ins)
            if start is not None:
                ref = ref.at[pl.ds(start, size)]
                place = out.at[pl.ds(at, size)]
            else:
                place = out.at[at] if len(ref.shape) < len(out.shape) else out
            at += size
            copies.append(pltpu.make_async_copy(ref, place, sems.at[len(copies)]))
    for copy in copies:
        copy.start()
    for copy in copies:
        copy.wait()


def stage(name, groups, after=()):
    arrays, plan, outs = [], [], []
    for group in groups:
        if not isinstance(group, list):
            arrays.append(group)
            plan.append(((None, 1),))
            outs.append(sds(group.shape, group.dtype))
            continue
        pieces, total = [], 0
        for piece in group:
            array, start, size = piece if isinstance(piece, tuple) else (piece, None, 1)
            arrays.append(array)
            pieces.append((start, size))
            total += size
        tail = array.shape if start is None else array.shape[1:]
        plan.append(tuple(pieces))
        outs.append(sds((total,) + tail, array.dtype))
    return call(
        functools.partial(stage_kernel, tuple(plan)),
        name,
        outs,
        [ANY] * len(arrays),
        [VM] * len(outs),
        arrays,
        scratch=[pltpu.SemaphoreType.DMA((len(arrays),))],
        vmem=12,
        after=after,
    )


def pack_kernel(*refs):
    ins, (out, sems) = refs[:-2], refs[-2:]
    at, copies = 0, []
    for i, ref in enumerate(ins):
        place = out.at[:, pl.ds(at, ref.shape[1])]
        copies.append(pltpu.make_async_copy(ref, place, sems.at[i]))
        at += ref.shape[1]
    for copy in copies:
        copy.start()
    for copy in copies:
        copy.wait()


def pack(shards, after=()):
    width = sum(x.shape[1] for x in shards)
    outs = [sds((shards[0].shape[0], width), BF)]
    return call(
        pack_kernel,
        "pack",
        outs,
        [ANY] * len(shards),
        [VM],
        shards,
        scratch=[pltpu.SemaphoreType.DMA((len(shards),))],
        vmem=8,
        after=after,
    )[0]


def along_line(shard):
    return [swap(shard, "a", d) for d in range(1, lax.axis_size("a"))]


def sideways(first):
    return swap(first, "r"), [swap(first, "b", dy) for dy in range(1, lax.axis_size("b"))]


def halves_of(side_r, sides_b):
    half = side_r.shape[0] // 2
    return [[(side, 0, half)] for side in sides_b] + [[(side_r, half, half)]]


def corners(halves):
    *sides_b, side_r = halves
    return [
        (swap(side_b, "r"), swap(side_r, "b", dy + 1)) for dy, side_b in enumerate(sides_b)
    ]


def span(dy, dr, start, stop):
    return [(dy, dr, dz) for dz in range(start, stop)]


def left_blocks(first, sides_b):
    line = first.shape[0]
    left = [(first, span(0, 0, 0, line))]
    return left + [(side, span(dy + 1, 0, 0, line)) for dy, side in enumerate(sides_b)]


def right_blocks(side_r, ends):
    line = side_r.shape[0]
    right = [(side_r, span(0, 1, 0, line))]
    for dy, (low, high) in enumerate(ends):
        right.append((low, span(dy + 1, 1, 0, line // 2)))
        right.append((high, span(dy + 1, 1, line // 2, line)))
    return right


def one_of(index):
    def spec(array):
        shape = (1,) * len(index) + array.shape[len(index) :]
        rest = (0,) * (array.ndim - len(index))
        return pl.BlockSpec(shape, lambda i: index + rest)

    return spec


class Scatter:
    def __init__(self, name, cuts):
        self.name, self.cuts = name, cuts
        self.half = lax.axis_size("a") // 2
        self.count_b = lax.axis_size("b")
        self.parts = {}

    def add(self, arrays, rights):
        for dy in range(self.count_b):
            for at, dr in enumerate(rights):
                index = (dy,) if len(rights) == 1 else (dy, at)
                self.parts[(dy, dr)] = [(array, index) for array in arrays]

    def step(self, label, body, outs, parts, extra, after):
        args = [array for array, _ in parts] + extra
        specs = [one_of(index)(array) for array, index in parts]
        specs += [fixed(*x.shape) for x in extra]
        return call(
            body,
            self.name + label,
            outs,
            specs,
            [fixed(*x.shape) for x in outs],
            args,
            grid=(1,),
            vmem=24,
            after=after,
        )

    def corner(self, after=()):
        self.first_r, self.first_b = {}, {}
        for dy in range(1, self.count_b):
            parts = self.parts[(dy, 1)]
            shape = parts[0][0].shape[-2:]

            def body(*refs):
                ins, outs = refs[:-2], refs[-2:]
                for t in range(2 * self.half):
                    total = sum(read(ref, t) for ref in ins)
                    outs[t // self.half][t % self.half] = total.astype(BF)

            first, second = self.step(
                "_corner", body, [sds((self.half,) + shape, BF)] * 2, parts, [], after
            )
            self.first_r[dy] = swap(first, "r")
            self.first_b[dy] = swap(second, "b", dy)
            token = first
        return token

    def side_r(self, after=()):
        parts = self.parts[(0, 1)]
        shape = parts[0][0].shape[-2:]
        extra = list(self.first_b.values())

        def body(*refs):
            ins, more, out = refs[: len(parts)], refs[len(parts) : -1], refs[-1]
            for t in range(2 * self.half):
                total = sum(read(ref, t) for ref in ins)
                if t >= self.half:
                    total = total + sum(ref[t - self.half].astype(F32) for ref in more)
                out[t] = total.astype(BF)

        side = self.step("_side_r", body, [sds((2 * self.half,) + shape, BF)], parts, extra, after)[0]
        self.from_r = swap(side, "r")
        return side

    def side_b(self, after=()):
        self.from_b = []
        for dy in range(1, self.count_b):
            parts = self.parts[(dy, 0)]
            shape = parts[0][0].shape[-2:]

            def body(*refs):
                ins, (more, out) = refs[:-2], refs[-2:]
                for t in range(2 * self.half):
                    total = sum(read(ref, t) for ref in ins)
                    if t < self.half:
                        total = total + more[t].astype(F32)
                    out[t] = total.astype(BF)

            outs = [sds((2 * self.half,) + shape, BF)]
            side = self.step("_side_b", body, outs, parts, [self.first_r[dy]], after)[0]
            self.from_b.append(swap(side, "b", dy))
            token = side
        return token

    def line(self, after=()):
        parts = self.parts[(0, 0)]
        shape = parts[0][0].shape[-2:]

        def body(*refs):
            ins, more, outs = refs[: len(parts)], refs[len(parts) : -2 * self.half], refs[-2 * self.half :]
            for t in range(2 * self.half):
                total = sum(read(ref, t) for ref in ins) + sum(ref[t].astype(F32) for ref in more)
                outs[t][...] = total.astype(outs[t].dtype)

        outs = [sds(shape, F32)] + [sds(shape, BF)] * (2 * self.half - 1)
        sums = self.step("_line", body, outs, parts, [self.from_r, *self.from_b], after)
        self.own = sums[0]
        self.from_a = [swap(sums[dz], "a", dz) for dz in range(1, 2 * self.half)]
        return sums[0]

    def line_halves(self, after=()):
        parts = self.parts[(0, 0)]
        shape = parts[0][0].shape[-2:]
        half = self.half

        def body(*refs):
            ins, more, (keep, sent) = refs[: len(parts)], refs[len(parts) : -2], refs[-2:]
            for t in range(2 * half):
                total = sum(read(ref, t) for ref in ins) + sum(ref[t].astype(F32) for ref in more)
                if t < half:
                    keep[t] = total
                else:
                    sent[t - half] = total.astype(BF)

        outs = [sds((half,) + shape, F32), sds((half,) + shape, BF)]
        keep, sent = self.step("_line", body, outs, parts, [self.from_r, *self.from_b], after)
        self.own, self.from_a = keep, [swap(sent, "a", half)]
        return sent

    def line_end(self, after=()):
        shape = self.own.shape[1:]

        def body(keep, recv, own, sent):
            own[...] = keep[0] + recv[0].astype(F32)
            sent[...] = (keep[1] + recv[1].astype(F32)).astype(BF)

        outs = [sds(shape, F32), sds(shape, BF)]
        own, sent = self.step("_line_end", body, outs, [], [self.own, *self.from_a], after)
        self.own, self.from_a = own, [swap(sent, "a", 1)]
        return sent

    def final(self, after=()):
        depth = self.own.shape[0]

        def body(own, *refs):
            ins, outs = refs[: len(self.from_a)], refs[len(self.from_a) :]
            total = own[...] + sum(ref[...].astype(F32) for ref in ins)
            at = 0
            for out in outs:
                out[...] = total[:, at : at + out.shape[1]]
                at += out.shape[1]

        outs = [sds((depth, width), F32) for width in self.cuts]
        return self.step("_final", body, outs, [], [self.own, *self.from_a], after)


def read(ref, t):
    return ref[(0,) * (len(ref.shape) - 3) + (t,)].astype(F32)


def assemble_kernel(meta, keep_r, count_b, *refs):
    ins, out, sems = refs[: len(meta)], refs[len(meta)], refs[len(meta) + 1]
    at_a, at_b, at_r = (lax.axis_index(name) for name in ("a", "b", "r"))
    copies = []
    for ref, places in zip(ins, meta):
        depth = ref.shape[1]
        for t, (dy, dr, dz) in enumerate(places):
            row = pl.multiple_of(((at_a ^ dz) * count_b + (at_b ^ dy)) * depth, depth)
            place = out.at[at_r ^ dr] if keep_r else out
            copy = pltpu.make_async_copy(
                ref.at[t], place.at[pl.ds(row, depth), :], sems.at[len(copies)]
            )
            copy.start()
            copies.append(copy)
    for copy in copies:
        copy.wait()


def assemble(pieces, name, after=(), keep_r=True):
    count_a, count_b = lax.axis_size("a"), lax.axis_size("b")
    arrays = [piece for piece, _ in pieces]
    meta = [places for _, places in pieces]
    _, depth, width = arrays[0].shape
    shape = (count_a * count_b * depth, width)
    if keep_r:
        shape = (2,) + shape
    total = sum(x.shape[0] for x in arrays)
    return call(
        functools.partial(assemble_kernel, tuple(meta), keep_r, count_b),
        name,
        [sds(shape, BF)],
        [ANY] * len(arrays),
        [VM],
        arrays,
        scratch=[pltpu.SemaphoreType.DMA((total,))],
        vmem=16,
        after=after,
    )[0]


def normed(values):
    centre = values - jnp.mean(values, axis=-1, keepdims=True)
    spread = lax.rsqrt(jnp.mean(centre * centre, axis=-1, keepdims=True) + 1e-06)
    return centre * spread, spread


def norm_back(grad, norm, spread):
    return spread * (
        grad
        - jnp.mean(grad, axis=-1, keepdims=True)
        - norm * jnp.mean(grad * norm, axis=-1, keepdims=True)
    )


def matmul_kernel(x_ref, y_ref, out_ref):
    out_ref[...] = dot(x_ref[...], y_ref[...])


def ada_back_kernel(low_ref, rows_ref, ada_ref, grad_ref, d_low_ref):
    rows = rows_ref[...]
    kinds = dict(preferred_element_type=F32, precision=HIGH)
    grad_ref[...] = lax.dot_general(low_ref[...].astype(F32), rows, TN, **kinds)
    d_low_ref[...] = lax.dot_general(rows, ada_ref[...].astype(F32), NT, **kinds)


def attn_input_kernel(steps, *refs):
    mod_ref, out_ref = refs[-2:]
    at = pl.program_id(0) // steps
    x = refs[0][...]
    for i, ref in enumerate(refs[1:-2]):
        x = jnp.where(at == i + 1, ref[...], x)
    norm, _ = normed(x.astype(F32))
    out_ref[...] = (norm * (1.0 + mod_ref[1:2, :]) + mod_ref[0:1, :]).astype(BF)


def lane_ids(width=PAIR):
    return lax.broadcasted_iota(jnp.int32, (1, width), 1)


def turn(values, cosine, sine):
    early = lane_ids() % HEAD_DIM < HEAD_DIM // 2
    step = HEAD_DIM // 2
    other = jnp.where(early, pltpu.roll(values, PAIR - step, 1), pltpu.roll(values, step, 1))
    return values * cosine + other * sine


def qkv_kernel(x_ref, w_ref, cos_ref, sin_ref, q_ref, k_ref, v_ref):
    width = q_ref.shape[1]
    both = dot(x_ref[...], w_ref[...])
    cosine, sine = cos_ref[...], sin_ref[...]
    for lane in range(0, width, PAIR):
        q_ref[:, lane : lane + PAIR] = (
            turn(both[:, lane : lane + PAIR], cosine, sine) * (HEAD_DIM**-0.5 * LOG2E)
        ).astype(BF)
        at = width + lane
        k_ref[:, lane : lane + PAIR] = turn(both[:, at : at + PAIR], cosine, sine).astype(BF)
    v_ref[...] = both[:, 2 * width :].astype(BF)


def attend_kernel(block, q_ref, k_ref, v_ref, aq_ref, ak_ref, *refs):
    o_refs, lse_ref = refs[:-1], refs[-1]
    depth = o_refs[0].shape[0]
    frames = q_ref.shape[0]
    keys = jnp.concatenate([k_ref[...], ak_ref[...]], axis=1)
    values = v_ref[...]
    low = lane_ids() < HEAD_DIM
    zero, one = jnp.zeros((), BF), jnp.ones((), BF)

    def attend(with_max):
        for start in range(0, frames, block):
            rows = pl.ds(start, block)
            query, extra = q_ref[rows, :], aq_ref[rows, :]
            outs, logs = [], []
            for head in range(2):
                mine = low if head == 0 else jnp.logical_not(low)
                left = jnp.concatenate([jnp.where(mine, query, zero), extra], axis=1)
                scores = dot(left, keys, NT)
                if with_max:
                    top = jnp.max(scores, axis=1, keepdims=True)
                    scores = scores - top
                weights = jnp.exp2(scores).astype(BF)
                mixed = dot(weights, jnp.where(mine, values, one))
                outs.append(mixed / pltpu.roll(mixed, HEAD_DIM, 1))
                log = jnp.log2(jnp.maximum(mixed, 1e-30))
                logs.append(log + top if with_max else log)
            both = jnp.where(low, outs[0], outs[1]).astype(BF)
            o_refs[start // depth][pl.ds(start % depth, block), :] = both
            lse_ref[rows, :] = jnp.where(low, logs[1], logs[0])

    query_all, key_all = q_ref[...].astype(F32), k_ref[...].astype(F32)
    bound = jnp.max(jnp.sum(query_all * query_all, axis=1)) * jnp.max(
        jnp.sum(key_all * key_all, axis=1)
    )
    small = bound < 3600.0

    @pl.when(small)
    def _():
        attend(False)

    @pl.when(jnp.logical_not(small))
    def _():
        attend(True)


def split3(values):
    first = values.astype(BF)
    rest = values - first.astype(F32)
    second = rest.astype(BF)
    return first, second, (rest - second.astype(F32)).astype(BF)


def placed(parts, start, base):
    lanes = lane_ids()
    for i, part in enumerate(parts):
        base = jnp.where(lanes == start + i, part, base)
    return base


def attend_back_kernel(block, parts, q_ref, k_ref, v_ref, aq_ref, ak_ref, lse_ref, cos_ref, sin_ref, *refs):
    o_refs, do_refs, (dq_ref, dk_ref, dv_ref) = refs[:parts], refs[parts : 2 * parts], refs[2 * parts :]
    frames = q_ref.shape[0]
    lanes = lane_ids()
    low = lanes < HEAD_DIM
    zero = jnp.zeros((), BF)
    query, extra, lse = q_ref[...], aq_ref[...], lse_ref[...]
    grad = jnp.concatenate([ref[...] for ref in do_refs], axis=0)
    out = jnp.concatenate([ref[...] for ref in o_refs], axis=0)
    product = grad.astype(F32) * out.astype(F32)
    queries, grads, lefts, rights = [], [], [], []
    for head in range(2):
        mine = low if head == 0 else jnp.logical_not(low)
        log = lse[:, HEAD_DIM : HEAD_DIM + 1] if head == 0 else lse[:, 0:1]
        queries.append(jnp.where(mine, query, zero))
        lefts.append(jnp.concatenate([queries[-1], placed(split3(-log), 8, extra)], axis=1))
        inner = -jnp.sum(jnp.where(mine, product, 0.0), axis=1, keepdims=True)
        grads.append(jnp.where(mine, grad, zero))
        tail = placed(split3(inner), 0, jnp.zeros((frames, PAIR), BF))
        rights.append(jnp.concatenate([grads[-1], tail], axis=1))
    ones = jnp.where(lanes < 3, 1.0, 0.0).astype(BF)
    dq_turned = jnp.zeros((PAIR, frames), F32)
    for start in range(0, frames, block):
        rows = pl.ds(start, block)
        key, value = k_ref[rows, :], v_ref[rows, :]
        keys = jnp.concatenate([key, ak_ref[rows, :]], axis=1)
        values = jnp.concatenate([value, jnp.broadcast_to(ones, value.shape)], axis=1)
        dv, dk = 0.0, 0.0
        for head in range(2):
            mine = low if head == 0 else jnp.logical_not(low)
            soft = jnp.exp2(dot(keys, lefts[head], NT))
            d_scores = (soft * dot(values, rights[head], NT)).astype(BF)
            dv = dv + dot(soft.astype(BF), grads[head])
            dk = dk + dot(d_scores, queries[head])
            dq_turned = dq_turned + dot(jnp.where(mine, key, zero), d_scores, TN)
        dv_ref[rows, :] = dv.astype(BF)
        dk_ref[rows, :] = turn(dk * LN2, cos_ref[rows, :], -sin_ref[rows, :]).astype(BF)
    dq = dq_turned.T * HEAD_DIM**-0.5
    dq_ref[...] = turn(dq, cos_ref[...], -sin_ref[...]).astype(BF)


def column(dr, dp):
    at_r, at_p = lax.axis_index("r"), lax.axis_index("p")
    return (at_r ^ dr) * lax.axis_size("p") + (at_p ^ dp)


def lanes_of(index, width):
    return pl.ds(pl.multiple_of(index * width, width), width)


def column_blocks(weight_refs):
    count_r = lax.axis_size("r")
    count_p = lax.axis_size("p")
    at_p = lax.axis_index("p")
    for dp, ref in enumerate(weight_refs):
        for r in range(count_r):
            yield r * count_p + (at_p ^ dp), ref, r


def out_kernel(count_p, x_ref, mod_ref, *refs):
    att_refs = refs[: 2 * count_p]
    w_refs = refs[2 * count_p : 3 * count_p]
    branch_ref, mid_ref, ffn_ref, att_ref, sum_ref = refs[3 * count_p :]
    width = att_refs[0].shape[1]
    for dp in range(count_p):
        for dr in range(2):
            att_ref[:, lanes_of(column(dr, dp), width)] = att_refs[2 * dp + dr][...]
    att = att_ref[...]
    for j, ref, r in column_blocks(w_refs):
        sum_ref[:, lanes_of(j, ref.shape[2])] = dot(att, ref[r])
    branch = sum_ref[...]
    branch_ref[...] = branch.astype(BF)
    mid = x_ref[...].astype(F32) + mod_ref[2:3, :] * branch
    mid_ref[...] = mid
    norm, _ = normed(mid)
    ffn_ref[...] = (norm * (1.0 + mod_ref[4:5, :]) + mod_ref[3:4, :]).astype(BF)


def up_kernel(count_p, x_ref, cot_ref, mod_ref, *refs):
    w_refs, (gelu_ref, slope_ref, dbf_ref) = refs[:count_p], refs[count_p:]
    dbf_ref[...] = (cot_ref[...].astype(F32) * mod_ref[5:6, :]).astype(BF)
    x = x_ref[...]
    root = 0.7978845608028654
    for j, ref, r in column_blocks(w_refs):
        up = dot(x, ref[r])
        square = up * up
        tanh = jnp.tanh(root * (up + 0.044715 * up * square))
        half = 0.5 * (1.0 + tanh)
        at = lanes_of(j, ref.shape[2])
        gelu_ref[:, at] = (up * half).astype(BF)
        slope = half + 0.5 * up * (1.0 - tanh * tanh) * (root * (1.0 + 0.134145 * square))
        slope_ref[:, at] = slope.astype(BF)


def down_kernel(count_p, gelu_ref, mid_ref, cot_ref, mod_ref, *refs):
    w_refs = refs[:count_p]
    out_ref, dgate_ref, sum_ref = refs[count_p:]
    gelu = gelu_ref[...]
    for j, ref, r in column_blocks(w_refs):
        sum_ref[:, lanes_of(j, ref.shape[2])] = dot(gelu, ref[r])
    branch = sum_ref[...]
    gate = mod_ref[5:6, :]
    out_ref[...] = (mid_ref[...] + gate * branch).astype(BF)
    cot = cot_ref[...].astype(F32)

    @pl.when(pl.program_id(0) == 0)
    def _():
        dgate_ref[...] = jnp.zeros_like(dgate_ref)

    dgate_ref[...] += jnp.sum(cot * branch, axis=0, keepdims=True)


def turned_dot(x_ref, w_refs):
    total = 0.0
    for j, ref, r in column_blocks(w_refs):
        total = total + dot(x_ref[:, lanes_of(j, ref.shape[2])], ref[r], NT)
    return total


def d_up_kernel(count_p, dbf_ref, slope_ref, *refs):
    w_refs, (out_ref,) = refs[:count_p], refs[count_p:]
    out_ref[...] = (turned_dot(dbf_ref, w_refs) * slope_ref[...].astype(F32)).astype(BF)


def mid_back_kernel(count_p, d_up_ref, mid_ref, cot_ref, branch_ref, mod_ref, *refs):
    up_refs, o_refs = refs[:count_p], refs[count_p : 2 * count_p]
    d_mid_ref, dba_ref, sums_ref = refs[2 * count_p : 2 * count_p + 3]
    att_refs, att_all = refs[2 * count_p + 3 : -1], refs[-1]
    d_in = turned_dot(d_up_ref, up_refs)
    norm, spread = normed(mid_ref[...])

    @pl.when(pl.program_id(0) == 0)
    def _():
        sums_ref[...] = jnp.zeros_like(sums_ref)

    sums_ref[1:2, :] += jnp.sum(d_in, axis=0, keepdims=True)
    sums_ref[2:3, :] += jnp.sum(d_in * norm, axis=0, keepdims=True)
    d_mid = cot_ref[...].astype(F32) + norm_back(d_in * (1.0 + mod_ref[4:5, :]), norm, spread)
    d_mid_ref[...] = d_mid
    sums_ref[0:1, :] += jnp.sum(d_mid * branch_ref[...].astype(F32), axis=0, keepdims=True)
    dba_ref[...] = (d_mid * mod_ref[2:3, :]).astype(BF)
    att_all[...] = turned_dot(dba_ref, o_refs)
    for dp in range(count_p):
        for dr in range(2):
            ref = att_refs[2 * dp + dr]
            ref[...] = att_all[:, lanes_of(column(dr, dp), ref.shape[1])].astype(BF)


def weight_grad_kernel(counts, places, sizes, *refs):
    count_x, count_y = counts
    x_refs, y_refs = refs[:count_x], refs[count_x : count_x + count_y]
    out_refs = refs[count_x + count_y : -2]
    held, sems = refs[-2:]
    count_a, count_b = sizes
    count_p = lax.axis_size("p")
    at_a, at_b = lax.axis_index("a"), lax.axis_index("b")
    depth = out_refs[0].shape[-2]
    xs = [ref[...] for ref in x_refs] * (count_y // count_x)
    copies = []
    for slot, (dp, dr) in enumerate(places):
        at = 0
        for x, ref in zip(xs, y_refs):
            if dr is None:
                width = ref.shape[1]
                y = ref[...]
            else:
                width = ref.shape[1] // (2 * count_p)
                y = ref[:, lanes_of(column(dr, dp), width)]
            held[slot, :, at : at + width] = dot(x, y, TN).astype(BF)
            at += width
        for dy in range(count_b):
            for dz in range(count_a):
                row = pl.multiple_of(((at_a ^ dz) * count_b + (at_b ^ dy)) * depth, depth)
                place = out_refs[0].at[dy, dz] if dr is None else out_refs[0].at[dy, dr, dz]
                copy = pltpu.make_async_copy(
                    held.at[slot, pl.ds(row, depth), :], place, sems.at[len(copies)]
                )
                copy.start()
                copies.append(copy)
    for copy in copies:
        copy.wait()


def weight_grad(name, xs, ys, dp=None, after=()):
    count_a, count_b = lax.axis_size("a"), lax.axis_size("b")
    depth = xs[0].shape[1] // (count_a * count_b)
    width = sum(y.shape[1] for y in ys)
    if dp is not None:
        width //= 2 * lax.axis_size("p")
        places = [(dp, dr) for dr in reversed(range(2))]
        outs = [sds((count_b, 2, count_a, depth, width), BF)]
    else:
        places = [(0, None)]
        outs = [sds((count_b, count_a, depth, width), BF)]
    return call(
        functools.partial(
            weight_grad_kernel, (len(xs), len(ys)), tuple(places), (count_a, count_b)
        ),
        name,
        outs,
        [VM] * (len(xs) + len(ys)),
        [ANY],
        [*xs, *ys],
        scratch=[
            pltpu.VMEM((len(places), xs[0].shape[1], width), BF),
            pltpu.SemaphoreType.DMA((len(places) * count_a * count_b,)),
        ],
        after=after,
    )[0]


def split_grad(name, xs, ys, after=()):
    count_p = lax.axis_size("p")
    parts = []
    for dp in range(1, count_p):
        sent = weight_grad(name, xs, ys, dp, after)
        after = [sent]
        parts.append(swap(sent, "p", dp))
    return [weight_grad(name, xs, ys, 0, after)] + parts


def qkv_turned(refs, ws):
    total = 0.0
    for t, ref in enumerate(refs):
        width = ref.shape[1]
        at = (t % 3) * width
        total = total + dot(ref[...], ws[t // 3][:, at : at + width], NT)
    return total


def d_attn_send_kernel(*refs):
    refs[-1][...] = qkv_turned(refs[:6], refs[6:8]).astype(BF)


def hidden_back_kernel(count_recv, *refs):
    d_refs, ws = refs[:6], refs[6:8]
    recv = refs[8 : 8 + count_recv]
    x_ref, d_mid_ref, mod_ref, out_ref, sums_ref = refs[8 + count_recv :]
    d_in = qkv_turned(d_refs, ws)
    for ref in recv:
        d_in = d_in + ref[...].astype(F32)
    norm, spread = normed(x_ref[...].astype(F32))

    @pl.when(pl.program_id(0) == 0)
    def _():
        sums_ref[...] = jnp.zeros_like(sums_ref)

    sums_ref[0:1, :] += jnp.sum(d_in, axis=0, keepdims=True)
    sums_ref[1:2, :] += jnp.sum(d_in * norm, axis=0, keepdims=True)
    back = norm_back(d_in * (1.0 + mod_ref[1:2, :]), norm, spread)
    out_ref[...] = (d_mid_ref[...] + back).astype(BF)


def exchange_rows(rows):
    at_r = lax.axis_index("r")
    own = lax.dynamic_index_in_dim(rows, at_r, keepdims=False)
    other = swap(lax.dynamic_index_in_dim(rows, 1 - at_r, keepdims=False), "r")
    return jnp.concatenate([own, other], axis=0)


def restore_rows(frames):
    half = frames.shape[0] // 2
    own, other = frames[:half], swap(frames[half:], "r")
    return jnp.where(lax.axis_index("r") == 0, jnp.stack([own, other]), jnp.stack([other, own]))


def local(
    hidden_in,
    time_embed,
    seg_lengths,
    ada_weight,
    query_weight,
    key_weight,
    value_weight,
    out_weight,
    up_weight,
    down_weight,
    out_cotangent,
):
    count_a, count_b, count_p = (lax.axis_size(name) for name in ("a", "b", "p"))
    at_a, at_b, at_r, at_p = (lax.axis_index(name) for name in ("a", "b", "r", "p"))
    width = hidden_in.shape[2]
    block = hidden_in.shape[1]
    mine = 2 * block
    frames = mine * count_p
    heads_wide = query_weight.shape[1]
    ffn = up_weight.shape[1] * 2 * count_p
    others = range(1, count_p)

    qkv_shard = pack([query_weight, key_weight, value_weight])
    qkv_z = along_line(qkv_shard)
    hidden = exchange_rows(hidden_in)

    every = ("a", "b", "r", "p")
    time_vecs = time_embed.astype(F32)
    time_low = jax.nn.silu(time_vecs).astype(BF)
    low_mine = lax.all_to_all(time_low, ("a", "b"), split_axis=1, concat_axis=0, tiled=True)
    ada_rows, ada_cols = ada_weight.shape
    part = call(
        matmul_kernel,
        "modulation_part",
        [sds((low_mine.shape[0], ada_cols), F32)],
        [VM, VM],
        [VM],
        [low_mine, ada_weight],
        vmem=8,
    )[0]
    qkv_line, up_shard, out_shard = stage(
        "stage1", [[qkv_shard, *qkv_z], up_weight, out_weight], [hidden, part]
    )

    uo_shard = pack([up_shard, out_shard])
    qkv_r, qkv_b = sideways(qkv_line)
    uo_z = along_line(uo_shard)
    hidden_parts = [hidden] + [swap(hidden, "p", dp) for dp in others]
    part = lax.all_to_all(
        jnp.repeat(part, count_p, axis=0), every, split_axis=0, concat_axis=0, tiled=True
    )
    modulation = jnp.sum(part.reshape(count_a * count_b, -1), axis=0).reshape(6, width)

    lengths = lax.dynamic_index_in_dim(seg_lengths, at_r, keepdims=False)
    frame_ids = jnp.concatenate(
        [
            ((at_r ^ dr) * count_p + (at_p ^ dp)) * block + jnp.arange(block, dtype=jnp.int32)
            for dp in range(count_p)
            for dr in range(2)
        ]
    )
    passed = frame_ids[:, None] >= jnp.cumsum(lengths)[None, :]
    seg_ids = jnp.sum(passed.astype(jnp.int32), axis=1)
    positions = frame_ids - jnp.sum(jnp.where(passed, lengths[None, :], 0), axis=1)
    half_dim = HEAD_DIM // 2
    lane = jnp.arange(PAIR, dtype=jnp.int32)
    inverse = 10000.0 ** (-(lane % half_dim).astype(F32) / half_dim)
    angles = positions.astype(F32)[:, None] * inverse[None, :]
    cosine = jnp.cos(angles)
    sine = jnp.where(lane % HEAD_DIM < half_dim, -1.0, 1.0)[None, :] * jnp.sin(angles)
    segs = seg_lengths.shape[1]
    same = seg_ids[:, None] == lane[None, :]
    real = (lane < segs)[None, :]
    extra_q = jnp.where(real & ~same, -1e30, 0.0).astype(BF)
    extra_k = jnp.where((real & same) | ((lane >= 8) & (lane < 11))[None, :], 1.0, 0.0).astype(BF)

    pair_block = pl.BlockSpec((frames, PAIR), lambda i: (0, i))
    pair_rows = pl.BlockSpec((mine, PAIR), lambda i: (0, i))
    pair_fixed = fixed(frames, PAIR)
    heads = sds((frames, heads_wide), BF)
    tile = min(256, mine)
    steps = mine // tile
    grid = (steps,)
    full = rows_of(tile, width)
    wide = rows_of(tile, ffn)
    part = rows_of(tile, heads_wide)
    mod_spec = fixed(6, width)

    def project(x, weights, after):
        return call(
            qkv_kernel,
            "qkv",
            [heads] * 3,
            [full, fixed(width, 3 * heads_wide)] + [rows_of(tile, PAIR)] * 2,
            [part] * 3,
            [x, weights, cosine, sine],
            grid=(frames // tile,),
            after=after,
        )

    def attend(three, after):
        return call(
            functools.partial(attend_kernel, min(256, frames)),
            "attend",
            [sds((mine, heads_wide), BF)] * count_p + [sds((frames, heads_wide), F32)],
            [pair_block] * 3 + [pair_fixed] * 2,
            [pair_rows] * count_p + [pair_block],
            [*three, extra_q, extra_k],
            grid=(heads_wide // PAIR,),
            after=after,
        )

    *qkv_halves, uo_shard2 = stage(
        "stage2", halves_of(qkv_r, qkv_b) + [uo_shard], [*qkv_b, *uo_z[:-1], hidden_parts[-1]]
    )
    uo_z = uo_z[:-1] + [swap(uo_shard2, "a", count_a - 1)]
    qkv_ends = corners(qkv_halves)
    cot_own = stage("cot", [out_cotangent], [uo_shard2])[0]
    cotangent = exchange_rows(cot_own)
    attn_input = call(
        functools.partial(attn_input_kernel, steps),
        "attn_input",
        [sds((frames, width), BF)],
        [
            pl.BlockSpec((tile, width), lambda i, dp=dp: (jnp.clip(i - dp * steps, 0, steps - 1), 0))
            for dp in range(count_p)
        ]
        + [mod_spec],
        [full],
        [*hidden_parts, modulation],
        grid=(frames // tile,),
        after=[cot_own],
    )[0]
    qkv_w = [assemble(left_blocks(qkv_line, qkv_b), "assemble_qkv", [attn_input], False)]
    qkv = [project(attn_input, qkv_w[0], ())]
    attended = [attend(qkv[0], ())]

    uo_line, down_shard = stage(
        "stage3", [[uo_shard, *uo_z], down_weight], [attended[0][0], cotangent, *qkv_ends[-1]]
    )
    uo_r, uo_b = sideways(uo_line)
    down_z = along_line(down_shard)
    qkv_w.append(assemble(right_blocks(qkv_r, qkv_ends), "assemble_qkv", [uo_line], False))
    qkv.append(project(attn_input, qkv_w[1], ()))

    *uo_halves, down_line = stage(
        "stage4", halves_of(uo_r, uo_b) + [[down_shard, *down_z]], [qkv[1][0], *uo_b]
    )
    uo_ends = corners(uo_halves)
    attended.append(attend(qkv[1], [down_line]))

    uo_pieces = left_blocks(uo_line, uo_b) + right_blocks(uo_r, uo_ends)
    uo_w = [assemble(uo_pieces, "assemble_uo", [attended[1][0]])]
    uo_w += [swap(uo_w[0], "p", dp) for dp in others]
    down_line = stage("stage5", [down_line], [uo_w[0]])[0]
    down_r, down_b = sideways(down_line)
    att = [attended[dr][0] for dr in range(2)]
    for dp in others:
        att += [swap(attended[dr][dp], "p", dp) for dr in range(2)]
    ffn_block = ffn // (2 * count_p)
    up_specs = [pl.BlockSpec((2, width, ffn_block), lambda i: (0, 0, 0))] * count_p
    out_specs = [pl.BlockSpec((2, width, heads_wide), lambda i: (0, 0, ffn_block // heads_wide))] * count_p
    branch_attn, mid, ffn_input, att_all = call(
        functools.partial(out_kernel, count_p),
        "attn_out",
        [sds((mine, width), BF), sds((mine, width), F32), sds((mine, width), BF), sds((mine, width), BF)],
        [full, mod_spec] + [part] * (2 * count_p) + out_specs,
        [full] * 4,
        [hidden, modulation, *att, *uo_w],
        grid=grid,
        scratch=[pltpu.VMEM((tile, width), F32)],
        after=[down_line],
    )
    gelu_low, slope, d_branch_ffn = call(
        functools.partial(up_kernel, count_p),
        "ffn_up",
        [sds((mine, ffn), BF)] * 2 + [sds((mine, width), BF)],
        [full, full, mod_spec] + up_specs,
        [wide, wide, full],
        [ffn_input, cotangent, modulation, *uo_w],
        grid=grid,
    )

    down_halves = stage("stage6", halves_of(down_r, down_b), [gelu_low, *down_b])
    down_ends = corners(down_halves)
    down_sum = Scatter("down", [width // (2 * count_p)])
    uo_sum = Scatter("uo", [ffn_block, heads_wide])
    qkv_sum = Scatter("qkv", [heads_wide] * 3)
    down_parts = split_grad("down_grad", [gelu_low], [d_branch_ffn], [down_halves[0]])
    down_sum.add(down_parts, (0, 1))

    down_pieces = left_blocks(down_line, down_b) + right_blocks(down_r, down_ends)
    down_w = [assemble(down_pieces, "assemble_down", [down_parts[0]])]
    down_w += [swap(down_w[0], "p", dp) for dp in others]
    down_specs = [fixed(*w.shape) for w in down_w]
    token = down_sum.corner([down_w[0]])
    d_up = call(
        functools.partial(d_up_kernel, count_p),
        "d_up",
        [sds((mine, ffn), BF)],
        [full, wide] + down_specs,
        [wide],
        [d_branch_ffn, slope, *down_w],
        grid=grid,
        after=[token],
    )[0]

    token = down_sum.side_b([down_sum.side_r([d_up])])
    d_mid, d_branch_attn, sums_mid, *d_att = call(
        functools.partial(mid_back_kernel, count_p),
        "mid_back",
        [sds((mine, width), F32), sds((mine, width), BF), sds((3, width), F32)]
        + [sds((mine, heads_wide), BF)] * (2 * count_p),
        [wide, full, full, full, mod_spec] + up_specs + out_specs,
        [full, full, fixed(3, width)] + [part] * (2 * count_p),
        [d_up, mid, cotangent, branch_attn, modulation, *uo_w, *uo_w],
        grid=grid,
        scratch=[pltpu.VMEM((tile, width), F32)],
        after=[token],
    )
    hidden_out, d_ffn_gate = call(
        functools.partial(down_kernel, count_p),
        "ffn_down",
        [sds((mine, width), BF), sds((1, width), F32)],
        [wide, full, full, mod_spec] + down_specs,
        [full, fixed(1, width)],
        [gelu_low, mid, cotangent, modulation, *down_w],
        grid=grid,
        scratch=[pltpu.VMEM((tile, width), F32)],
        after=[d_branch_attn],
    )

    token = down_sum.line([hidden_out])
    hidden_out = restore_rows(hidden_out)
    uo_parts = split_grad("uo_grad", [ffn_input, att_all], [d_up, d_branch_attn], [token])
    uo_sum.add(uo_parts, (0, 1))

    def attend_back(dr, after):
        d_heads = [d_att[dr]] + [swap(d_att[2 * dp + dr], "p", dp) for dp in others]
        return call(
            functools.partial(attend_back_kernel, min(512, frames), count_p),
            "attend_back",
            [sds((frames, heads_wide), BF)] * 3,
            [pair_block] * 3
            + [pair_fixed] * 2
            + [pair_block]
            + [pair_fixed] * 2
            + [pair_rows] * (2 * count_p),
            [pair_block] * 3,
            [*qkv[dr], extra_q, extra_k, attended[dr][-1], cosine, sine, *attended[dr][:-1], *d_heads],
            grid=(heads_wide // PAIR,),
            vmem=24,
            after=after,
        )

    def qkv_parts(dr, after):
        return [weight_grad("qkv_grad", [attn_input], d_qkv[dr], None, after)]

    d_qkv = [None, None]

    token = uo_sum.corner([uo_parts[0]])
    d_qkv[1] = attend_back(1, [token])

    down_grad = down_sum.final([d_qkv[1][0]])[0]
    token = uo_sum.side_b([uo_sum.side_r([down_grad, hidden_out])])
    qkv_sum.add(qkv_parts(1, [token]), (1,))
    token = qkv_sum.corner()
    d_qkv[0] = attend_back(0, [token])

    qkv_sum.add(qkv_parts(0, ()), (0,))
    token = qkv_sum.side_b()
    token = qkv_sum.side_r([token])
    token = uo_sum.line_halves([token])
    six = [*d_qkv[0], *d_qkv[1]]
    w_specs = [fixed(width, 3 * heads_wide)] * 2
    received, after = [], [token]
    for dp in others:
        first = dp * mine // tile
        part_spec = pl.BlockSpec((tile, heads_wide), lambda i, first=first: (i + first, 0))
        sent = call(
            d_attn_send_kernel,
            "d_attn_send",
            [sds((mine, width), BF)],
            [part_spec] * 6 + w_specs,
            [full],
            [*six, *qkv_w],
            grid=grid,
            vmem=24,
            after=after,
        )[0]
        after = [sent]
        received.append(swap(sent, "p", dp))
    hidden_grad, sums_in = call(
        functools.partial(hidden_back_kernel, len(received)),
        "hidden_back",
        [sds((mine, width), BF), sds((2, width), F32)],
        [part] * 6 + w_specs + [full] * len(received) + [full, full, mod_spec],
        [full, fixed(2, width)],
        [*six, *qkv_w, *received, hidden, d_mid, modulation],
        grid=grid,
        vmem=32,
        after=after,
    )

    d_mod = jnp.concatenate([sums_in, sums_mid, d_ffn_gate], axis=0).reshape(2 * count_p, ada_cols)
    d_rows = lax.all_to_all(
        jnp.tile(d_mod, (count_a * count_b, 1)), every, split_axis=0, concat_axis=0, tiled=True
    )
    d_rows = jnp.sum(d_rows.reshape(-1, count_p, ada_cols), axis=1)

    token = qkv_sum.line([d_rows])
    token = uo_sum.line_end([token])
    hidden_grad = restore_rows(hidden_grad)
    ada_grad, d_low = call(
        ada_back_kernel,
        "ada_back",
        [sds(ada_weight.shape, F32), sds((d_rows.shape[0], ada_rows), F32)],
        [VM] * 3,
        [VM] * 2,
        [low_mine, d_rows, ada_weight],
        vmem=16,
        after=[token],
    )
    d_low = d_low.reshape(count_a * count_b, 1, -1)
    d_low = jnp.broadcast_to(d_low, (d_low.shape[0], 2 * count_p, d_low.shape[2]))
    d_low = lax.all_to_all(
        d_low.reshape(-1, d_low.shape[2]), every, split_axis=0, concat_axis=0, tiled=True
    )
    d_low = jnp.sum(d_low.reshape(count_a * count_b, 2 * count_p, 2, ada_rows), axis=1)
    d_time_low = jnp.moveaxis(d_low, 0, 1).reshape(2, width)
    _, silu_pullback = jax.vjp(jax.nn.silu, time_vecs)
    time_grad = silu_pullback(d_time_low)[0]
    up_grad, out_grad = uo_sum.final()
    query_grad, key_grad, value_grad = qkv_sum.final()

    return (
        hidden_out,
        hidden_grad,
        time_grad,
        ada_grad,
        query_grad,
        key_grad,
        value_grad,
        out_grad,
        up_grad,
        down_grad,
    )


def solution(mesh):
    count_dp, count_sp = mesh.shape["dp"], mesh.shape["sp"]
    fine = Mesh(mesh.devices.reshape(4, count_dp // 4, 2, count_sp // 2), ("a", "b", "r", "p"))
    dp, sp = ("a", "b"), ("r", "p")
    in_specs = (
        (P(dp, sp, None), P(dp, None), P(dp, None)) + (P(dp, sp),) * 7 + (P(dp, sp, None),)
    )
    out_specs = (P(dp, sp, None), P(dp, sp, None), P(dp, None)) + (P(dp, sp),) * 7
    return jax.shard_map(local, mesh=fine, in_specs=in_specs, out_specs=out_specs, check_vma=False)
```

```python
import functools

import jax
import jax.numpy as jnp
from jax import lax
from jax.experimental import pallas as pl
from jax.experimental.pallas import tpu as pltpu
from jax.sharding import Mesh
from jax.sharding import PartitionSpec as P

HEAD_DIM = 64
PAIR = 2 * HEAD_DIM
LOG2E = 1.4426950408889634
LN2 = 0.6931471805599453
HIGH = lax.Precision.HIGHEST
F32 = jnp.float32
BF = jnp.bfloat16
NN = (((1,), (0,)), ((), ()))
NT = (((1,), (1,)), ((), ()))
TN = (((0,), (0,)), ((), ()))
ANY = pl.BlockSpec(memory_space=pl.ANY)
HBM = pl.BlockSpec(memory_space=pltpu.HBM)
VM = pl.BlockSpec(memory_space=pltpu.VMEM)
MIB = 1 << 20


def dot(left, right, dims=NN):
    return lax.dot_general(left, right, dims, preferred_element_type=F32)


def sds(shape, dtype):
    return jax.ShapeDtypeStruct(shape, dtype)


def call(kernel, name, outs, in_specs, out_specs, args, grid=(), scratch=(), vmem=24, after=()):
    taken = len(args)

    def body(*refs):
        kernel(*refs[:taken], *refs[taken + len(after) :])

    args = [*args, *after]
    in_specs = [*in_specs] + [ANY] * len(after)
    return pl.pallas_call(
        body,
        name=name,
        grid=grid,
        in_specs=in_specs,
        out_specs=out_specs,
        out_shape=outs,
        scratch_shapes=scratch,
        compiler_params=pltpu.CompilerParams(vmem_limit_bytes=vmem * MIB),
        cost_estimate=pl.CostEstimate(flops=1, bytes_accessed=1, transcendentals=0),
    )(*args)


def rows_of(block, width):
    return pl.BlockSpec((block, width), lambda i: (i, 0))


def fixed(*shape):
    return pl.BlockSpec(shape, lambda *_: (0,) * len(shape))


def swap(value, axis, offset=1):
    count = lax.axis_size(axis)
    return lax.ppermute(value, axis, [(i, i ^ offset) for i in range(count)])


def stage_kernel(plan, *refs):
    count = sum(len(pieces) for pieces in plan)
    ins, outs = iter(refs[:count]), refs[count:]
    for pieces, out in zip(plan, outs):
        at = 0
        for start, size in pieces:
            ref = next(ins)
            if start is not None:
                out[at : at + size] = ref[start : start + size]
            elif len(ref.shape) < len(out.shape):
                out[at] = ref[...]
            else:
                out[...] = ref[...]
            at += size


def stage(name, groups, after=()):
    arrays, plan, outs = [], [], []
    for group in groups:
        if not isinstance(group, list):
            arrays.append(group)
            plan.append(((None, 1),))
            outs.append(sds(group.shape, group.dtype))
            continue
        pieces, total = [], 0
        for piece in group:
            array, start, size = piece if isinstance(piece, tuple) else (piece, None, 1)
            arrays.append(array)
            pieces.append((start, size))
            total += size
        tail = array.shape if start is None else array.shape[1:]
        plan.append(tuple(pieces))
        outs.append(sds((total,) + tail, array.dtype))
    return call(
        functools.partial(stage_kernel, tuple(plan)),
        name,
        outs,
        [VM] * len(arrays),
        [VM] * len(outs),
        arrays,
        vmem=12,
        after=after,
    )


def pick_kernel(*refs):
    count = (len(refs) - 1) // 3
    ins, outs, sems = refs[:count], refs[count:-1], refs[-1]
    at_r = lax.axis_index("r")
    copies = []
    for i, ref in enumerate(ins):
        for j, row in enumerate((at_r, 1 - at_r)):
            at = 2 * i + j
            copies.append(pltpu.make_async_copy(ref.at[row], outs[at], sems.at[at]))
    for copy in copies:
        copy.start()
    for copy in copies:
        copy.wait()


def exchange_rows(arrays, after=()):
    outs = [sds(x.shape[1:], x.dtype) for x in arrays for _ in range(2)]
    picked = call(
        pick_kernel,
        "pick_rows",
        outs,
        [HBM] * len(arrays),
        [VM] * len(outs),
        arrays,
        scratch=[pltpu.SemaphoreType.DMA((len(outs),))],
        vmem=60,
        after=after,
    )
    return [(own, swap(other, "r")) for own, other in zip(picked[::2], picked[1::2])]


def place_kernel(own_ref, other_ref, out_ref):
    at_r = lax.axis_index("r")
    out_ref[at_r] = own_ref[...]
    out_ref[1 - at_r] = other_ref[...]


def restore_rows(own, other, after=()):
    outs = [sds((2,) + own.shape, own.dtype)]
    args = [own, swap(other, "r")]
    return call(place_kernel, "place_rows", outs, [VM] * 2, [VM], args, vmem=8, after=after)[0]


def pack_kernel(*refs):
    ins, (out, sems) = refs[:-2], refs[-2:]
    at, copies = 0, []
    for i, ref in enumerate(ins):
        place = out.at[:, pl.ds(at, ref.shape[1])]
        copies.append(pltpu.make_async_copy(ref, place, sems.at[i]))
        at += ref.shape[1]
    for copy in copies:
        copy.start()
    for copy in copies:
        copy.wait()


def pack(shards, after=(), vmem=8):
    width = sum(x.shape[1] for x in shards)
    outs = [sds((shards[0].shape[0], width), BF)]
    return call(
        pack_kernel,
        "pack",
        outs,
        [HBM] * len(shards),
        [VM],
        shards,
        scratch=[pltpu.SemaphoreType.DMA((len(shards),))],
        vmem=vmem,
        after=after,
    )[0]


def along_line(shard):
    return [swap(shard, "a", d) for d in range(1, lax.axis_size("a"))]


def sideways(first):
    return swap(first, "r"), [swap(first, "b", dy) for dy in range(1, lax.axis_size("b"))]


def halves_of(side_r, sides_b):
    half = side_r.shape[0] // 2
    return [[(side, 0, half)] for side in sides_b] + [[(side_r, half, half)]]


def corners(halves):
    *sides_b, side_r = halves
    return [
        (swap(side_b, "r"), swap(side_r, "b", dy + 1)) for dy, side_b in enumerate(sides_b)
    ]


def span(dy, dr, start, stop):
    return [(dy, dr, dz) for dz in range(start, stop)]


def left_blocks(first, sides_b):
    line = first.shape[0]
    left = [(first, span(0, 0, 0, line))]
    return left + [(side, span(dy + 1, 0, 0, line)) for dy, side in enumerate(sides_b)]


def right_blocks(side_r, ends):
    line = side_r.shape[0]
    right = [(side_r, span(0, 1, 0, line))]
    for dy, (low, high) in enumerate(ends):
        right.append((low, span(dy + 1, 1, 0, line // 2)))
        right.append((high, span(dy + 1, 1, line // 2, line)))
    return right


def one_of(index):
    def spec(array):
        shape = (1,) * len(index) + array.shape[len(index) :]
        rest = (0,) * (array.ndim - len(index))
        return pl.BlockSpec(shape, lambda i: index + rest)

    return spec


def totals(refs, members, t):
    wide, at = [], 0
    for member in members:
        wide.append(sum(read(ref, t) for ref in refs[at : at + len(member)]))
        at += len(member)
    return wide[0] if len(wide) == 1 else jnp.concatenate(wide, axis=1)


def read(ref, t):
    return ref[(0,) * (len(ref.shape) - 3) + (t,)].astype(F32)


class Scatter:
    def __init__(self, name, cuts, cut):
        self.name, self.cuts, self.cut = name, cuts, cut
        self.line_count = lax.axis_size("a")
        self.count_b = lax.axis_size("b")
        self.parts = {}
        self.first_r = {dy: [] for dy in range(1, self.count_b)}
        self.first_b = {dy: [] for dy in range(1, self.count_b)}

    def add(self, members, rights):
        for dy in range(self.count_b):
            for at, dr in enumerate(rights):
                index = (dy,) if len(rights) == 1 else (dy, at)
                found = self.parts.setdefault((dy, dr), [])
                found += [[(x, index) for x in member] for member in members]

    def step(self, label, body, shapes, members, extra, after):
        pairs = [pair for member in members for pair in member]
        specs = [one_of(index)(array) for array, index in pairs]
        return call(
            body,
            self.name + label,
            shapes,
            specs + [fixed(*x.shape) for x in extra],
            [fixed(*x.shape) for x in shapes],
            [array for array, _ in pairs] + extra,
            grid=(1,),
            vmem=24,
            after=after,
        )

    def block(self, members):
        return members[0][0][0].shape[-2], sum(member[0][0].shape[-1] for member in members)

    def corner(self, after=(), some=slice(None)):
        cut, line = self.cut, self.line_count
        for dy in range(1, self.count_b):
            members = self.parts[(dy, 1)][some]
            shape = self.block(members)

            def body(*refs, members=members):
                for t in range(line):
                    out, at = (refs[-2], t) if t < cut else (refs[-1], t - cut)
                    out[at] = totals(refs, members, t).astype(BF)

            shapes = [sds((cut,) + shape, BF), sds((line - cut,) + shape, BF)]
            first, second = self.step("_corner", body, shapes, members, [], after)
            self.first_r[dy].append(swap(first, "r"))
            self.first_b[dy].append(swap(second, "b", dy))
        return first

    def side_r(self, after=()):
        members = self.parts[(0, 1)]
        groups = list(self.first_b.values())
        extra = [x for group in groups for x in group]
        cut, line = self.cut, self.line_count

        def body(*refs):
            more, out = refs[-1 - len(extra) : -1], refs[-1]
            for t in range(line):
                total = totals(refs, members, t)
                if t >= cut:
                    total = total + self.added(more, len(groups), t - cut)
                out[t] = total.astype(BF)

        shapes = [sds((line,) + self.block(members), BF)]
        after = [*after, *[x for group in self.first_r.values() for x in group]]
        side = self.step("_side_r", body, shapes, members, extra, after)[0]
        self.from_r = swap(side, "r")
        return side

    def added(self, refs, groups, t):
        each = len(refs) // groups
        total = 0.0
        for at in range(0, len(refs), each):
            pieces = [ref[t].astype(F32) for ref in refs[at : at + each]]
            total = total + (pieces[0] if each == 1 else jnp.concatenate(pieces, axis=1))
        return total

    def side_b(self, after=()):
        self.from_b = []
        cut, line = self.cut, self.line_count
        for dy in range(1, self.count_b):
            members = self.parts[(dy, 0)]
            extra = self.first_r[dy]

            def body(*refs, members=members, extra=extra):
                more, out = refs[-1 - len(extra) : -1], refs[-1]
                for t in range(line):
                    total = totals(refs, members, t)
                    if t < cut:
                        total = total + self.added(more, 1, t)
                    out[t] = total.astype(BF)

            shapes = [sds((line,) + self.block(members), BF)]
            side = self.step("_side_b", body, shapes, members, extra, after)[0]
            self.from_b.append(swap(side, "b", dy))
        return side

    def line(self, after=()):
        members = self.parts[(0, 0)]
        shape, line = self.block(members), self.line_count
        extra = [self.from_r, *self.from_b]
        kept = line // 2

        def body(*refs):
            more, (keep, sent) = refs[-2 - len(extra) : -2], refs[-2:]
            for t in range(line):
                total = totals(refs, members, t) + sum(ref[t].astype(F32) for ref in more)
                if t % 2:
                    sent[t // 2] = total.astype(BF)
                else:
                    keep[t // 2] = total

        shapes = [sds((kept,) + shape, F32), sds((kept,) + shape, BF)]
        self.keep, sent = self.step("_line", body, shapes, members, extra, after)
        self.step_size, self.from_a = 1, swap(sent, "a", 1)
        return sent

    def line_next(self, after=()):
        kept = self.keep.shape[0] // 2
        shape = self.keep.shape[1:]

        def body(keep_ref, recv_ref, keep, sent):
            for t in range(2 * kept):
                total = keep_ref[t] + recv_ref[t].astype(F32)
                if t % 2:
                    sent[t // 2] = total.astype(BF)
                else:
                    keep[t // 2] = total

        shapes = [sds((kept,) + shape, F32), sds((kept,) + shape, BF)]
        self.keep, sent = self.step("_line_next", body, shapes, [], [self.keep, self.from_a], after)
        self.step_size *= 2
        self.from_a = swap(sent, "a", self.step_size)
        return sent

    def final(self, after=()):
        depth = self.keep.shape[1]
        cuts = self.cuts

        def body(keep_ref, recv_ref, *outs):
            total = keep_ref[0] + recv_ref[0].astype(F32)
            at = 0
            for out, (width, fold) in zip(outs, cuts):
                for i in range(fold):
                    out[i * depth : (i + 1) * depth, :] = total[:, at : at + width]
                    at += width

        shapes = [sds((depth * fold, width), F32) for width, fold in cuts]
        return self.step("_final", body, shapes, [], [self.keep, self.from_a], after)


def assemble_kernel(meta, keep_r, count_b, *refs):
    ins, out = refs[: len(meta)], refs[len(meta)]
    at_a, at_b, at_r = (lax.axis_index(name) for name in ("a", "b", "r"))
    for ref, places in zip(ins, meta):
        depth = ref.shape[1]
        for t, (dy, dr, dz) in enumerate(places):
            row = pl.multiple_of(((at_a ^ dz) * count_b + (at_b ^ dy)) * depth, depth)
            if keep_r:
                out[at_r ^ dr, pl.ds(row, depth), :] = ref[t]
            else:
                out[pl.ds(row, depth), :] = ref[t]


def assemble(pieces, name, after=(), keep_r=True):
    count_a, count_b = lax.axis_size("a"), lax.axis_size("b")
    arrays = [piece for piece, _ in pieces]
    meta = [places for _, places in pieces]
    _, depth, width = arrays[0].shape
    shape = (count_a * count_b * depth, width)
    if keep_r:
        shape = (2,) + shape
    return call(
        functools.partial(assemble_kernel, tuple(meta), keep_r, count_b),
        name,
        [sds(shape, BF)],
        [VM] * len(arrays),
        [VM],
        arrays,
        vmem=16,
        after=after,
    )[0]


def normed(values):
    centre = values - jnp.mean(values, axis=-1, keepdims=True)
    spread = lax.rsqrt(jnp.mean(centre * centre, axis=-1, keepdims=True) + 1e-06)
    return centre * spread, spread


def norm_back(grad, norm, spread):
    return spread * (
        grad
        - jnp.mean(grad, axis=-1, keepdims=True)
        - norm * jnp.mean(grad * norm, axis=-1, keepdims=True)
    )


def modulation_part_kernel(low_ref, ada_ref, out_ref):
    low = low_ref[...]
    for i in range(out_ref.shape[1]):
        out_ref[:, i, :] = dot(low, ada_ref[:, i * PAIR : (i + 1) * PAIR])


def modulation_sum_kernel(blocks, in_ref, out_ref):
    groups, slabs = in_ref.shape[0] // blocks, in_ref.shape[1]
    wide = out_ref.shape[1] // PAIR
    for block in range(blocks):
        total = in_ref[block]
        for group in range(1, groups):
            total = total + in_ref[group * blocks + block]
        for i in range(slabs):
            m, c = divmod(block * slabs + i, wide)
            out_ref[m : m + 1, c * PAIR : (c + 1) * PAIR] = total[i : i + 1]


def d_modulation_kernel(blocks, in_ref, mid_ref, gate_ref, out_ref):
    groups, slabs = out_ref.shape[0] // blocks, out_ref.shape[1]
    rows = [in_ref[m : m + 1] for m in range(2)] + [mid_ref[m : m + 1] for m in range(3)]
    rows.append(gate_ref[...])
    wide = gate_ref.shape[1] // PAIR
    for block in range(blocks):
        for i in range(slabs):
            m, c = divmod(block * slabs + i, wide)
            value = rows[m][:, c * PAIR : (c + 1) * PAIR]
            for group in range(groups):
                out_ref[group * blocks + block, i : i + 1, :] = value


def ada_back_kernel(copies, low_ref, rows_ref, ada_ref, grad_ref, out_ref):
    kinds = dict(preferred_element_type=F32, precision=HIGH)
    low, d_low = low_ref[...].astype(F32), 0.0
    for i in range(rows_ref.shape[1]):
        lanes = slice(i * PAIR, (i + 1) * PAIR)
        rows = rows_ref[:, i, :]
        grad_ref[:, lanes] = lax.dot_general(low, rows, TN, **kinds)
        d_low = d_low + lax.dot_general(rows, ada_ref[:, lanes].astype(F32), NT, **kinds)
    for i in range(out_ref.shape[0]):
        start = i // copies * copies
        out_ref[i] = d_low[start : start + copies]


def time_grad_kernel(copies, count_p, in_ref, time_ref, out_ref):
    depth = in_ref.shape[2]
    time = time_ref[...].astype(F32)
    sigmoid = 1.0 / (1.0 + jnp.exp(-time))
    slope = sigmoid * (1.0 + time * (1.0 - sigmoid))
    for group in range(in_ref.shape[0] // copies):
        total = in_ref[group * copies]
        for i in range(1, copies):
            total = total + in_ref[group * copies + i]
        lanes = slice(group * depth, (group + 1) * depth)
        for r in range(2):
            row = jnp.sum(total[r * count_p : (r + 1) * count_p], axis=0, keepdims=True)
            out_ref[r : r + 1, lanes] = row * slope[r : r + 1, lanes]


def attn_input_kernel(steps, *refs):
    x_refs, (mod_ref, out_ref, norm_ref) = refs[:-3], refs[-3:]
    norm, _ = normed(chunk_of(x_refs, steps).astype(F32))
    norm_ref[...] = norm.astype(BF)
    out_ref[...] = (norm * (1.0 + mod_ref[1:2, :]) + mod_ref[0:1, :]).astype(BF)


def lane_ids(width=PAIR):
    return lax.broadcasted_iota(jnp.int32, (1, width), 1)


def turn(values, cosine, sine):
    early = lane_ids() % HEAD_DIM < HEAD_DIM // 2
    step = HEAD_DIM // 2
    other = jnp.where(early, pltpu.roll(values, PAIR - step, 1), pltpu.roll(values, step, 1))
    return values * cosine + other * sine


def qkv_kernel(x_ref, w_ref, cos_ref, sin_ref, q_ref, k_ref, v_ref):
    width = q_ref.shape[1]
    both = dot(x_ref[...], w_ref[...])
    cosine, sine = cos_ref[...], sin_ref[...]
    for lane in range(0, width, PAIR):
        q_ref[:, lane : lane + PAIR] = (
            turn(both[:, lane : lane + PAIR], cosine, sine) * (HEAD_DIM**-0.5 * LOG2E)
        ).astype(BF)
        at = width + lane
        k_ref[:, lane : lane + PAIR] = turn(both[:, at : at + PAIR], cosine, sine).astype(BF)
    v_ref[...] = both[:, 2 * width :].astype(BF)


def attend_kernel(block, q_ref, k_ref, v_ref, aq_ref, ak_ref, *refs):
    o_refs, lse_ref = refs[:-1], refs[-1]
    depth = o_refs[0].shape[0]
    frames = q_ref.shape[0]
    keys = jnp.concatenate([k_ref[...], ak_ref[...]], axis=1)
    values = v_ref[...]
    low = lane_ids() < HEAD_DIM
    zero, one = jnp.zeros((), BF), jnp.ones((), BF)

    def attend(with_max):
        for start in range(0, frames, block):
            rows = pl.ds(start, block)
            query, extra = q_ref[rows, :], aq_ref[rows, :]
            outs, logs = [], []
            for head in range(2):
                mine = low if head == 0 else jnp.logical_not(low)
                left = jnp.concatenate([jnp.where(mine, query, zero), extra], axis=1)
                scores = dot(left, keys, NT)
                if with_max:
                    top = jnp.max(scores, axis=1, keepdims=True)
                    scores = scores - top
                weights = jnp.exp2(scores).astype(BF)
                mixed = dot(weights, jnp.where(mine, values, one))
                outs.append(mixed / pltpu.roll(mixed, HEAD_DIM, 1))
                log = jnp.log2(jnp.maximum(mixed, 1e-30))
                logs.append(log + top if with_max else log)
            both = jnp.where(low, outs[0], outs[1]).astype(BF)
            o_refs[start // depth][pl.ds(start % depth, block), :] = both
            lse_ref[rows, :] = jnp.where(low, logs[1], logs[0])

    query_all, key_all = q_ref[...].astype(F32), k_ref[...].astype(F32)
    bound = jnp.max(jnp.sum(query_all * query_all, axis=1)) * jnp.max(
        jnp.sum(key_all * key_all, axis=1)
    )
    small = bound < 3600.0

    @pl.when(small)
    def _():
        attend(False)

    @pl.when(jnp.logical_not(small))
    def _():
        attend(True)


def split3(values):
    first = values.astype(BF)
    rest = values - first.astype(F32)
    second = rest.astype(BF)
    return first, second, (rest - second.astype(F32)).astype(BF)


def placed(parts, start, base):
    lanes = lane_ids()
    for i, part in enumerate(parts):
        base = jnp.where(lanes == start + i, part, base)
    return base


def attend_back_kernel(block, parts, q_ref, k_ref, v_ref, aq_ref, ak_ref, lse_ref, cos_ref, sin_ref, *refs):
    o_refs, do_refs, (dq_ref, dk_ref, dv_ref) = refs[:parts], refs[parts : 2 * parts], refs[2 * parts :]
    frames = q_ref.shape[0]
    lanes = lane_ids()
    low = lanes < HEAD_DIM
    zero = jnp.zeros((), BF)
    query, extra, lse = q_ref[...], aq_ref[...], lse_ref[...]
    grad = jnp.concatenate([ref[...] for ref in do_refs], axis=0)
    out = jnp.concatenate([ref[...] for ref in o_refs], axis=0)
    product = grad.astype(F32) * out.astype(F32)
    queries, grads, lefts, rights = [], [], [], []
    for head in range(2):
        mine = low if head == 0 else jnp.logical_not(low)
        log = lse[:, HEAD_DIM : HEAD_DIM + 1] if head == 0 else lse[:, 0:1]
        queries.append(jnp.where(mine, query, zero))
        lefts.append(jnp.concatenate([queries[-1], placed(split3(-log), 8, extra)], axis=1))
        inner = -jnp.sum(jnp.where(mine, product, 0.0), axis=1, keepdims=True)
        grads.append(jnp.where(mine, grad, zero))
        tail = placed(split3(inner), 0, jnp.zeros((frames, PAIR), BF))
        rights.append(jnp.concatenate([grads[-1], tail], axis=1))
    ones = jnp.where(lanes < 3, 1.0, 0.0).astype(BF)
    dq_turned = jnp.zeros((PAIR, frames), F32)
    for start in range(0, frames, block):
        rows = pl.ds(start, block)
        key, value = k_ref[rows, :], v_ref[rows, :]
        keys = jnp.concatenate([key, ak_ref[rows, :]], axis=1)
        values = jnp.concatenate([value, jnp.broadcast_to(ones, value.shape)], axis=1)
        dv, dk = 0.0, 0.0
        for head in range(2):
            mine = low if head == 0 else jnp.logical_not(low)
            soft = jnp.exp2(dot(keys, lefts[head], NT))
            d_scores = (soft * dot(values, rights[head], NT)).astype(BF)
            dv = dv + dot(soft.astype(BF), grads[head])
            dk = dk + dot(d_scores, queries[head])
            dq_turned = dq_turned + dot(jnp.where(mine, key, zero), d_scores, TN)
        dv_ref[rows, :] = dv.astype(BF)
        dk_ref[rows, :] = turn(dk * LN2, cos_ref[rows, :], -sin_ref[rows, :]).astype(BF)
    dq = dq_turned.T * HEAD_DIM**-0.5
    dq_ref[...] = turn(dq, cos_ref[...], -sin_ref[...]).astype(BF)


def column(dr, dp):
    at_r, at_p = lax.axis_index("r"), lax.axis_index("p")
    return (at_r ^ dr) * lax.axis_size("p") + (at_p ^ dp)


def lanes_of(index, width):
    return pl.ds(pl.multiple_of(index * width, width), width)


def column_blocks(weight_refs):
    count_r = lax.axis_size("r")
    count_p = lax.axis_size("p")
    at_p = lax.axis_index("p")
    for dp, ref in enumerate(weight_refs):
        for r in range(count_r):
            yield r * count_p + (at_p ^ dp), ref, r


def out_kernel(count_p, x_ref, mod_ref, *refs):
    att_refs = refs[: 2 * count_p]
    w_refs = refs[2 * count_p : 3 * count_p]
    branch_ref, mid_ref, ffn_ref, att_ref, sum_ref = refs[3 * count_p :]
    width = att_refs[0].shape[1]
    for dp in range(count_p):
        for dr in range(2):
            att_ref[:, lanes_of(column(dr, dp), width)] = att_refs[2 * dp + dr][...]
    att = att_ref[...]
    for j, ref, r in column_blocks(w_refs):
        sum_ref[:, lanes_of(j, ref.shape[2])] = dot(att, ref[r])
    branch = sum_ref[...]
    branch_ref[...] = branch.astype(BF)
    mid = x_ref[...].astype(F32) + mod_ref[2:3, :] * branch
    mid_ref[...] = mid
    norm, _ = normed(mid)
    ffn_ref[...] = (norm * (1.0 + mod_ref[4:5, :]) + mod_ref[3:4, :]).astype(BF)


def up_kernel(count_p, x_ref, cot_ref, mod_ref, *refs):
    w_refs, (gelu_ref, slope_ref, dbf_ref) = refs[:count_p], refs[count_p:]
    dbf_ref[...] = (cot_ref[...].astype(F32) * mod_ref[5:6, :]).astype(BF)
    x = x_ref[...]
    root = 0.7978845608028654
    for j, ref, r in column_blocks(w_refs):
        up = dot(x, ref[r])
        square = up * up
        tanh = jnp.tanh(root * (up + 0.044715 * up * square))
        half = 0.5 * (1.0 + tanh)
        at = lanes_of(j, ref.shape[2])
        gelu_ref[:, at] = (up * half).astype(BF)
        slope = half + 0.5 * up * (1.0 - tanh * tanh) * (root * (1.0 + 0.134145 * square))
        slope_ref[:, at] = slope.astype(BF)


def down_kernel(count_p, gelu_ref, mid_ref, cot_ref, mod_ref, *refs):
    w_refs = refs[:count_p]
    own_ref, other_ref, dgate_ref, sum_ref = refs[count_p:]
    gelu = gelu_ref[...]
    for j, ref, r in column_blocks(w_refs):
        sum_ref[:, lanes_of(j, ref.shape[2])] = dot(gelu, ref[r])
    branch = sum_ref[...]
    gate = mod_ref[5:6, :]
    split_rows((mid_ref[...] + gate * branch).astype(BF), own_ref, other_ref)
    cot = cot_ref[...].astype(F32)

    @pl.when(pl.program_id(0) == 0)
    def _():
        dgate_ref[...] = jnp.zeros_like(dgate_ref)

    dgate_ref[...] += jnp.sum(cot * branch, axis=0, keepdims=True)


def turned_dot(x_ref, w_refs):
    total = 0.0
    for j, ref, r in column_blocks(w_refs):
        total = total + dot(x_ref[:, lanes_of(j, ref.shape[2])], ref[r], NT)
    return total


def d_up_kernel(count_p, dbf_ref, slope_ref, *refs):
    w_refs, (out_ref,) = refs[:count_p], refs[count_p:]
    out_ref[...] = (turned_dot(dbf_ref, w_refs) * slope_ref[...].astype(F32)).astype(BF)


def mid_back_kernel(count_p, d_up_ref, mid_ref, cot_ref, branch_ref, mod_ref, *refs):
    up_refs, o_refs = refs[:count_p], refs[count_p : 2 * count_p]
    d_mid_ref, dba_ref, sums_ref = refs[2 * count_p : 2 * count_p + 3]
    att_refs, att_all = refs[2 * count_p + 3 : -1], refs[-1]
    d_in = turned_dot(d_up_ref, up_refs)
    norm, spread = normed(mid_ref[...])

    @pl.when(pl.program_id(0) == 0)
    def _():
        sums_ref[...] = jnp.zeros_like(sums_ref)

    sums_ref[1:2, :] += jnp.sum(d_in, axis=0, keepdims=True)
    sums_ref[2:3, :] += jnp.sum(d_in * norm, axis=0, keepdims=True)
    d_mid = cot_ref[...].astype(F32) + norm_back(d_in * (1.0 + mod_ref[4:5, :]), norm, spread)
    d_mid_ref[...] = d_mid
    sums_ref[0:1, :] += jnp.sum(d_mid * branch_ref[...].astype(F32), axis=0, keepdims=True)
    dba_ref[...] = (d_mid * mod_ref[2:3, :]).astype(BF)
    att_all[...] = turned_dot(dba_ref, o_refs)
    for dp in range(count_p):
        for dr in range(2):
            ref = att_refs[2 * dp + dr]
            ref[...] = att_all[:, lanes_of(column(dr, dp), ref.shape[1])].astype(BF)


def weight_grad_kernel(counts, places, sizes, *refs):
    count_x, count_y = counts
    x_refs, y_refs, out_ref = refs[:count_x], refs[count_x:-1], refs[-1]
    count_a, count_b = sizes
    count_p = lax.axis_size("p")
    at_a, at_b = lax.axis_index("a"), lax.axis_index("b")
    depth = x_refs[0].shape[1] // (count_a * count_b)
    fold = depth // out_ref.shape[-2]
    xs = [ref[...] for ref in x_refs]
    for dp, dr in places:
        if dr is None:
            ys = [jnp.concatenate([ref[...] for ref in y_refs], axis=1)]
        else:
            ys = []
            for ref in y_refs:
                ys.append(ref[:, lanes_of(column(dr, dp), ref.shape[1] // (2 * count_p))])
        at = 0
        for x, y in zip(xs, ys):
            grad = dot(x, y, TN).astype(BF)
            part = depth // fold
            for i in range(count_a * count_b * fold):
                block, piece = divmod(i, fold)
                dz, dy = at_a ^ (block // count_b), at_b ^ (block % count_b)
                rows = grad[i * part : (i + 1) * part]
                lanes = slice(at + piece * y.shape[1], at + (piece + 1) * y.shape[1])
                if dr is None:
                    out_ref[dy, dz, :, lanes] = rows
                else:
                    out_ref[dy, dr, dz, :, lanes] = rows
            at += y.shape[1] * fold


def weight_grad(name, xs, ys, dp=None, after=(), fold=1):
    count_a, count_b = lax.axis_size("a"), lax.axis_size("b")
    depth = xs[0].shape[1] // (count_a * count_b)
    width = sum(y.shape[1] for y in ys)
    if dp is not None:
        width //= 2 * lax.axis_size("p")
        places = [(dp, dr) for dr in reversed(range(2))]
        outs = [sds((count_b, 2, count_a, depth // fold, width * fold), BF)]
    else:
        places = [(0, None)]
        outs = [sds((count_b, count_a, depth, width), BF)]
    return call(
        functools.partial(
            weight_grad_kernel, (len(xs), len(ys)), tuple(places), (count_a, count_b)
        ),
        name,
        outs,
        [VM] * (len(xs) + len(ys)),
        [VM],
        [*xs, *ys],
        after=after,
    )[0]


def chunk_of(refs, steps):
    at = pl.program_id(0) // steps
    value = refs[0][...]
    for i, ref in enumerate(refs[1:]):
        value = jnp.where(at == i + 1, ref[...], value)
    return value


def chunk_specs(tile, steps, count, width):
    return [
        pl.BlockSpec((tile, width), lambda i, c=c: (jnp.clip(i - c * steps, 0, steps - 1), 0))
        for c in range(count)
    ]


def d_attn_kernel(steps, count_p, count_d, *refs):
    d_refs, ws = refs[:count_d], refs[count_d : count_d + 2]
    x_ref, own_ref, outs, sums_ref = refs[count_d + 2], refs[count_d + 3], refs[count_d + 4 : -1], refs[-1]
    d_in = 0.0
    for half, w_ref in enumerate(ws):
        parts = d_refs[half * count_d // 2 : (half + 1) * count_d // 2]
        d_in = d_in + dot(jnp.concatenate([ref[...] for ref in parts], axis=1), w_ref[...], NT)
    norm = x_ref[...].astype(F32)

    @pl.when(pl.program_id(0) == 0)
    def _():
        sums_ref[...] = jnp.zeros_like(sums_ref)

    sums_ref[0:1, :] += jnp.sum(d_in, axis=0, keepdims=True)
    sums_ref[1:2, :] += jnp.sum(d_in * norm, axis=0, keepdims=True)
    at = pl.program_id(0) // steps
    pieces = len(outs) // (count_p - 1) if outs else 0
    for c in range(count_p):

        @pl.when(at == c)
        def _(c=c):
            if c == 0:
                own_ref[...] = d_in
            for i in range(pieces if c else 0):
                out = outs[(c - 1) * pieces + i]
                out[...] = d_in[i * out.shape[0] : (i + 1) * out.shape[0]].astype(BF)


def hidden_back_kernel(pieces, *refs):
    recv, (own_d_ref, x_ref, d_mid_ref, mod_ref, own_ref, other_ref) = refs[:-6], refs[-6:]
    d_in = own_d_ref[...]
    half = pieces // 2
    for i in range(0, len(recv), pieces):
        first = jnp.concatenate([ref[...] for ref in recv[i : i + half]], axis=0)
        second = jnp.concatenate([ref[...] for ref in recv[i + half : i + pieces]], axis=0)
        d_in = d_in + jnp.where(pl.program_id(0) == 0, first, second).astype(F32)
    norm, spread = normed(x_ref[...].astype(F32))
    back = norm_back(d_in * (1.0 + mod_ref[1:2, :]), norm, spread)
    split_rows((d_mid_ref[...] + back).astype(BF), own_ref, other_ref)


def split_rows(value, own_ref, other_ref):
    @pl.when(pl.program_id(0) == 0)
    def _():
        own_ref[...] = value

    @pl.when(pl.program_id(0) == 1)
    def _():
        other_ref[...] = value


def local(
    hidden_in,
    time_embed,
    seg_lengths,
    ada_weight,
    query_weight,
    key_weight,
    value_weight,
    out_weight,
    up_weight,
    down_weight,
    out_cotangent,
):
    count_a, count_b, count_p = (lax.axis_size(name) for name in ("a", "b", "p"))
    at_a, at_b, at_r, at_p = (lax.axis_index(name) for name in ("a", "b", "r", "p"))
    width = hidden_in.shape[2]
    block = hidden_in.shape[1]
    mine = 2 * block
    frames = mine * count_p
    heads_wide = query_weight.shape[1]
    ffn = up_weight.shape[1] * 2 * count_p
    others = range(1, count_p)

    qkv_shard = pack([query_weight, key_weight, value_weight], vmem=60)
    qkv_z = along_line(qkv_shard)
    every = ("a", "b", "r", "p")
    time_vecs = time_embed.astype(F32)
    time_low = jax.nn.silu(time_vecs).astype(BF)
    low_mine = lax.all_to_all(time_low, ("a", "b"), split_axis=1, concat_axis=0, tiled=True)
    low_mine = jnp.repeat(low_mine, count_p, axis=0)
    ada_rows, ada_cols = ada_weight.shape
    devices, blocks = low_mine.shape[0], 2 * count_p
    part = call(
        modulation_part_kernel,
        "modulation_part",
        [sds((devices, ada_cols // PAIR, PAIR), F32)],
        [VM, VM],
        [VM],
        [low_mine, ada_weight],
        vmem=8,
    )[0]
    (hidden_own, hidden_other), (cot_own, cot_other) = exchange_rows(
        [hidden_in, out_cotangent], [qkv_shard]
    )
    qkv_line = stage("stage1", [[qkv_shard, *qkv_z]], [hidden_other, cot_other, part])[0]

    uo_shard = pack([up_weight, out_weight], [qkv_line])
    qkv_r, qkv_b = sideways(qkv_line)
    uo_z = along_line(uo_shard)
    hidden, cotangent = stage(
        "join", [[hidden_own, hidden_other], [cot_own, cot_other]], [uo_shard]
    )
    hidden, cotangent = hidden.reshape(mine, width), cotangent.reshape(mine, width)
    hidden_parts = [hidden] + [swap(hidden, "p", dp) for dp in others]
    part = lax.all_to_all(part, every, split_axis=0, concat_axis=0, tiled=True)
    modulation = call(
        functools.partial(modulation_sum_kernel, blocks),
        "modulation",
        [sds((6, width), F32)],
        [VM],
        [VM],
        [part],
        vmem=8,
    )[0]

    lengths = lax.dynamic_index_in_dim(seg_lengths, at_r, keepdims=False)
    frame_ids = jnp.concatenate(
        [
            ((at_r ^ dr) * count_p + (at_p ^ dp)) * block + jnp.arange(block, dtype=jnp.int32)
            for dp in range(count_p)
            for dr in range(2)
        ]
    )
    passed = frame_ids[:, None] >= jnp.cumsum(lengths)[None, :]
    seg_ids = jnp.sum(passed.astype(jnp.int32), axis=1)
    positions = frame_ids - jnp.sum(jnp.where(passed, lengths[None, :], 0), axis=1)
    half_dim = HEAD_DIM // 2
    lane = jnp.arange(PAIR, dtype=jnp.int32)
    inverse = 10000.0 ** (-(lane % half_dim).astype(F32) / half_dim)
    angles = positions.astype(F32)[:, None] * inverse[None, :]
    cosine = jnp.cos(angles)
    sine = jnp.where(lane % HEAD_DIM < half_dim, -1.0, 1.0)[None, :] * jnp.sin(angles)
    segs = seg_lengths.shape[1]
    same = seg_ids[:, None] == lane[None, :]
    real = (lane < segs)[None, :]
    extra_q = jnp.where(real & ~same, -1e30, 0.0).astype(BF)
    extra_k = jnp.where((real & same) | ((lane >= 8) & (lane < 11))[None, :], 1.0, 0.0).astype(BF)

    pair_block = pl.BlockSpec((frames, PAIR), lambda i: (0, i))
    pair_rows = pl.BlockSpec((mine, PAIR), lambda i: (0, i))
    pair_fixed = fixed(frames, PAIR)
    heads = sds((frames, heads_wide), BF)
    tile = block
    steps = 2
    grid = (steps,)
    full = rows_of(tile, width)
    wide = rows_of(tile, ffn)
    part = rows_of(tile, heads_wide)
    mod_spec = fixed(6, width)

    def project(x, weights, after):
        return call(
            qkv_kernel,
            "qkv",
            [heads] * 3,
            [full, fixed(width, 3 * heads_wide)] + [rows_of(tile, PAIR)] * 2,
            [part] * 3,
            [x, weights, cosine, sine],
            grid=(frames // tile,),
            after=after,
        )

    def attend(three, after):
        return call(
            functools.partial(attend_kernel, min(256, frames)),
            "attend",
            [sds((mine, heads_wide), BF)] * count_p + [sds((frames, heads_wide), F32)],
            [pair_block] * 3 + [pair_fixed] * 2,
            [pair_rows] * count_p + [pair_block],
            [*three, extra_q, extra_k],
            grid=(heads_wide // PAIR,),
            after=after,
        )

    *qkv_halves, uo_shard2 = stage(
        "stage2", halves_of(qkv_r, qkv_b) + [uo_shard], [*qkv_b, *uo_z[:-1]]
    )
    uo_z = uo_z[:-1] + [swap(uo_shard2, "a", count_a - 1)]
    qkv_ends = corners(qkv_halves)
    attn_input, hidden_norm = call(
        functools.partial(attn_input_kernel, steps),
        "attn_input",
        [sds((frames, width), BF)] * 2,
        chunk_specs(tile, steps, count_p, width) + [mod_spec],
        [full] * 2,
        [*hidden_parts, modulation],
        grid=(frames // tile,),
        after=[qkv_halves[0]],
    )
    qkv_w = [assemble(left_blocks(qkv_line, qkv_b), "assemble_qkv", [attn_input], False)]
    qkv = [project(attn_input, qkv_w[0], ())]
    qkv_w.append(assemble(right_blocks(qkv_r, qkv_ends), "assemble_qkv", [qkv[0][0]], False))

    uo_line = stage("stage3", [[uo_shard, *uo_z]], [qkv_w[1]])[0]
    down_shard = pack([down_weight], [uo_line])
    uo_r, uo_b = sideways(uo_line)
    down_z = along_line(down_shard)
    attended = [attend(qkv[0], [down_shard])]
    qkv.append(project(attn_input, qkv_w[1], [attended[0][0]]))
    attended.append(attend(qkv[1], ()))

    *uo_halves, down_line = stage(
        "stage4", halves_of(uo_r, uo_b) + [[down_shard, *down_z]], [attended[1][0], *uo_b]
    )
    uo_ends = corners(uo_halves)

    uo_pieces = left_blocks(uo_line, uo_b) + right_blocks(uo_r, uo_ends)
    uo_w = [assemble(uo_pieces, "assemble_uo", [down_line])]
    uo_w += [swap(uo_w[0], "p", dp) for dp in others]
    down_line = stage("stage5", [down_line], [uo_w[0]])[0]
    down_r, down_b = sideways(down_line)
    att = [attended[dr][0] for dr in range(2)]
    for dp in others:
        att += [swap(attended[dr][dp], "p", dp) for dr in range(2)]
    ffn_block = ffn // (2 * count_p)
    up_specs = [pl.BlockSpec((2, width, ffn_block), lambda i: (0, 0, 0))] * count_p
    out_specs = [pl.BlockSpec((2, width, heads_wide), lambda i: (0, 0, ffn_block // heads_wide))] * count_p
    branch_attn, mid, ffn_input, att_all = call(
        functools.partial(out_kernel, count_p),
        "attn_out",
        [sds((mine, width), BF), sds((mine, width), F32), sds((mine, width), BF), sds((mine, width), BF)],
        [full, mod_spec] + [part] * (2 * count_p) + out_specs,
        [full] * 4,
        [hidden, modulation, *att, *uo_w],
        grid=grid,
        scratch=[pltpu.VMEM((tile, width), F32)],
        after=[down_line],
    )
    gelu_low, slope, d_branch_ffn = call(
        functools.partial(up_kernel, count_p),
        "ffn_up",
        [sds((mine, ffn), BF)] * 2 + [sds((mine, width), BF)],
        [full, full, mod_spec] + up_specs,
        [wide, wide, full],
        [ffn_input, cotangent, modulation, *uo_w],
        grid=grid,
    )

    down_halves = stage("stage6", halves_of(down_r, down_b), [gelu_low, *down_b])
    down_ends = corners(down_halves)
    fold = down_weight.shape[0] // up_weight.shape[0]
    down_wide = down_weight.shape[1]
    down_sum = Scatter("down", [(down_wide, fold)], count_a // 2)
    uo_sum = Scatter("uo", [(ffn_block, 1), (heads_wide, 1)], count_a // 2)
    qkv_sum = Scatter("qkv", [(heads_wide, 1)] * 3, count_a // 4)

    def split_grad(name, xs, ys, token, fold=1):
        sent = []
        for dp in others:
            token = weight_grad(name, xs, ys, dp, [token], fold)
            sent.append(swap(token, "p", dp))
        own = weight_grad(name, xs, ys, 0, [token], fold)
        return [own, *sent]

    down_parts = split_grad("down_grad", [gelu_low], [d_branch_ffn], down_halves[0], fold)
    down_sum.add([down_parts], (0, 1))

    down_pieces = left_blocks(down_line, down_b) + right_blocks(down_r, down_ends)
    down_w = [assemble(down_pieces, "assemble_down", [down_parts[0]])]
    down_w += [swap(down_w[0], "p", dp) for dp in others]
    down_specs = [fixed(*w.shape) for w in down_w]
    token = down_sum.corner([down_w[0]])
    d_up = call(
        functools.partial(d_up_kernel, count_p),
        "d_up",
        [sds((mine, ffn), BF)],
        [full, wide] + down_specs,
        [wide],
        [d_branch_ffn, slope, *down_w],
        grid=grid,
        after=[token],
    )[0]

    token = down_sum.side_b([down_sum.side_r([d_up])])
    d_mid, d_branch_attn, sums_mid, *d_att = call(
        functools.partial(mid_back_kernel, count_p),
        "mid_back",
        [sds((mine, width), F32), sds((mine, width), BF), sds((3, width), F32)]
        + [sds((mine, heads_wide), BF)] * (2 * count_p),
        [wide, full, full, full, mod_spec] + up_specs + out_specs,
        [full, full, fixed(3, width)] + [part] * (2 * count_p),
        [d_up, mid, cotangent, branch_attn, modulation, *uo_w, *uo_w],
        grid=grid,
        scratch=[pltpu.VMEM((tile, width), F32)],
        after=[token],
    )
    token = d_branch_attn
    *out_parts, d_ffn_gate = call(
        functools.partial(down_kernel, count_p),
        "ffn_down",
        [sds((block, width), BF)] * 2 + [sds((1, width), F32)],
        [wide, full, full, mod_spec] + down_specs,
        [fixed(block, width)] * 2 + [fixed(1, width)],
        [gelu_low, mid, cotangent, modulation, *down_w],
        grid=grid,
        scratch=[pltpu.VMEM((tile, width), F32)],
        after=[token],
    )

    token = down_sum.line([out_parts[0]])
    uo_parts = split_grad("uo_grad", [ffn_input, att_all], [d_up, d_branch_attn], token)
    uo_sum.add([uo_parts], (0, 1))
    token = uo_sum.corner()

    pairs = heads_wide // PAIR
    d_heads = [
        [d_att[dr]] + [swap(d_att[2 * dp + dr], "p", dp) for dp in others] for dr in range(2)
    ]

    def attend_back(dr, pair, after):
        whole = pl.BlockSpec((frames, PAIR), lambda i: (0, pair))
        rows = pl.BlockSpec((mine, PAIR), lambda i: (0, pair))
        return call(
            functools.partial(attend_back_kernel, min(512, frames), count_p),
            "attend_back",
            [sds((frames, PAIR), BF)] * 3,
            [whole] * 3 + [pair_fixed] * 2 + [whole] + [pair_fixed] * 2 + [rows] * (2 * count_p),
            [pair_fixed] * 3,
            [
                *qkv[dr],
                extra_q,
                extra_k,
                attended[dr][-1],
                cosine,
                sine,
                *attended[dr][:-1],
                *d_heads[dr],
            ],
            grid=(1,),
            vmem=24,
            after=after,
        )

    def qkv_parts(dr, after):
        return [[weight_grad("qkv_grad", [attn_input], d_qkv[dr], None, after)]]

    d_pairs = [[None] * pairs, [None] * pairs]
    d_qkv = [None, None]

    d_pairs[1][0] = attend_back(1, 0, [token])
    token = down_sum.line_next([d_pairs[1][0][0]])
    token = uo_sum.side_b([uo_sum.side_r([token])])
    for pair in range(1, pairs):
        d_pairs[1][pair] = attend_back(1, pair, [token])
        token = d_pairs[1][pair][0]
    d_qkv[1] = [d_pairs[1][pair][t] for t in range(3) for pair in range(pairs)]
    qkv_sum.add(qkv_parts(1, [token]), (1,))
    down_grad = down_sum.final([qkv_sum.parts[(0, 1)][0][0][0]])[0]
    token = uo_sum.line([down_grad])
    token = qkv_sum.corner([token])
    d_pairs[0][0] = attend_back(0, 0, [token])
    token = uo_sum.line_next([d_pairs[0][0][0]])
    for pair in range(1, pairs):
        d_pairs[0][pair] = attend_back(0, pair, [token])
        token = d_pairs[0][pair][0]
    d_qkv[0] = [d_pairs[0][pair][t] for t in range(3) for pair in range(pairs)]
    qkv_sum.add(qkv_parts(0, [token]), (0,))
    token = qkv_sum.parts[(0, 0)][0][0][0]
    up_grad, out_grad = uo_sum.final([token])
    token = qkv_sum.side_b([qkv_sum.side_r([up_grad])])

    every_d = [*d_qkv[0], *d_qkv[1]]
    pieces = 4
    piece = sds((mine // pieces, width), BF)
    d_own, *d_sent, sums_in = call(
        functools.partial(d_attn_kernel, 1, count_p, len(every_d)),
        "d_attn",
        [sds((mine, width), F32)] + [piece] * (pieces * (count_p - 1)) + [sds((2, width), F32)],
        [rows_of(mine, PAIR)] * len(every_d)
        + [fixed(width, 3 * heads_wide)] * 2
        + [rows_of(mine, width)],
        [fixed(mine, width)]
        + [fixed(*piece.shape)] * (pieces * (count_p - 1))
        + [fixed(2, width)],
        [*every_d, *qkv_w, hidden_norm],
        grid=(count_p,),
        vmem=32,
        after=[token],
    )
    received = [swap(x, "p", 1 + i // pieces) for i, x in enumerate(d_sent)]
    grad_parts = call(
        functools.partial(hidden_back_kernel, pieces),
        "hidden_back",
        [sds((block, width), BF)] * 2,
        [fixed(*piece.shape)] * len(received) + [full, full, full, mod_spec],
        [fixed(block, width)] * 2,
        [*received, d_own, hidden, d_mid, modulation],
        grid=grid,
        after=[token],
    )

    d_mod = call(
        functools.partial(d_modulation_kernel, blocks),
        "d_modulation",
        [sds((devices, ada_cols // PAIR, PAIR), F32)],
        [VM] * 3,
        [VM],
        [sums_in, sums_mid, d_ffn_gate],
        vmem=8,
        after=[grad_parts[0]],
    )[0]
    d_rows = lax.all_to_all(d_mod, every, split_axis=0, concat_axis=0, tiled=True)
    token = qkv_sum.line([d_rows])
    ada_grad, d_low = call(
        functools.partial(ada_back_kernel, blocks),
        "ada_back",
        [sds(ada_weight.shape, F32), sds((devices, blocks, ada_rows), F32)],
        [VM] * 3,
        [VM] * 2,
        [low_mine, d_rows, ada_weight],
        vmem=16,
        after=[token],
    )
    token = qkv_sum.line_next([d_low])
    hidden_out = restore_rows(*out_parts, [token])
    d_low = lax.all_to_all(d_low, every, split_axis=0, concat_axis=0, tiled=True)
    time_grad = call(
        functools.partial(time_grad_kernel, blocks, count_p),
        "time_grad",
        [sds((2, width), F32)],
        [VM] * 2,
        [VM],
        [d_low, time_embed],
        vmem=8,
    )[0]
    hidden_grad = restore_rows(*grad_parts, [time_grad])
    query_grad, key_grad, value_grad = qkv_sum.final([hidden_grad])

    return (
        hidden_out,
        hidden_grad,
        time_grad,
        ada_grad,
        query_grad,
        key_grad,
        value_grad,
        out_grad,
        up_grad,
        down_grad,
    )


def solution(mesh):
    count_dp, count_sp = mesh.shape["dp"], mesh.shape["sp"]
    fine = Mesh(mesh.devices.reshape(4, count_dp // 4, 2, count_sp // 2), ("a", "b", "r", "p"))
    dp, sp = ("a", "b"), ("r", "p")
    in_specs = (
        (P(dp, sp, None), P(dp, None), P(dp, None)) + (P(dp, sp),) * 7 + (P(dp, sp, None),)
    )
    out_specs = (P(dp, sp, None), P(dp, sp, None), P(dp, None)) + (P(dp, sp),) * 7
    return jax.shard_map(local, mesh=fine, in_specs=in_specs, out_specs=out_specs, check_vma=False)
```

```python
import functools

import jax
import jax.numpy as jnp
from jax import lax
from jax.experimental import pallas as pl
from jax.experimental.pallas import tpu as pltpu
from jax.sharding import Mesh
from jax.sharding import PartitionSpec as P

HEAD_DIM = 64
PAIR = 2 * HEAD_DIM
LOG2E = 1.4426950408889634
LN2 = 0.6931471805599453
HIGH = lax.Precision.HIGHEST
F32 = jnp.float32
BF = jnp.bfloat16
NN = (((1,), (0,)), ((), ()))
NT = (((1,), (1,)), ((), ()))
TN = (((0,), (0,)), ((), ()))
ANY = pl.BlockSpec(memory_space=pl.ANY)
HBM = pl.BlockSpec(memory_space=pltpu.HBM)
VM = pl.BlockSpec(memory_space=pltpu.VMEM)
MIB = 1 << 20
TILE = 128


def dot(left, right, dims=NN):
    return lax.dot_general(left, right, dims, preferred_element_type=F32)


def sds(shape, dtype):
    return jax.ShapeDtypeStruct(shape, dtype)


def call(kernel, name, outs, args, scratch=(), vmem=9, after=(), spec=VM, to=VM):
    taken = len(args)

    def body(*refs):
        kernel(*refs[:taken], *refs[taken + len(after) :])

    return pl.pallas_call(
        body,
        name=name,
        in_specs=[spec] * taken + [ANY] * len(after),
        out_specs=[to] * len(outs),
        out_shape=outs,
        scratch_shapes=scratch,
        compiler_params=pltpu.CompilerParams(vmem_limit_bytes=vmem * MIB),
        cost_estimate=pl.CostEstimate(flops=1, bytes_accessed=1, transcendentals=0),
    )(*args, *after)


def swap(value, axis, offset=1):
    count = lax.axis_size(axis)
    return lax.ppermute(value, axis, [(i, i ^ offset) for i in range(count)])


def stage_kernel(plan, *refs):
    count = sum(len(pieces) for pieces in plan)
    ins, outs = iter(refs[:count]), refs[count:]
    for pieces, out in zip(plan, outs):
        at = 0
        for start, size in pieces:
            ref = next(ins)
            if start is not None:
                out[at : at + size] = ref[start : start + size]
            elif len(ref.shape) < len(out.shape):
                out[at] = ref[...]
            else:
                out[...] = ref[...]
            at += size


def stage(name, groups, after=()):
    arrays, plan, outs = [], [], []
    for group in groups:
        if not isinstance(group, list):
            arrays.append(group)
            plan.append(((None, 1),))
            outs.append(sds(group.shape, group.dtype))
            continue
        pieces, total = [], 0
        for piece in group:
            array, start, size = piece if isinstance(piece, tuple) else (piece, None, 1)
            arrays.append(array)
            pieces.append((start, size))
            total += size
        tail = array.shape if start is None else array.shape[1:]
        plan.append(tuple(pieces))
        outs.append(sds((total,) + tail, array.dtype))
    return call(
        functools.partial(stage_kernel, tuple(plan)),
        name,
        outs,
        arrays,
        vmem=12,
        after=after,
    )


def pick_kernel(*refs):
    count = (len(refs) - 1) // 3
    ins, outs, sems = refs[:count], refs[count:-1], refs[-1]
    at_r = lax.axis_index("r")
    copies = []
    for i, ref in enumerate(ins):
        for j, row in enumerate((at_r, 1 - at_r)):
            at = 2 * i + j
            copies.append(pltpu.make_async_copy(ref.at[row], outs[at], sems.at[at]))
    for copy in copies:
        copy.start()
    for copy in copies:
        copy.wait()


def exchange_rows(arrays, after=()):
    outs = [sds(x.shape[1:], x.dtype) for x in arrays for _ in range(2)]
    picked = call(
        pick_kernel,
        "pick_rows",
        outs,
        arrays,
        scratch=[pltpu.SemaphoreType.DMA((len(outs),))],
        vmem=60,
        after=after,
        spec=HBM,
    )
    return [(own, swap(other, "r")) for own, other in zip(picked[::2], picked[1::2])]


def place_kernel(own_ref, other_ref, out_ref, sems):
    at_r = lax.axis_index("r")
    copies = [
        pltpu.make_async_copy(own_ref, out_ref.at[at_r], sems.at[0]),
        pltpu.make_async_copy(other_ref, out_ref.at[1 - at_r], sems.at[1]),
    ]
    for copy in copies:
        copy.start()
    for copy in copies:
        copy.wait()


def restore_rows(own, other, after=()):
    outs = [sds((2,) + own.shape, own.dtype)]
    args = [own, swap(other, "r")]
    sems = [pltpu.SemaphoreType.DMA((2,))]
    return call(
        place_kernel, "place_rows", outs, args, scratch=sems, vmem=8, after=after, to=HBM
    )[0]


def pack_kernel(*refs):
    ins, (out, sems) = refs[:-2], refs[-2:]
    at, copies = 0, []
    for i, ref in enumerate(ins):
        place = out.at[:, pl.ds(at, ref.shape[1])]
        copies.append(pltpu.make_async_copy(ref, place, sems.at[i]))
        at += ref.shape[1]
    for copy in copies:
        copy.start()
    for copy in copies:
        copy.wait()


def pack(shards, after=(), vmem=8):
    width = sum(x.shape[1] for x in shards)
    outs = [sds((shards[0].shape[0], width), BF)]
    return call(
        pack_kernel,
        "pack",
        outs,
        shards,
        scratch=[pltpu.SemaphoreType.DMA((len(shards),))],
        vmem=vmem,
        after=after,
        spec=HBM,
    )[0]


def along_line(shard):
    return [swap(shard, "a", d) for d in range(1, lax.axis_size("a"))]


def sideways(first):
    return swap(first, "r"), [swap(first, "b", dy) for dy in range(1, lax.axis_size("b"))]


def halves_of(side_r, sides_b):
    half = side_r.shape[0] // 2
    return [[(side, 0, half)] for side in sides_b] + [[(side_r, half, half)]]


def corners(halves):
    *sides_b, side_r = halves
    return [
        (swap(side_b, "r"), swap(side_r, "b", dy + 1)) for dy, side_b in enumerate(sides_b)
    ]


def span(dy, dr, start, stop):
    return [(dy, dr, dz) for dz in range(start, stop)]


def left_blocks(first, sides_b):
    line = first.shape[0]
    left = [(first, span(0, 0, 0, line))]
    return left + [(side, span(dy + 1, 0, 0, line)) for dy, side in enumerate(sides_b)]


def right_blocks(side_r, ends):
    line = side_r.shape[0]
    right = [(side_r, span(0, 1, 0, line))]
    for dy, (low, high) in enumerate(ends):
        right.append((low, span(dy + 1, 1, 0, line // 2)))
        right.append((high, span(dy + 1, 1, line // 2, line)))
    return right


def totals(refs, members, t):
    wide, refs = [], iter(refs)
    for member in members:
        wide.append(sum(next(refs)[index + (t,)].astype(F32) for _, index in member))
    return wide[0] if len(wide) == 1 else jnp.concatenate(wide, axis=1)


class Scatter:
    def __init__(self, name, cuts, cut):
        self.name, self.cuts, self.cut = name, cuts, cut
        self.line_count = lax.axis_size("a")
        self.count_b = lax.axis_size("b")
        self.parts = {}
        self.first_r = {dy: [] for dy in range(1, self.count_b)}
        self.first_b = {dy: [] for dy in range(1, self.count_b)}

    def add(self, members, rights):
        for dy in range(self.count_b):
            for at, dr in enumerate(rights):
                index = (dy,) if len(rights) == 1 else (dy, at)
                found = self.parts.setdefault((dy, dr), [])
                found += [[(x, index) for x in member] for member in members]

    def step(self, label, body, shapes, members, extra, after):
        arrays = [array for member in members for array, _ in member]
        return call(body, self.name + label, shapes, arrays + extra, after=after)

    def block(self, members):
        return members[0][0][0].shape[-2], sum(member[0][0].shape[-1] for member in members)

    def corner(self, after=(), some=slice(None)):
        cut, line = self.cut, self.line_count
        for dy in range(1, self.count_b):
            members = self.parts[(dy, 1)][some]
            shape = self.block(members)

            def body(*refs, members=members):
                for t in range(line):
                    out, at = (refs[-2], t) if t < cut else (refs[-1], t - cut)
                    out[at] = totals(refs, members, t).astype(BF)

            shapes = [sds((cut,) + shape, BF), sds((line - cut,) + shape, BF)]
            first, second = self.step("_corner", body, shapes, members, [], after)
            self.first_r[dy].append(swap(first, "r"))
            self.first_b[dy].append(swap(second, "b", dy))
        return first

    def side_r(self, after=()):
        members = self.parts[(0, 1)]
        groups = list(self.first_b.values())
        extra = [x for group in groups for x in group]
        cut, line = self.cut, self.line_count

        def body(*refs):
            more, out = refs[-1 - len(extra) : -1], refs[-1]
            for t in range(line):
                total = totals(refs, members, t)
                if t >= cut:
                    total = total + self.added(more, len(groups), t - cut)
                out[t] = total.astype(BF)

        shapes = [sds((line,) + self.block(members), BF)]
        after = [*after, *[x for group in self.first_r.values() for x in group]]
        side = self.step("_side_r", body, shapes, members, extra, after)[0]
        self.from_r = swap(side, "r")
        return side

    def added(self, refs, groups, t):
        each = len(refs) // groups
        total = 0.0
        for at in range(0, len(refs), each):
            pieces = [ref[t].astype(F32) for ref in refs[at : at + each]]
            total = total + (pieces[0] if each == 1 else jnp.concatenate(pieces, axis=1))
        return total

    def side_b(self, after=()):
        self.from_b = []
        cut, line = self.cut, self.line_count
        for dy in range(1, self.count_b):
            members = self.parts[(dy, 0)]
            extra = self.first_r[dy]

            def body(*refs, members=members, extra=extra):
                more, out = refs[-1 - len(extra) : -1], refs[-1]
                for t in range(line):
                    total = totals(refs, members, t)
                    if t < cut:
                        total = total + self.added(more, 1, t)
                    out[t] = total.astype(BF)

            shapes = [sds((line,) + self.block(members), BF)]
            side = self.step("_side_b", body, shapes, members, extra, after)[0]
            self.from_b.append(swap(side, "b", dy))
        return side

    def line(self, after=()):
        members = self.parts[(0, 0)]
        shape, line = self.block(members), self.line_count
        extra = [self.from_r, *self.from_b]
        kept = line // 2

        def body(*refs):
            more, (keep, sent) = refs[-2 - len(extra) : -2], refs[-2:]
            for t in range(line):
                total = totals(refs, members, t) + sum(ref[t].astype(F32) for ref in more)
                if t % 2:
                    sent[t // 2] = total.astype(BF)
                else:
                    keep[t // 2] = total

        shapes = [sds((kept,) + shape, F32), sds((kept,) + shape, BF)]
        self.keep, sent = self.step("_line", body, shapes, members, extra, after)
        self.step_size, self.from_a = 1, swap(sent, "a", 1)
        return sent

    def line_next(self, after=()):
        kept = self.keep.shape[0] // 2
        shape = self.keep.shape[1:]

        def body(keep_ref, recv_ref, keep, sent):
            for t in range(2 * kept):
                total = keep_ref[t] + recv_ref[t].astype(F32)
                if t % 2:
                    sent[t // 2] = total.astype(BF)
                else:
                    keep[t // 2] = total

        shapes = [sds((kept,) + shape, F32), sds((kept,) + shape, BF)]
        self.keep, sent = self.step("_line_next", body, shapes, [], [self.keep, self.from_a], after)
        self.step_size *= 2
        self.from_a = swap(sent, "a", self.step_size)
        return sent

    def final(self, after=()):
        depth = self.keep.shape[1]
        cuts = self.cuts

        def body(keep_ref, recv_ref, *outs):
            total = keep_ref[0] + recv_ref[0].astype(F32)
            at = 0
            for out, (width, fold) in zip(outs, cuts):
                for i in range(fold):
                    out[i * depth : (i + 1) * depth, :] = total[:, at : at + width]
                    at += width

        shapes = [sds((depth * fold, width), F32) for width, fold in cuts]
        return self.step("_final", body, shapes, [], [self.keep, self.from_a], after)


def assemble_kernel(meta, keep_r, count_b, *refs):
    ins, out = refs[: len(meta)], refs[len(meta)]
    at_a, at_b, at_r = (lax.axis_index(name) for name in ("a", "b", "r"))
    for ref, places in zip(ins, meta):
        depth = ref.shape[1]
        for t, (dy, dr, dz) in enumerate(places):
            row = pl.multiple_of(((at_a ^ dz) * count_b + (at_b ^ dy)) * depth, depth)
            if keep_r:
                out[at_r ^ dr, pl.ds(row, depth), :] = ref[t]
            else:
                out[pl.ds(row, depth), :] = ref[t]


def assemble(pieces, name, after=(), keep_r=True):
    count_a, count_b = lax.axis_size("a"), lax.axis_size("b")
    arrays = [piece for piece, _ in pieces]
    meta = [places for _, places in pieces]
    _, depth, width = arrays[0].shape
    shape = (count_a * count_b * depth, width)
    if keep_r:
        shape = (2,) + shape
    return call(
        functools.partial(assemble_kernel, tuple(meta), keep_r, count_b),
        name,
        [sds(shape, BF)],
        arrays,
        vmem=16,
        after=after,
    )[0]


def normed(values):
    centre = values - jnp.mean(values, axis=-1, keepdims=True)
    spread = lax.rsqrt(jnp.mean(centre * centre, axis=-1, keepdims=True) + 1e-06)
    return centre * spread, spread


def norm_back(grad, norm, spread):
    return spread * (
        grad
        - jnp.mean(grad, axis=-1, keepdims=True)
        - norm * jnp.mean(grad * norm, axis=-1, keepdims=True)
    )


def modulation_part_kernel(low_ref, ada_ref, out_ref):
    low = low_ref[...]
    for i in range(out_ref.shape[1]):
        out_ref[:, i, :] = dot(low, ada_ref[:, i * PAIR : (i + 1) * PAIR])


def modulation_sum_kernel(blocks, in_ref, out_ref):
    groups, slabs = in_ref.shape[0] // blocks, in_ref.shape[1]
    wide = out_ref.shape[1] // PAIR
    for block in range(blocks):
        total = in_ref[block]
        for group in range(1, groups):
            total = total + in_ref[group * blocks + block]
        for i in range(slabs):
            m, c = divmod(block * slabs + i, wide)
            out_ref[m : m + 1, c * PAIR : (c + 1) * PAIR] = total[i : i + 1]


def d_modulation_kernel(blocks, in_ref, mid_ref, gate_ref, out_ref):
    groups, slabs = out_ref.shape[0] // blocks, out_ref.shape[1]
    rows = [in_ref[m : m + 1] for m in range(2)] + [mid_ref[m : m + 1] for m in range(3)]
    rows.append(gate_ref[...])
    wide = gate_ref.shape[1] // PAIR
    for block in range(blocks):
        for i in range(slabs):
            m, c = divmod(block * slabs + i, wide)
            value = rows[m][:, c * PAIR : (c + 1) * PAIR]
            for group in range(groups):
                out_ref[group * blocks + block, i : i + 1, :] = value


def ada_back_kernel(copies, low_ref, rows_ref, ada_ref, grad_ref, out_ref):
    kinds = dict(preferred_element_type=F32, precision=HIGH)
    low, d_low = low_ref[...].astype(F32), 0.0
    for i in range(rows_ref.shape[1]):
        lanes = slice(i * PAIR, (i + 1) * PAIR)
        rows = rows_ref[:, i, :]
        grad_ref[:, lanes] = lax.dot_general(low, rows, TN, **kinds)
        d_low = d_low + lax.dot_general(rows, ada_ref[:, lanes].astype(F32), NT, **kinds)
    for i in range(out_ref.shape[0]):
        start = i // copies * copies
        out_ref[i] = d_low[start : start + copies]


def time_grad_kernel(copies, count_p, in_ref, time_ref, out_ref):
    depth = in_ref.shape[2]
    time = time_ref[...].astype(F32)
    sigmoid = 1.0 / (1.0 + jnp.exp(-time))
    slope = sigmoid * (1.0 + time * (1.0 - sigmoid))
    for group in range(in_ref.shape[0] // copies):
        total = in_ref[group * copies]
        for i in range(1, copies):
            total = total + in_ref[group * copies + i]
        lanes = slice(group * depth, (group + 1) * depth)
        for r in range(2):
            row = jnp.sum(total[r * count_p : (r + 1) * count_p], axis=0, keepdims=True)
            out_ref[r : r + 1, lanes] = row * slope[r : r + 1, lanes]


def attn_input_kernel(*refs):
    x_refs, (mod_ref, out_ref, norm_ref) = refs[:-3], refs[-3:]
    scale, shift = 1.0 + mod_ref[1:2, :], mod_ref[0:1, :]
    at = 0
    for ref in x_refs:
        for row in range(0, ref.shape[0], TILE):
            norm, _ = normed(ref[row : row + TILE, :].astype(F32))
            rows = slice(at + row, at + row + TILE)
            norm_ref[rows, :] = norm.astype(BF)
            out_ref[rows, :] = (norm * scale + shift).astype(BF)
        at += ref.shape[0]


def lane_ids(width=PAIR):
    return lax.broadcasted_iota(jnp.int32, (1, width), 1)


def turn(values, cosine, sine):
    early = lane_ids() % HEAD_DIM < HEAD_DIM // 2
    step = HEAD_DIM // 2
    other = jnp.where(early, pltpu.roll(values, PAIR - step, 1), pltpu.roll(values, step, 1))
    return values * cosine + other * sine


def qkv_kernel(x_ref, w_ref, cos_ref, sin_ref, q_ref, k_ref, v_ref):
    width = q_ref.shape[1]
    weights = w_ref[...]
    step = min(512, x_ref.shape[0])
    for row in range(0, x_ref.shape[0], step):
        rows = slice(row, row + step)
        both = dot(x_ref[rows, :], weights)
        cosine, sine = cos_ref[rows, :], sin_ref[rows, :]
        for lane in range(0, width, PAIR):
            lanes, at = slice(lane, lane + PAIR), width + lane
            query = turn(both[:, lanes], cosine, sine) * (HEAD_DIM**-0.5 * LOG2E)
            q_ref[rows, lanes] = query.astype(BF)
            k_ref[rows, lanes] = turn(both[:, at : at + PAIR], cosine, sine).astype(BF)
        v_ref[rows, :] = both[:, 2 * width :].astype(BF)


def attend_kernel(block, q_ref, k_ref, v_ref, aq_ref, ak_ref, *refs):
    o_refs, lse_ref = refs[:-1], refs[-1]
    depth = o_refs[0].shape[0]
    frames = q_ref.shape[0]
    keys = jnp.concatenate([k_ref[...], ak_ref[...]], axis=1)
    values = v_ref[...]
    low = lane_ids() < HEAD_DIM
    zero, one = jnp.zeros((), BF), jnp.ones((), BF)

    def attend(with_max):
        for start in range(0, frames, block):
            rows = pl.ds(start, block)
            query, extra = q_ref[rows, :], aq_ref[rows, :]
            outs, logs = [], []
            for head in range(2):
                mine = low if head == 0 else jnp.logical_not(low)
                left = jnp.concatenate([jnp.where(mine, query, zero), extra], axis=1)
                scores = dot(left, keys, NT)
                if with_max:
                    top = jnp.max(scores, axis=1, keepdims=True)
                    scores = scores - top
                weights = jnp.exp2(scores).astype(BF)
                mixed = dot(weights, jnp.where(mine, values, one))
                outs.append(mixed / pltpu.roll(mixed, HEAD_DIM, 1))
                log = jnp.log2(jnp.maximum(mixed, 1e-30))
                logs.append(log + top if with_max else log)
            both = jnp.where(low, outs[0], outs[1]).astype(BF)
            o_refs[start // depth][pl.ds(start % depth, block), :] = both
            lse_ref[rows, :] = jnp.where(low, logs[1], logs[0])

    query_all, key_all = q_ref[...].astype(F32), k_ref[...].astype(F32)
    bound = jnp.max(jnp.sum(query_all * query_all, axis=1)) * jnp.max(
        jnp.sum(key_all * key_all, axis=1)
    )
    small = bound < 3600.0

    @pl.when(small)
    def _():
        attend(False)

    @pl.when(jnp.logical_not(small))
    def _():
        attend(True)


def split3(values):
    first = values.astype(BF)
    rest = values - first.astype(F32)
    second = rest.astype(BF)
    return first, second, (rest - second.astype(F32)).astype(BF)


def placed(parts, start, base):
    lanes = lane_ids()
    for i, part in enumerate(parts):
        base = jnp.where(lanes == start + i, part, base)
    return base


def attend_back_kernel(block, parts, lanes_at, q_ref, k_ref, v_ref, aq_ref, ak_ref, lse_ref, cos_ref, sin_ref, *refs):
    o_refs, do_refs, (dq_ref, dk_ref, dv_ref) = refs[:parts], refs[parts : 2 * parts], refs[2 * parts :]
    frames = q_ref.shape[0]
    at = slice(lanes_at, lanes_at + PAIR)
    lanes = lane_ids()
    low = lanes < HEAD_DIM
    zero = jnp.zeros((), BF)
    query, extra, lse = q_ref[:, at], aq_ref[...], lse_ref[:, at]
    grad = jnp.concatenate([ref[:, at] for ref in do_refs], axis=0)
    out = jnp.concatenate([ref[:, at] for ref in o_refs], axis=0)
    product = grad.astype(F32) * out.astype(F32)
    queries, grads, lefts, rights = [], [], [], []
    for head in range(2):
        mine = low if head == 0 else jnp.logical_not(low)
        log = lse[:, HEAD_DIM : HEAD_DIM + 1] if head == 0 else lse[:, 0:1]
        queries.append(jnp.where(mine, query, zero))
        lefts.append(jnp.concatenate([queries[-1], placed(split3(-log), 8, extra)], axis=1))
        inner = -jnp.sum(jnp.where(mine, product, 0.0), axis=1, keepdims=True)
        grads.append(jnp.where(mine, grad, zero))
        tail = placed(split3(inner), 0, jnp.zeros((frames, PAIR), BF))
        rights.append(jnp.concatenate([grads[-1], tail], axis=1))
    ones = jnp.where(lanes < 3, 1.0, 0.0).astype(BF)
    dq_turned = jnp.zeros((PAIR, frames), F32)
    for start in range(0, frames, block):
        rows = pl.ds(start, block)
        key, value = k_ref[rows, at], v_ref[rows, at]
        keys = jnp.concatenate([key, ak_ref[rows, :]], axis=1)
        values = jnp.concatenate([value, jnp.broadcast_to(ones, value.shape)], axis=1)
        dv, dk = 0.0, 0.0
        for head in range(2):
            mine = low if head == 0 else jnp.logical_not(low)
            soft = jnp.exp2(dot(keys, lefts[head], NT))
            d_scores = (soft * dot(values, rights[head], NT)).astype(BF)
            dv = dv + dot(soft.astype(BF), grads[head])
            dk = dk + dot(d_scores, queries[head])
            dq_turned = dq_turned + dot(jnp.where(mine, key, zero), d_scores, TN)
        dv_ref[rows, :] = dv.astype(BF)
        dk_ref[rows, :] = turn(dk * LN2, cos_ref[rows, :], -sin_ref[rows, :]).astype(BF)
    dq = dq_turned.T * HEAD_DIM**-0.5
    dq_ref[...] = turn(dq, cos_ref[...], -sin_ref[...]).astype(BF)


def column(dr, dp):
    at_r, at_p = lax.axis_index("r"), lax.axis_index("p")
    return (at_r ^ dr) * lax.axis_size("p") + (at_p ^ dp)


def lanes_of(index, width):
    return pl.ds(pl.multiple_of(index * width, width), width)


def column_blocks(weight_refs):
    count_r = lax.axis_size("r")
    count_p = lax.axis_size("p")
    at_p = lax.axis_index("p")
    for dp, ref in enumerate(weight_refs):
        for r in range(count_r):
            yield r * count_p + (at_p ^ dp), ref, r


def out_kernel(count_p, at_lane, x_ref, mod_ref, *refs):
    att_refs = refs[: 2 * count_p]
    w_refs = refs[2 * count_p : 3 * count_p]
    branch_ref, mid_ref, ffn_ref, att_ref, sum_ref = refs[3 * count_p :]
    width = att_refs[0].shape[1]
    for dp in range(count_p):
        for dr in range(2):
            att_ref[:, lanes_of(column(dr, dp), width)] = att_refs[2 * dp + dr][...]
    att = att_ref[...]
    for j, ref, r in column_blocks(w_refs):
        sum_ref[:, lanes_of(j, width)] = dot(att, ref[r, :, at_lane : at_lane + width])
    gate, scale, shift = mod_ref[2:3, :], 1.0 + mod_ref[4:5, :], mod_ref[3:4, :]
    for row in range(0, x_ref.shape[0], TILE):
        rows = slice(row, row + TILE)
        branch = sum_ref[rows, :]
        branch_ref[rows, :] = branch.astype(BF)
        mid = x_ref[rows, :].astype(F32) + gate * branch
        mid_ref[rows, :] = mid
        norm, _ = normed(mid)
        ffn_ref[rows, :] = (norm * scale + shift).astype(BF)


def up_kernel(count_p, wide, x_ref, cot_ref, mod_ref, *refs):
    w_refs, (gelu_ref, slope_ref, dbf_ref) = refs[:count_p], refs[count_p:]
    dbf_ref[...] = (cot_ref[...].astype(F32) * mod_ref[5:6, :]).astype(BF)
    x = x_ref[...]
    root = 0.7978845608028654
    for j, ref, r in column_blocks(w_refs):
        up = dot(x, ref[r, :, :wide])
        square = up * up
        tanh = jnp.tanh(up * (root + (root * 0.044715) * square))
        half = 0.5 + 0.5 * tanh
        at = lanes_of(j, wide)
        gelu_ref[:, at] = (up * half).astype(BF)
        slope = half + up * (1.0 - tanh * tanh) * (0.5 * root + (0.5 * root * 0.134145) * square)
        slope_ref[:, at] = slope.astype(BF)


def down_kernel(count_p, gelu_ref, mid_ref, cot_ref, mod_ref, *refs):
    w_refs = refs[:count_p]
    out_refs, (dgate_ref, sum_ref) = refs[count_p:-2], refs[-2:]
    gelu = gelu_ref[...]
    for j, ref, r in column_blocks(w_refs):
        sum_ref[:, lanes_of(j, ref.shape[2])] = dot(gelu, ref[r])
    gate, total, depth = mod_ref[5:6, :], 0.0, out_refs[0].shape[0]
    for row in range(0, mid_ref.shape[0], TILE):
        rows = slice(row, row + TILE)
        branch = sum_ref[rows, :]
        place = out_refs[row // depth]
        place[row % depth : row % depth + TILE, :] = (mid_ref[rows, :] + gate * branch).astype(BF)
        total = total + jnp.sum(cot_ref[rows, :].astype(F32) * branch, axis=0, keepdims=True)
    dgate_ref[...] = total


def turned_dot(x_ref, w_refs, start=0, width=None):
    total = 0.0
    for j, ref, r in column_blocks(w_refs):
        wide = width or ref.shape[2]
        total = total + dot(x_ref[:, lanes_of(j, wide)], ref[r, :, start : start + wide], NT)
    return total


def d_up_kernel(count_p, dbf_ref, slope_ref, *refs):
    w_refs, (out_ref,) = refs[:count_p], refs[count_p:]
    out_ref[...] = (turned_dot(dbf_ref, w_refs) * slope_ref[...].astype(F32)).astype(BF)


def mid_back_kernel(count_p, wide, d_up_ref, mid_ref, cot_ref, branch_ref, mod_ref, *refs):
    w_refs = refs[:count_p]
    d_mid_ref, dba_ref, sums_ref = refs[count_p : count_p + 3]
    att_refs, all_ref = refs[count_p + 3 : -1], refs[-1]
    all_ref[...] = turned_dot(d_up_ref, w_refs, 0, wide)
    scale, gate = 1.0 + mod_ref[4:5, :], mod_ref[2:3, :]
    sums = [0.0, 0.0, 0.0]
    for row in range(0, mid_ref.shape[0], TILE):
        rows = slice(row, row + TILE)
        d_in = all_ref[rows, :]
        norm, spread = normed(mid_ref[rows, :])
        d_mid = cot_ref[rows, :].astype(F32) + norm_back(d_in * scale, norm, spread)
        d_mid_ref[rows, :] = d_mid.astype(BF)
        dba_ref[rows, :] = (d_mid * gate).astype(BF)
        parts = (d_mid * branch_ref[rows, :].astype(F32), d_in, d_in * norm)
        sums = [s + jnp.sum(part, axis=0, keepdims=True) for s, part in zip(sums, parts)]
    for i in range(3):
        sums_ref[i : i + 1, :] = sums[i]
    width = att_refs[0].shape[1]
    all_ref[...] = turned_dot(dba_ref, w_refs, wide, width)
    for dp in range(count_p):
        for dr in range(2):
            att_refs[2 * dp + dr][...] = all_ref[:, lanes_of(column(dr, dp), width)].astype(BF)


def weight_grad_kernel(counts, places, sizes, *refs):
    count_x, count_y = counts
    x_refs, y_refs, out_ref = refs[:count_x], refs[count_x:-1], refs[-1]
    count_a, count_b = sizes
    count_p = lax.axis_size("p")
    at_a, at_b = lax.axis_index("a"), lax.axis_index("b")
    depth = x_refs[0].shape[1] // (count_a * count_b)
    fold = depth // out_ref.shape[-2]
    xs = [ref[...] for ref in x_refs]
    for dp, dr in places:
        if dr is None:
            ys = [jnp.concatenate([ref[...] for ref in y_refs], axis=1)]
        else:
            ys = []
            for ref in y_refs:
                ys.append(ref[:, lanes_of(column(dr, dp), ref.shape[1] // (2 * count_p))])
        at = 0
        for x, y in zip(xs, ys):
            grad = dot(x, y, TN).astype(BF)
            part = depth // fold
            for i in range(count_a * count_b * fold):
                block, piece = divmod(i, fold)
                dz, dy = at_a ^ (block // count_b), at_b ^ (block % count_b)
                rows = grad[i * part : (i + 1) * part]
                lanes = slice(at + piece * y.shape[1], at + (piece + 1) * y.shape[1])
                if dr is None:
                    out_ref[dy, dz, :, lanes] = rows
                else:
                    out_ref[dy, dr, dz, :, lanes] = rows
            at += y.shape[1] * fold


def weight_grad(name, xs, ys, dp=None, after=(), fold=1):
    count_a, count_b = lax.axis_size("a"), lax.axis_size("b")
    depth = xs[0].shape[1] // (count_a * count_b)
    width = sum(y.shape[1] for y in ys)
    if dp is not None:
        width //= 2 * lax.axis_size("p")
        places = [(dp, dr) for dr in reversed(range(2))]
        outs = [sds((count_b, 2, count_a, depth // fold, width * fold), BF)]
    else:
        places = [(0, None)]
        outs = [sds((count_b, count_a, depth, width), BF)]
    return call(
        functools.partial(
            weight_grad_kernel, (len(xs), len(ys)), tuple(places), (count_a, count_b)
        ),
        name,
        outs,
        [*xs, *ys],
        after=after,
    )[0]


def d_attn_kernel(count_p, count_d, *refs):
    d_refs, ws = refs[:count_d], refs[count_d : count_d + 2]
    x_ref, own_ref, outs, sums_ref = refs[count_d + 2], refs[count_d + 3], refs[count_d + 4 : -1], refs[-1]
    depth = x_ref.shape[0] // count_p
    pieces = len(outs) // (count_p - 1) if outs else 0
    sums = [0.0, 0.0]
    for c in reversed(range(count_p)):
        rows = slice(c * depth, (c + 1) * depth)
        d_in = 0.0
        for half, w_ref in enumerate(ws):
            parts = d_refs[half * count_d // 2 : (half + 1) * count_d // 2]
            left = jnp.concatenate([ref[rows, :] for ref in parts], axis=1)
            d_in = d_in + dot(left, w_ref[...], NT)
        norm = x_ref[rows, :].astype(F32)
        sums[0] = sums[0] + jnp.sum(d_in, axis=0, keepdims=True)
        sums[1] = sums[1] + jnp.sum(d_in * norm, axis=0, keepdims=True)
        if c == 0:
            own_ref[...] = d_in.astype(BF)
        for i in range(pieces if c else 0):
            out = outs[(c - 1) * pieces + i]
            out[...] = d_in[i * out.shape[0] : (i + 1) * out.shape[0]].astype(BF)
    for i in range(2):
        sums_ref[i : i + 1, :] = sums[i]


def hidden_back_kernel(pieces, *refs):
    recv, (own_d_ref, x_ref, d_mid_ref, mod_ref, *out_refs) = refs[:-6], refs[-6:]
    scale, depth = 1.0 + mod_ref[1:2, :], out_refs[0].shape[0]
    step = recv[0].shape[0] if recv else depth
    for row in range(0, x_ref.shape[0], step):
        rows = slice(row, row + step)
        d_in = own_d_ref[rows, :].astype(F32)
        for i in range(0, len(recv), pieces):
            d_in = d_in + recv[i + row // step][...].astype(F32)
        norm, spread = normed(x_ref[rows, :].astype(F32))
        value = d_mid_ref[rows, :].astype(F32) + norm_back(d_in * scale, norm, spread)
        out_refs[row // depth][row % depth : row % depth + step, :] = value.astype(BF)


def local(
    hidden_in,
    time_embed,
    seg_lengths,
    ada_weight,
    query_weight,
    key_weight,
    value_weight,
    out_weight,
    up_weight,
    down_weight,
    out_cotangent,
):
    count_a, count_b, count_p = (lax.axis_size(name) for name in ("a", "b", "p"))
    at_a, at_b, at_r, at_p = (lax.axis_index(name) for name in ("a", "b", "r", "p"))
    width = hidden_in.shape[2]
    block = hidden_in.shape[1]
    mine = 2 * block
    frames = mine * count_p
    heads_wide = query_weight.shape[1]
    ffn = up_weight.shape[1] * 2 * count_p
    others = range(1, count_p)

    qkv_shard = pack([query_weight, key_weight, value_weight], vmem=60)
    qkv_z = along_line(qkv_shard)
    every = ("a", "b", "r", "p")
    time_vecs = time_embed.astype(F32)
    time_low = jax.nn.silu(time_vecs).astype(BF)
    low_mine = lax.all_to_all(time_low, ("a", "b"), split_axis=1, concat_axis=0, tiled=True)
    low_mine = jnp.repeat(low_mine, count_p, axis=0)
    ada_rows, ada_cols = ada_weight.shape
    devices, blocks = low_mine.shape[0], 2 * count_p
    part = call(
        modulation_part_kernel,
        "modulation_part",
        [sds((devices, ada_cols // PAIR, PAIR), F32)],
        [low_mine, ada_weight],
        vmem=8,
    )[0]
    (hidden_own, hidden_other), (cot_own, cot_other) = exchange_rows(
        [hidden_in, out_cotangent], [qkv_shard]
    )
    qkv_line = stage("stage1", [[qkv_shard, *qkv_z]], [hidden_other, cot_other, part])[0]

    uo_shard = pack([up_weight, out_weight], [qkv_line])
    qkv_r, qkv_b = sideways(qkv_line)
    uo_z = along_line(uo_shard)
    hidden, cotangent = stage(
        "join", [[hidden_own, hidden_other], [cot_own, cot_other]], [uo_shard]
    )
    hidden, cotangent = hidden.reshape(mine, width), cotangent.reshape(mine, width)
    hidden_parts = [hidden] + [swap(hidden, "p", dp) for dp in others]
    part = lax.all_to_all(part, every, split_axis=0, concat_axis=0, tiled=True)
    modulation = call(
        functools.partial(modulation_sum_kernel, blocks),
        "modulation",
        [sds((6, width), F32)],
        [part],
        vmem=8,
    )[0]

    lengths = lax.dynamic_index_in_dim(seg_lengths, at_r, keepdims=False)
    frame_ids = jnp.concatenate(
        [
            ((at_r ^ dr) * count_p + (at_p ^ dp)) * block + jnp.arange(block, dtype=jnp.int32)
            for dp in range(count_p)
            for dr in range(2)
        ]
    )
    passed = frame_ids[:, None] >= jnp.cumsum(lengths)[None, :]
    seg_ids = jnp.sum(passed.astype(jnp.int32), axis=1)
    positions = frame_ids - jnp.sum(jnp.where(passed, lengths[None, :], 0), axis=1)
    half_dim = HEAD_DIM // 2
    lane = jnp.arange(PAIR, dtype=jnp.int32)
    inverse = 10000.0 ** (-(lane % half_dim).astype(F32) / half_dim)
    angles = positions.astype(F32)[:, None] * inverse[None, :]
    cosine = jnp.cos(angles)
    sine = jnp.where(lane % HEAD_DIM < half_dim, -1.0, 1.0)[None, :] * jnp.sin(angles)
    segs = seg_lengths.shape[1]
    same = seg_ids[:, None] == lane[None, :]
    real = (lane < segs)[None, :]
    extra_q = jnp.where(real & ~same, -1e30, 0.0).astype(BF)
    extra_k = jnp.where((real & same) | ((lane >= 8) & (lane < 11))[None, :], 1.0, 0.0).astype(BF)

    heads = sds((frames, heads_wide), BF)
    whole = sds((mine, width), BF)

    def project(x, weights, after):
        return call(qkv_kernel, "qkv", [heads] * 3, [x, weights, cosine, sine], after=after)

    def attend(three, after):
        pair_block = pl.BlockSpec((frames, PAIR), lambda i: (0, i))
        pair_rows = pl.BlockSpec((mine, PAIR), lambda i: (0, i))
        pair_fixed = pl.BlockSpec((frames, PAIR), lambda i: (0, 0))
        return pl.pallas_call(
            lambda *refs: attend_kernel(min(256, mine), *refs[:5], *refs[5 + len(after) :]),
            name="attend",
            grid=(heads_wide // PAIR,),
            in_specs=[pair_block] * 3 + [pair_fixed] * 2 + [ANY] * len(after),
            out_specs=[pair_rows] * count_p + [pair_block],
            out_shape=[sds((mine, heads_wide), BF)] * count_p + [sds((frames, heads_wide), F32)],
            compiler_params=pltpu.CompilerParams(vmem_limit_bytes=9 * MIB),
            cost_estimate=pl.CostEstimate(flops=1, bytes_accessed=1, transcendentals=0),
        )(*three, extra_q, extra_k, *after)

    *qkv_halves, uo_shard2 = stage(
        "stage2", halves_of(qkv_r, qkv_b) + [uo_shard], [*qkv_b, *uo_z[:-1]]
    )
    uo_z = uo_z[:-1] + [swap(uo_shard2, "a", count_a - 1)]
    qkv_ends = corners(qkv_halves)
    attn_input, hidden_norm = call(
        attn_input_kernel,
        "attn_input",
        [sds((frames, width), BF)] * 2,
        [*hidden_parts, modulation],
        after=[qkv_halves[0]],
    )
    qkv_w = [assemble(left_blocks(qkv_line, qkv_b), "assemble_qkv", [attn_input], False)]
    qkv = [project(attn_input, qkv_w[0], ())]
    qkv_w.append(assemble(right_blocks(qkv_r, qkv_ends), "assemble_qkv", [qkv[0][0]], False))

    uo_line = stage("stage3", [[uo_shard, *uo_z]], [qkv_w[1]])[0]
    down_shard = pack([down_weight], [uo_line])
    uo_r, uo_b = sideways(uo_line)
    down_z = along_line(down_shard)
    attended = [attend(qkv[0], [down_shard])]
    qkv.append(project(attn_input, qkv_w[1], [attended[0][0]]))
    attended.append(attend(qkv[1], ()))

    *uo_halves, down_line = stage(
        "stage4", halves_of(uo_r, uo_b) + [[down_shard, *down_z]], [attended[1][0], *uo_b]
    )
    uo_ends = corners(uo_halves)

    uo_pieces = left_blocks(uo_line, uo_b) + right_blocks(uo_r, uo_ends)
    uo_w = [assemble(uo_pieces, "assemble_uo", [down_line])]
    uo_w += [swap(uo_w[0], "p", dp) for dp in others]
    down_line = stage("stage5", [down_line], [uo_w[0]])[0]
    down_r, down_b = sideways(down_line)
    att = [attended[dr][0] for dr in range(2)]
    for dp in others:
        att += [swap(attended[dr][dp], "p", dp) for dr in range(2)]
    ffn_block = ffn // (2 * count_p)
    branch_attn, mid, ffn_input, att_all = call(
        functools.partial(out_kernel, count_p, ffn_block),
        "attn_out",
        [whole, sds((mine, width), F32), whole, whole],
        [hidden, modulation, *att, *uo_w],
        scratch=[pltpu.VMEM((mine, width), F32)],
        after=[down_line],
    )
    gelu_low, slope, d_branch_ffn = call(
        functools.partial(up_kernel, count_p, ffn_block),
        "ffn_up",
        [sds((mine, ffn), BF)] * 2 + [whole],
        [ffn_input, cotangent, modulation, *uo_w],
    )

    down_halves = stage("stage6", halves_of(down_r, down_b), [gelu_low, *down_b])
    down_ends = corners(down_halves)
    fold = down_weight.shape[0] // up_weight.shape[0]
    down_wide = down_weight.shape[1]
    down_sum = Scatter("down", [(down_wide, fold)], count_a // 2)
    uo_sum = Scatter("uo", [(ffn_block, 1), (heads_wide, 1)], count_a // 2)
    qkv_sum = Scatter("qkv", [(heads_wide, 1)] * 3, count_a // 4)

    def split_grad(name, xs, ys, token, fold=1):
        sent = []
        for dp in others:
            token = weight_grad(name, xs, ys, dp, [token], fold)
            sent.append(swap(token, "p", dp))
        own = weight_grad(name, xs, ys, 0, [token], fold)
        return [own, *sent]

    down_parts = split_grad("down_grad", [gelu_low], [d_branch_ffn], down_halves[0], fold)
    down_sum.add([down_parts], (0, 1))

    down_pieces = left_blocks(down_line, down_b) + right_blocks(down_r, down_ends)
    down_w = [assemble(down_pieces, "assemble_down", [down_parts[0]])]
    down_w += [swap(down_w[0], "p", dp) for dp in others]
    token = down_sum.corner([down_w[0]])
    d_up = call(
        functools.partial(d_up_kernel, count_p),
        "d_up",
        [sds((mine, ffn), BF)],
        [d_branch_ffn, slope, *down_w],
        after=[token],
    )[0]
    token = down_sum.side_b([down_sum.side_r([d_up])])
    up_sums = split_grad("up_grad", [ffn_input], [d_up], token)
    token = up_sums[0]
    d_mid, d_branch_attn, sums_mid, *d_att = call(
        functools.partial(mid_back_kernel, count_p, ffn_block),
        "mid_back",
        [whole, whole, sds((3, width), F32)]
        + [sds((mine, heads_wide), BF)] * (2 * count_p),
        [d_up, mid, cotangent, branch_attn, modulation, *uo_w],
        scratch=[pltpu.VMEM((mine, width), F32)],
        after=[token],
    )
    *out_parts, d_ffn_gate = call(
        functools.partial(down_kernel, count_p),
        "ffn_down",
        [sds((block, width), BF)] * 2 + [sds((1, width), F32)],
        [gelu_low, mid, cotangent, modulation, *down_w],
        scratch=[pltpu.VMEM((mine, width), F32)],
        after=[d_branch_attn],
    )
    token = down_sum.line([out_parts[0]])
    out_sums = split_grad("out_grad", [att_all], [d_branch_attn], token)
    uo_sum.add([up_sums, out_sums], (0, 1))

    pairs = heads_wide // PAIR
    d_heads = [
        [d_att[dr]] + [swap(d_att[2 * dp + dr], "p", dp) for dp in others] for dr in range(2)
    ]

    def attend_back(dr, pair, after):
        return call(
            functools.partial(attend_back_kernel, min(512, frames), count_p, pair * PAIR),
            "attend_back",
            [sds((frames, PAIR), BF)] * 3,
            [
                *qkv[dr],
                extra_q,
                extra_k,
                attended[dr][-1],
                cosine,
                sine,
                *attended[dr][:-1],
                *d_heads[dr],
            ],
            after=after,
        )

    def qkv_parts(dr, after):
        return [[weight_grad("qkv_grad", [attn_input], d_qkv[dr], None, after)]]

    d_pairs = [[None] * pairs, [None] * pairs]
    d_qkv = [None, None]

    token = uo_sum.corner(d_heads[1][1:])
    d_pairs[1][0] = attend_back(1, 0, [token])
    token = down_sum.line_next([d_pairs[1][0][0]])
    token = uo_sum.side_b([uo_sum.side_r([token])])
    for pair in range(1, pairs):
        d_pairs[1][pair] = attend_back(1, pair, [token])
        token = d_pairs[1][pair][0]
    d_qkv[1] = [d_pairs[1][pair][t] for t in range(3) for pair in range(pairs)]
    qkv_sum.add(qkv_parts(1, [token]), (1,))
    down_grad = down_sum.final([qkv_sum.parts[(0, 1)][0][0][0], *d_heads[0][1:]])[0]
    token = uo_sum.line([down_grad])
    token = qkv_sum.corner([token])
    d_pairs[0][0] = attend_back(0, 0, [token])
    token = uo_sum.line_next([d_pairs[0][0][0]])
    for pair in range(1, pairs):
        d_pairs[0][pair] = attend_back(0, pair, [token])
        token = d_pairs[0][pair][0]
    d_qkv[0] = [d_pairs[0][pair][t] for t in range(3) for pair in range(pairs)]
    qkv_sum.add(qkv_parts(0, [token]), (0,))
    token = qkv_sum.side_b([qkv_sum.side_r([qkv_sum.parts[(0, 0)][0][0][0]])])

    every_d = [*d_qkv[0], *d_qkv[1]]
    pieces = 4
    piece = sds((mine // pieces, width), BF)
    d_own, *d_sent, sums_in = call(
        functools.partial(d_attn_kernel, count_p, len(every_d)),
        "d_attn",
        [whole] + [piece] * (pieces * (count_p - 1)) + [sds((2, width), F32)],
        [*every_d, *qkv_w, hidden_norm],
        after=[token],
    )
    received = [swap(x, "p", 1 + i // pieces) for i, x in enumerate(d_sent)]
    d_mod = call(
        functools.partial(d_modulation_kernel, blocks),
        "d_modulation",
        [sds((devices, ada_cols // PAIR, PAIR), F32)],
        [sums_in, sums_mid, d_ffn_gate],
        vmem=8,
    )[0]
    d_rows = lax.all_to_all(d_mod, every, split_axis=0, concat_axis=0, tiled=True)
    grad_parts = call(
        functools.partial(hidden_back_kernel, pieces),
        "hidden_back",
        [sds((block, width), BF)] * 2,
        [*received, d_own, hidden, d_mid, modulation],
        after=[d_mod],
    )

    d_rows = stage("modulation_rows", [d_rows], [grad_parts[0]])[0]
    token = qkv_sum.line([d_rows])
    ada_grad, d_low = call(
        functools.partial(ada_back_kernel, blocks),
        "ada_back",
        [sds(ada_weight.shape, F32), sds((devices, blocks, ada_rows), F32)],
        [low_mine, d_rows, ada_weight],
        vmem=16,
        after=[token],
    )
    token = qkv_sum.line_next([d_low])
    up_grad, out_grad = uo_sum.final([token])
    hidden_out = restore_rows(*out_parts, [up_grad])
    d_low = lax.all_to_all(d_low, every, split_axis=0, concat_axis=0, tiled=True)
    hidden_grad = restore_rows(*grad_parts, [hidden_out])
    query_grad, key_grad, value_grad = qkv_sum.final([hidden_grad])

    time_grad = call(
        functools.partial(time_grad_kernel, blocks, count_p),
        "time_grad",
        [sds((2, width), F32)],
        [d_low, time_embed],
        vmem=8,
        after=[query_grad],
    )[0]
    return (
        hidden_out,
        hidden_grad,
        time_grad,
        ada_grad,
        query_grad,
        key_grad,
        value_grad,
        out_grad,
        up_grad,
        down_grad,
    )


def solution(mesh):
    count_dp, count_sp = mesh.shape["dp"], mesh.shape["sp"]
    fine = Mesh(mesh.devices.reshape(4, count_dp // 4, 2, count_sp // 2), ("a", "b", "r", "p"))
    dp, sp = ("a", "b"), ("r", "p")
    in_specs = (
        (P(dp, sp, None), P(dp, None), P(dp, None)) + (P(dp, sp),) * 7 + (P(dp, sp, None),)
    )
    out_specs = (P(dp, sp, None), P(dp, sp, None), P(dp, None)) + (P(dp, sp),) * 7
    return jax.shard_map(local, mesh=fine, in_specs=in_specs, out_specs=out_specs, check_vma=False)
```

```python
import functools

import jax
import jax.numpy as jnp
from jax import lax
from jax.experimental import pallas as pl
from jax.experimental.pallas import tpu as pltpu
from jax.sharding import Mesh
from jax.sharding import PartitionSpec as P

HEAD_DIM = 64
PAIR = 2 * HEAD_DIM
LOG2E = 1.4426950408889634
LN2 = 0.6931471805599453
HIGH = lax.Precision.HIGHEST
F32 = jnp.float32
BF = jnp.bfloat16
NN = (((1,), (0,)), ((), ()))
NT = (((1,), (1,)), ((), ()))
TN = (((0,), (0,)), ((), ()))
ANY = pl.BlockSpec(memory_space=pl.ANY)
HBM = pl.BlockSpec(memory_space=pltpu.HBM)
VM = pl.BlockSpec(memory_space=pltpu.VMEM)
MIB = 1 << 20
TILE = 128


def dot(left, right, dims=NN):
    return lax.dot_general(left, right, dims, preferred_element_type=F32)


def sds(shape, dtype):
    return jax.ShapeDtypeStruct(shape, dtype)


def call(kernel, name, outs, args, scratch=(), vmem=9, after=(), spec=VM, to=VM):
    taken = len(args)

    def body(*refs):
        kernel(*refs[:taken], *refs[taken + len(after) :])

    return pl.pallas_call(
        body,
        name=name,
        in_specs=[spec] * taken + [ANY] * len(after),
        out_specs=[to] * len(outs),
        out_shape=outs,
        scratch_shapes=scratch,
        compiler_params=pltpu.CompilerParams(vmem_limit_bytes=vmem * MIB),
        cost_estimate=pl.CostEstimate(flops=1, bytes_accessed=1, transcendentals=0),
    )(*args, *after)


def swap(value, axis, offset=1):
    count = lax.axis_size(axis)
    return lax.ppermute(value, axis, [(i, i ^ offset) for i in range(count)])


def stage_kernel(plan, *refs):
    count = sum(len(pieces) for pieces in plan)
    ins, outs = iter(refs[:count]), refs[count:]
    for pieces, out in zip(plan, outs):
        at = 0
        for start, size in pieces:
            ref = next(ins)
            if start is not None:
                out[at : at + size] = ref[start : start + size]
            elif len(ref.shape) < len(out.shape):
                out[at] = ref[...]
            else:
                out[...] = ref[...]
            at += size


def stage(name, groups, after=()):
    arrays, plan, outs = [], [], []
    for group in groups:
        if not isinstance(group, list):
            arrays.append(group)
            plan.append(((None, 1),))
            outs.append(sds(group.shape, group.dtype))
            continue
        pieces, total = [], 0
        for piece in group:
            array, start, size = piece if isinstance(piece, tuple) else (piece, None, 1)
            arrays.append(array)
            pieces.append((start, size))
            total += size
        tail = array.shape if start is None else array.shape[1:]
        plan.append(tuple(pieces))
        outs.append(sds((total,) + tail, array.dtype))
    return call(
        functools.partial(stage_kernel, tuple(plan)),
        name,
        outs,
        arrays,
        vmem=12,
        after=after,
    )


def pick_kernel(*refs):
    count = (len(refs) - 1) // 3
    ins, outs, sems = refs[:count], refs[count:-1], refs[-1]
    at_r = lax.axis_index("r")
    copies = []
    for i, ref in enumerate(ins):
        for j, row in enumerate((at_r, 1 - at_r)):
            at = 2 * i + j
            copies.append(pltpu.make_async_copy(ref.at[row], outs[at], sems.at[at]))
    for copy in copies:
        copy.start()
    for copy in copies:
        copy.wait()


def exchange_rows(arrays, after=()):
    outs = [sds(x.shape[1:], x.dtype) for x in arrays for _ in range(2)]
    picked = call(
        pick_kernel,
        "pick_rows",
        outs,
        arrays,
        scratch=[pltpu.SemaphoreType.DMA((len(outs),))],
        vmem=60,
        after=after,
        spec=HBM,
    )
    return [(own, swap(other, "r")) for own, other in zip(picked[::2], picked[1::2])]


def place_kernel(own_ref, other_ref, out_ref, sems):
    at_r = lax.axis_index("r")
    copies = [
        pltpu.make_async_copy(own_ref, out_ref.at[at_r], sems.at[0]),
        pltpu.make_async_copy(other_ref, out_ref.at[1 - at_r], sems.at[1]),
    ]
    for copy in copies:
        copy.start()
    for copy in copies:
        copy.wait()


def restore_rows(own, other, after=()):
    outs = [sds((2,) + own.shape, own.dtype)]
    args = [own, swap(other, "r")]
    sems = [pltpu.SemaphoreType.DMA((2,))]
    return call(
        place_kernel, "place_rows", outs, args, scratch=sems, vmem=8, after=after, to=HBM
    )[0]


def pack_kernel(*refs):
    ins, (out, sems) = refs[:-2], refs[-2:]
    at, copies = 0, []
    for i, ref in enumerate(ins):
        place = out.at[:, pl.ds(at, ref.shape[1])]
        copies.append(pltpu.make_async_copy(ref, place, sems.at[i]))
        at += ref.shape[1]
    for copy in copies:
        copy.start()
    for copy in copies:
        copy.wait()


def pack(shards, after=(), vmem=8):
    width = sum(x.shape[1] for x in shards)
    outs = [sds((shards[0].shape[0], width), BF)]
    return call(
        pack_kernel,
        "pack",
        outs,
        shards,
        scratch=[pltpu.SemaphoreType.DMA((len(shards),))],
        vmem=vmem,
        after=after,
        spec=HBM,
    )[0]


def along_line(shard):
    return [swap(shard, "a", d) for d in range(1, lax.axis_size("a"))]


def sideways(first):
    return swap(first, "r"), [swap(first, "b", dy) for dy in range(1, lax.axis_size("b"))]


def halves_of(side_r, sides_b):
    half = side_r.shape[0] // 2
    return [[(side, 0, half)] for side in sides_b] + [[(side_r, half, half)]]


def corners(halves):
    *sides_b, side_r = halves
    return [
        (swap(side_b, "r"), swap(side_r, "b", dy + 1)) for dy, side_b in enumerate(sides_b)
    ]


def span(dy, dr, start, stop):
    return [(dy, dr, dz) for dz in range(start, stop)]


def left_blocks(first, sides_b):
    line = first.shape[0]
    left = [(first, span(0, 0, 0, line))]
    return left + [(side, span(dy + 1, 0, 0, line)) for dy, side in enumerate(sides_b)]


def right_blocks(side_r, ends):
    line = side_r.shape[0]
    right = [(side_r, span(0, 1, 0, line))]
    for dy, (low, high) in enumerate(ends):
        right.append((low, span(dy + 1, 1, 0, line // 2)))
        right.append((high, span(dy + 1, 1, line // 2, line)))
    return right


def totals(refs, members, t):
    wide, refs = [], iter(refs)
    for member in members:
        wide.append(sum(next(refs)[index + (t,)].astype(F32) for _, index in member))
    return wide[0] if len(wide) == 1 else jnp.concatenate(wide, axis=1)


class Scatter:
    def __init__(self, name, cuts, cut):
        self.name, self.cuts, self.cut = name, cuts, cut
        self.line_count = lax.axis_size("a")
        self.count_b = lax.axis_size("b")
        self.parts = {}
        self.first_r = {dy: [] for dy in range(1, self.count_b)}
        self.first_b = {dy: [] for dy in range(1, self.count_b)}

    def add(self, members, rights):
        for dy in range(self.count_b):
            for at, dr in enumerate(rights):
                index = (dy,) if len(rights) == 1 else (dy, at)
                found = self.parts.setdefault((dy, dr), [])
                found += [[(x, index) for x in member] for member in members]

    def step(self, label, body, shapes, members, extra, after):
        arrays = [array for member in members for array, _ in member]
        return call(body, self.name + label, shapes, arrays + extra, after=after)

    def block(self, members):
        return members[0][0][0].shape[-2], sum(member[0][0].shape[-1] for member in members)

    def corner(self, after=(), some=slice(None)):
        cut, line = self.cut, self.line_count
        for dy in range(1, self.count_b):
            members = self.parts[(dy, 1)][some]
            shape = self.block(members)

            def body(*refs, members=members):
                for t in range(line):
                    out, at = (refs[-2], t) if t < cut else (refs[-1], t - cut)
                    out[at] = totals(refs, members, t).astype(BF)

            shapes = [sds((cut,) + shape, BF), sds((line - cut,) + shape, BF)]
            first, second = self.step("_corner", body, shapes, members, [], after)
            self.first_r[dy].append(swap(first, "r"))
            self.first_b[dy].append(swap(second, "b", dy))
        return first

    def side_r(self, after=()):
        members = self.parts[(0, 1)]
        groups = list(self.first_b.values())
        extra = [x for group in groups for x in group]
        cut, line = self.cut, self.line_count

        def body(*refs):
            more, out = refs[-1 - len(extra) : -1], refs[-1]
            for t in range(line):
                total = totals(refs, members, t)
                if t >= cut:
                    total = total + self.added(more, len(groups), t - cut)
                out[t] = total.astype(BF)

        shapes = [sds((line,) + self.block(members), BF)]
        after = [*after, *[x for group in self.first_r.values() for x in group]]
        side = self.step("_side_r", body, shapes, members, extra, after)[0]
        self.from_r = swap(side, "r")
        return side

    def added(self, refs, groups, t):
        each = len(refs) // groups
        total = 0.0
        for at in range(0, len(refs), each):
            pieces = [ref[t].astype(F32) for ref in refs[at : at + each]]
            total = total + (pieces[0] if each == 1 else jnp.concatenate(pieces, axis=1))
        return total

    def side_b(self, after=()):
        self.from_b = []
        cut, line = self.cut, self.line_count
        for dy in range(1, self.count_b):
            members = self.parts[(dy, 0)]
            extra = self.first_r[dy]

            def body(*refs, members=members, extra=extra):
                more, out = refs[-1 - len(extra) : -1], refs[-1]
                for t in range(line):
                    total = totals(refs, members, t)
                    if t < cut:
                        total = total + self.added(more, 1, t)
                    out[t] = total.astype(BF)

            shapes = [sds((line,) + self.block(members), BF)]
            side = self.step("_side_b", body, shapes, members, extra, after)[0]
            self.from_b.append(swap(side, "b", dy))
        return side

    def line(self, after=()):
        members = self.parts[(0, 0)]
        shape, line = self.block(members), self.line_count
        extra = [self.from_r, *self.from_b]
        kept = line // 2

        def body(*refs):
            more, (keep, sent) = refs[-2 - len(extra) : -2], refs[-2:]
            for t in range(line):
                total = totals(refs, members, t) + sum(ref[t].astype(F32) for ref in more)
                if t % 2:
                    sent[t // 2] = total.astype(BF)
                else:
                    keep[t // 2] = total

        shapes = [sds((kept,) + shape, F32), sds((kept,) + shape, BF)]
        self.keep, sent = self.step("_line", body, shapes, members, extra, after)
        self.step_size, self.from_a = 1, swap(sent, "a", 1)
        return sent

    def line_next(self, after=()):
        kept = self.keep.shape[0] // 2
        shape = self.keep.shape[1:]

        def body(keep_ref, recv_ref, keep, sent):
            for t in range(2 * kept):
                total = keep_ref[t] + recv_ref[t].astype(F32)
                if t % 2:
                    sent[t // 2] = total.astype(BF)
                else:
                    keep[t // 2] = total

        shapes = [sds((kept,) + shape, F32), sds((kept,) + shape, BF)]
        self.keep, sent = self.step("_line_next", body, shapes, [], [self.keep, self.from_a], after)
        self.step_size *= 2
        self.from_a = swap(sent, "a", self.step_size)
        return sent

    def final(self, after=()):
        depth = self.keep.shape[1]
        cuts = self.cuts

        def body(keep_ref, recv_ref, *outs):
            total = keep_ref[0] + recv_ref[0].astype(F32)
            at = 0
            for out, (width, fold) in zip(outs, cuts):
                for i in range(fold):
                    out[i * depth : (i + 1) * depth, :] = total[:, at : at + width]
                    at += width

        shapes = [sds((depth * fold, width), F32) for width, fold in cuts]
        return self.step("_final", body, shapes, [], [self.keep, self.from_a], after)


def assemble_kernel(meta, keep_r, count_b, *refs):
    ins, out = refs[: len(meta)], refs[len(meta)]
    at_a, at_b, at_r = (lax.axis_index(name) for name in ("a", "b", "r"))
    for ref, places in zip(ins, meta):
        depth = ref.shape[1]
        for t, (dy, dr, dz) in enumerate(places):
            row = pl.multiple_of(((at_a ^ dz) * count_b + (at_b ^ dy)) * depth, depth)
            if keep_r:
                out[at_r ^ dr, pl.ds(row, depth), :] = ref[t]
            else:
                out[pl.ds(row, depth), :] = ref[t]


def assemble(pieces, name, after=(), keep_r=True):
    count_a, count_b = lax.axis_size("a"), lax.axis_size("b")
    arrays = [piece for piece, _ in pieces]
    meta = [places for _, places in pieces]
    _, depth, width = arrays[0].shape
    shape = (count_a * count_b * depth, width)
    if keep_r:
        shape = (2,) + shape
    return call(
        functools.partial(assemble_kernel, tuple(meta), keep_r, count_b),
        name,
        [sds(shape, BF)],
        arrays,
        vmem=16,
        after=after,
    )[0]


def normed(values):
    centre = values - jnp.mean(values, axis=-1, keepdims=True)
    spread = lax.rsqrt(jnp.mean(centre * centre, axis=-1, keepdims=True) + 1e-06)
    return centre * spread, spread


def norm_back(grad, norm, spread):
    return spread * (
        grad
        - jnp.mean(grad, axis=-1, keepdims=True)
        - norm * jnp.mean(grad * norm, axis=-1, keepdims=True)
    )


def modulation_part_kernel(low_ref, ada_ref, out_ref):
    low = low_ref[...]
    for i in range(out_ref.shape[1]):
        out_ref[:, i, :] = dot(low, ada_ref[:, i * PAIR : (i + 1) * PAIR])


def modulation_sum_kernel(blocks, in_ref, out_ref):
    groups, slabs = in_ref.shape[0] // blocks, in_ref.shape[1]
    wide = out_ref.shape[1] // PAIR
    for block in range(blocks):
        total = in_ref[block]
        for group in range(1, groups):
            total = total + in_ref[group * blocks + block]
        for i in range(slabs):
            m, c = divmod(block * slabs + i, wide)
            out_ref[m : m + 1, c * PAIR : (c + 1) * PAIR] = total[i : i + 1]


def d_modulation_kernel(blocks, in_ref, mid_ref, gate_ref, out_ref):
    groups, slabs = out_ref.shape[0] // blocks, out_ref.shape[1]
    rows = [in_ref[m : m + 1] for m in range(2)] + [mid_ref[m : m + 1] for m in range(3)]
    rows.append(gate_ref[...])
    wide = gate_ref.shape[1] // PAIR
    for block in range(blocks):
        for i in range(slabs):
            m, c = divmod(block * slabs + i, wide)
            value = rows[m][:, c * PAIR : (c + 1) * PAIR]
            for group in range(groups):
                out_ref[group * blocks + block, i : i + 1, :] = value


def ada_back_kernel(copies, low_ref, rows_ref, ada_ref, grad_ref, out_ref):
    kinds = dict(preferred_element_type=F32, precision=HIGH)
    low, d_low = low_ref[...].astype(F32), 0.0
    for i in range(rows_ref.shape[1]):
        lanes = slice(i * PAIR, (i + 1) * PAIR)
        rows = rows_ref[:, i, :]
        grad_ref[:, lanes] = lax.dot_general(low, rows, TN, **kinds)
        d_low = d_low + lax.dot_general(rows, ada_ref[:, lanes].astype(F32), NT, **kinds)
    for i in range(out_ref.shape[0]):
        start = i // copies * copies
        out_ref[i] = d_low[start : start + copies]


def time_grad_kernel(copies, count_p, in_ref, time_ref, out_ref):
    depth = in_ref.shape[2]
    time = time_ref[...].astype(F32)
    sigmoid = 1.0 / (1.0 + jnp.exp(-time))
    slope = sigmoid * (1.0 + time * (1.0 - sigmoid))
    for group in range(in_ref.shape[0] // copies):
        total = in_ref[group * copies]
        for i in range(1, copies):
            total = total + in_ref[group * copies + i]
        lanes = slice(group * depth, (group + 1) * depth)
        for r in range(2):
            row = jnp.sum(total[r * count_p : (r + 1) * count_p], axis=0, keepdims=True)
            out_ref[r : r + 1, lanes] = row * slope[r : r + 1, lanes]


def attn_input_kernel(*refs):
    x_refs, (mod_ref, out_ref, norm_ref) = refs[:-3], refs[-3:]
    scale, shift = 1.0 + mod_ref[1:2, :], mod_ref[0:1, :]
    at = 0
    for ref in x_refs:
        for row in range(0, ref.shape[0], TILE):
            norm, _ = normed(ref[row : row + TILE, :].astype(F32))
            rows = slice(at + row, at + row + TILE)
            norm_ref[rows, :] = norm.astype(BF)
            out_ref[rows, :] = (norm * scale + shift).astype(BF)
        at += ref.shape[0]


def lane_ids(width=PAIR):
    return lax.broadcasted_iota(jnp.int32, (1, width), 1)


def turn(values, cosine, sine):
    early = lane_ids() % HEAD_DIM < HEAD_DIM // 2
    step = HEAD_DIM // 2
    other = jnp.where(early, pltpu.roll(values, PAIR - step, 1), pltpu.roll(values, step, 1))
    return values * cosine + other * sine


def qkv_kernel(x_ref, w_ref, cos_ref, sin_ref, q_ref, k_ref, v_ref):
    width = q_ref.shape[1]
    weights = w_ref[...]
    step = min(512, x_ref.shape[0])
    for row in range(0, x_ref.shape[0], step):
        rows = slice(row, row + step)
        both = dot(x_ref[rows, :], weights)
        cosine, sine = cos_ref[rows, :], sin_ref[rows, :]
        for lane in range(0, width, PAIR):
            lanes, at = slice(lane, lane + PAIR), width + lane
            query = turn(both[:, lanes], cosine, sine) * (HEAD_DIM**-0.5 * LOG2E)
            q_ref[rows, lanes] = query.astype(BF)
            k_ref[rows, lanes] = turn(both[:, at : at + PAIR], cosine, sine).astype(BF)
        v_ref[rows, :] = both[:, 2 * width :].astype(BF)


def attend_kernel(block, q_ref, k_ref, v_ref, aq_ref, ak_ref, *refs):
    o_refs, lse_ref = refs[:-1], refs[-1]
    depth = o_refs[0].shape[0]
    frames = q_ref.shape[0]
    keys = jnp.concatenate([k_ref[...], ak_ref[...]], axis=1)
    values = v_ref[...]
    low = lane_ids() < HEAD_DIM
    zero, one = jnp.zeros((), BF), jnp.ones((), BF)

    def attend(with_max):
        for start in range(0, frames, block):
            rows = pl.ds(start, block)
            query, extra = q_ref[rows, :], aq_ref[rows, :]
            outs, logs = [], []
            for head in range(2):
                mine = low if head == 0 else jnp.logical_not(low)
                left = jnp.concatenate([jnp.where(mine, query, zero), extra], axis=1)
                scores = dot(left, keys, NT)
                if with_max:
                    top = jnp.max(scores, axis=1, keepdims=True)
                    scores = scores - top
                weights = jnp.exp2(scores).astype(BF)
                mixed = dot(weights, jnp.where(mine, values, one))
                outs.append(mixed / pltpu.roll(mixed, HEAD_DIM, 1))
                log = jnp.log2(jnp.maximum(mixed, 1e-30))
                logs.append(log + top if with_max else log)
            both = jnp.where(low, outs[0], outs[1]).astype(BF)
            o_refs[start // depth][pl.ds(start % depth, block), :] = both
            lse_ref[rows, :] = jnp.where(low, logs[1], logs[0])

    query_all, key_all = q_ref[...].astype(F32), k_ref[...].astype(F32)
    bound = jnp.max(jnp.sum(query_all * query_all, axis=1)) * jnp.max(
        jnp.sum(key_all * key_all, axis=1)
    )
    small = bound < 3600.0

    @pl.when(small)
    def _():
        attend(False)

    @pl.when(jnp.logical_not(small))
    def _():
        attend(True)


def split3(values):
    first = values.astype(BF)
    rest = values - first.astype(F32)
    second = rest.astype(BF)
    return first, second, (rest - second.astype(F32)).astype(BF)


def placed(parts, start, base):
    lanes = lane_ids()
    for i, part in enumerate(parts):
        base = jnp.where(lanes == start + i, part, base)
    return base


def attend_back_kernel(block, parts, lanes_at, q_ref, k_ref, v_ref, aq_ref, ak_ref, lse_ref, cos_ref, sin_ref, *refs):
    o_refs, do_refs, (dq_ref, dk_ref, dv_ref) = refs[:parts], refs[parts : 2 * parts], refs[2 * parts :]
    frames = q_ref.shape[0]
    at = slice(lanes_at, lanes_at + PAIR)
    lanes = lane_ids()
    low = lanes < HEAD_DIM
    zero = jnp.zeros((), BF)
    query, extra, lse = q_ref[:, at], aq_ref[...], lse_ref[:, at]
    grad = jnp.concatenate([ref[:, at] for ref in do_refs], axis=0)
    out = jnp.concatenate([ref[:, at] for ref in o_refs], axis=0)
    product = grad.astype(F32) * out.astype(F32)
    queries, grads, lefts, rights = [], [], [], []
    for head in range(2):
        mine = low if head == 0 else jnp.logical_not(low)
        log = lse[:, HEAD_DIM : HEAD_DIM + 1] if head == 0 else lse[:, 0:1]
        queries.append(jnp.where(mine, query, zero))
        lefts.append(jnp.concatenate([queries[-1], placed(split3(-log), 8, extra)], axis=1))
        inner = -jnp.sum(jnp.where(mine, product, 0.0), axis=1, keepdims=True)
        grads.append(jnp.where(mine, grad, zero))
        tail = placed(split3(inner), 0, jnp.zeros((frames, PAIR), BF))
        rights.append(jnp.concatenate([grads[-1], tail], axis=1))
    ones = jnp.where(lanes < 3, 1.0, 0.0).astype(BF)
    dq_turned = jnp.zeros((PAIR, frames), F32)
    for start in range(0, frames, block):
        rows = pl.ds(start, block)
        key, value = k_ref[rows, at], v_ref[rows, at]
        keys = jnp.concatenate([key, ak_ref[rows, :]], axis=1)
        values = jnp.concatenate([value, jnp.broadcast_to(ones, value.shape)], axis=1)
        dv, dk = 0.0, 0.0
        for head in range(2):
            mine = low if head == 0 else jnp.logical_not(low)
            soft = jnp.exp2(dot(keys, lefts[head], NT))
            d_scores = (soft * dot(values, rights[head], NT)).astype(BF)
            dv = dv + dot(soft.astype(BF), grads[head])
            dk = dk + dot(d_scores, queries[head])
            dq_turned = dq_turned + dot(jnp.where(mine, key, zero), d_scores, TN)
        dv_ref[rows, :] = dv.astype(BF)
        dk_ref[rows, :] = turn(dk * LN2, cos_ref[rows, :], -sin_ref[rows, :]).astype(BF)
    dq = dq_turned.T * HEAD_DIM**-0.5
    dq_ref[...] = turn(dq, cos_ref[...], -sin_ref[...]).astype(BF)


def column(dr, dp):
    at_r, at_p = lax.axis_index("r"), lax.axis_index("p")
    return (at_r ^ dr) * lax.axis_size("p") + (at_p ^ dp)


def lanes_of(index, width):
    return pl.ds(pl.multiple_of(index * width, width), width)


def column_blocks(weight_refs):
    count_r = lax.axis_size("r")
    count_p = lax.axis_size("p")
    at_p = lax.axis_index("p")
    for dp, ref in enumerate(weight_refs):
        for r in range(count_r):
            yield r * count_p + (at_p ^ dp), ref, r


def out_kernel(count_p, at_lane, x_ref, mod_ref, *refs):
    att_refs = refs[: 2 * count_p]
    w_refs = refs[2 * count_p : 3 * count_p]
    branch_ref, mid_ref, ffn_ref, att_ref, sum_ref = refs[3 * count_p :]
    width = att_refs[0].shape[1]
    for dp in range(count_p):
        for dr in range(2):
            att_ref[:, lanes_of(column(dr, dp), width)] = att_refs[2 * dp + dr][...]
    att = att_ref[...]
    for j, ref, r in column_blocks(w_refs):
        sum_ref[:, lanes_of(j, width)] = dot(att, ref[r, :, at_lane : at_lane + width])
    gate, scale, shift = mod_ref[2:3, :], 1.0 + mod_ref[4:5, :], mod_ref[3:4, :]
    for row in range(0, x_ref.shape[0], TILE):
        rows = slice(row, row + TILE)
        branch = sum_ref[rows, :]
        branch_ref[rows, :] = branch.astype(BF)
        mid = x_ref[rows, :].astype(F32) + gate * branch
        mid_ref[rows, :] = mid
        norm, _ = normed(mid)
        ffn_ref[rows, :] = (norm * scale + shift).astype(BF)


def up_kernel(count_p, wide, x_ref, cot_ref, mod_ref, *refs):
    w_refs, (gelu_ref, slope_ref, dbf_ref) = refs[:count_p], refs[count_p:]
    dbf_ref[...] = (cot_ref[...].astype(F32) * mod_ref[5:6, :]).astype(BF)
    x = x_ref[...]
    root = 0.7978845608028654
    for j, ref, r in column_blocks(w_refs):
        up = dot(x, ref[r, :, :wide])
        square = up * up
        tanh = jnp.tanh(up * (root + (root * 0.044715) * square))
        half = 0.5 + 0.5 * tanh
        at = lanes_of(j, wide)
        gelu_ref[:, at] = (up * half).astype(BF)
        slope = half + up * (1.0 - tanh * tanh) * (0.5 * root + (0.5 * root * 0.134145) * square)
        slope_ref[:, at] = slope.astype(BF)


def down_kernel(count_p, gelu_ref, mid_ref, cot_ref, mod_ref, *refs):
    w_refs = refs[:count_p]
    out_refs, (dgate_ref, sum_ref) = refs[count_p:-2], refs[-2:]
    gelu = gelu_ref[...]
    for j, ref, r in column_blocks(w_refs):
        sum_ref[:, lanes_of(j, ref.shape[2])] = dot(gelu, ref[r])
    gate, total, depth = mod_ref[5:6, :], 0.0, out_refs[0].shape[0]
    for row in range(0, mid_ref.shape[0], TILE):
        rows = slice(row, row + TILE)
        branch = sum_ref[rows, :]
        place = out_refs[row // depth]
        place[row % depth : row % depth + TILE, :] = (mid_ref[rows, :] + gate * branch).astype(BF)
        total = total + jnp.sum(cot_ref[rows, :].astype(F32) * branch, axis=0, keepdims=True)
    dgate_ref[...] = total


def turned_dot(x_ref, w_refs, start=0, width=None):
    total = 0.0
    for j, ref, r in column_blocks(w_refs):
        wide = width or ref.shape[2]
        total = total + dot(x_ref[:, lanes_of(j, wide)], ref[r, :, start : start + wide], NT)
    return total


def d_up_kernel(count_p, dbf_ref, slope_ref, *refs):
    w_refs, (out_ref,) = refs[:count_p], refs[count_p:]
    out_ref[...] = (turned_dot(dbf_ref, w_refs) * slope_ref[...].astype(F32)).astype(BF)


def mid_back_kernel(count_p, wide, d_up_ref, mid_ref, cot_ref, branch_ref, mod_ref, *refs):
    w_refs = refs[:count_p]
    d_mid_ref, dba_ref, sums_ref = refs[count_p : count_p + 3]
    att_refs, all_ref = refs[count_p + 3 : -1], refs[-1]
    all_ref[...] = turned_dot(d_up_ref, w_refs, 0, wide)
    scale, gate = 1.0 + mod_ref[4:5, :], mod_ref[2:3, :]
    sums = [0.0, 0.0, 0.0]
    for row in range(0, mid_ref.shape[0], TILE):
        rows = slice(row, row + TILE)
        d_in = all_ref[rows, :]
        norm, spread = normed(mid_ref[rows, :])
        d_mid = cot_ref[rows, :].astype(F32) + norm_back(d_in * scale, norm, spread)
        d_mid_ref[rows, :] = d_mid.astype(BF)
        dba_ref[rows, :] = (d_mid * gate).astype(BF)
        parts = (d_mid * branch_ref[rows, :].astype(F32), d_in, d_in * norm)
        sums = [s + jnp.sum(part, axis=0, keepdims=True) for s, part in zip(sums, parts)]
    for i in range(3):
        sums_ref[i : i + 1, :] = sums[i]
    width = att_refs[0].shape[1]
    all_ref[...] = turned_dot(dba_ref, w_refs, wide, width)
    for dp in range(count_p):
        for dr in range(2):
            att_refs[2 * dp + dr][...] = all_ref[:, lanes_of(column(dr, dp), width)].astype(BF)


def weight_grad_kernel(counts, places, sizes, *refs):
    count_x, count_y = counts
    x_refs, y_refs, out_ref = refs[:count_x], refs[count_x:-1], refs[-1]
    count_a, count_b = sizes
    count_p = lax.axis_size("p")
    at_a, at_b = lax.axis_index("a"), lax.axis_index("b")
    depth = x_refs[0].shape[1] // (count_a * count_b)
    fold = depth // out_ref.shape[-2]
    xs = [ref[...] for ref in x_refs]
    for dp, dr in places:
        if dr is None:
            ys = [jnp.concatenate([ref[...] for ref in y_refs], axis=1)]
        else:
            ys = []
            for ref in y_refs:
                ys.append(ref[:, lanes_of(column(dr, dp), ref.shape[1] // (2 * count_p))])
        at = 0
        for x, y in zip(xs, ys):
            grad = dot(x, y, TN).astype(BF)
            part = depth // fold
            for i in range(count_a * count_b * fold):
                block, piece = divmod(i, fold)
                dz, dy = at_a ^ (block // count_b), at_b ^ (block % count_b)
                rows = grad[i * part : (i + 1) * part]
                lanes = slice(at + piece * y.shape[1], at + (piece + 1) * y.shape[1])
                if dr is None:
                    out_ref[dy, dz, :, lanes] = rows
                else:
                    out_ref[dy, dr, dz, :, lanes] = rows
            at += y.shape[1] * fold


def weight_grad(name, xs, ys, dp=None, after=(), fold=1):
    count_a, count_b = lax.axis_size("a"), lax.axis_size("b")
    depth = xs[0].shape[1] // (count_a * count_b)
    width = sum(y.shape[1] for y in ys)
    if dp is not None:
        width //= 2 * lax.axis_size("p")
        places = [(dp, dr) for dr in reversed(range(2))]
        outs = [sds((count_b, 2, count_a, depth // fold, width * fold), BF)]
    else:
        places = [(0, None)]
        outs = [sds((count_b, count_a, depth, width), BF)]
    return call(
        functools.partial(
            weight_grad_kernel, (len(xs), len(ys)), tuple(places), (count_a, count_b)
        ),
        name,
        outs,
        [*xs, *ys],
        after=after,
    )[0]


def d_attn_kernel(count_p, count_d, *refs):
    d_refs, ws = refs[:count_d], refs[count_d : count_d + 2]
    x_ref, own_ref, outs, sums_ref = refs[count_d + 2], refs[count_d + 3], refs[count_d + 4 : -1], refs[-1]
    depth = x_ref.shape[0] // count_p
    pieces = len(outs) // (count_p - 1) if outs else 0
    sums = [0.0, 0.0]
    for c in reversed(range(count_p)):
        rows = slice(c * depth, (c + 1) * depth)
        d_in = 0.0
        for half, w_ref in enumerate(ws):
            parts = d_refs[half * count_d // 2 : (half + 1) * count_d // 2]
            left = jnp.concatenate([ref[rows, :] for ref in parts], axis=1)
            d_in = d_in + dot(left, w_ref[...], NT)
        norm = x_ref[rows, :].astype(F32)
        sums[0] = sums[0] + jnp.sum(d_in, axis=0, keepdims=True)
        sums[1] = sums[1] + jnp.sum(d_in * norm, axis=0, keepdims=True)
        if c == 0:
            own_ref[...] = d_in.astype(BF)
        for i in range(pieces if c else 0):
            out = outs[(c - 1) * pieces + i]
            out[...] = d_in[i * out.shape[0] : (i + 1) * out.shape[0]].astype(BF)
    for i in range(2):
        sums_ref[i : i + 1, :] = sums[i]


def hidden_back_kernel(pieces, *refs):
    recv, (own_d_ref, x_ref, d_mid_ref, mod_ref, *out_refs) = refs[:-6], refs[-6:]
    scale, depth = 1.0 + mod_ref[1:2, :], out_refs[0].shape[0]
    step = recv[0].shape[0] if recv else depth
    for row in range(0, x_ref.shape[0], step):
        rows = slice(row, row + step)
        d_in = own_d_ref[rows, :].astype(F32)
        for i in range(0, len(recv), pieces):
            d_in = d_in + recv[i + row // step][...].astype(F32)
        norm, spread = normed(x_ref[rows, :].astype(F32))
        value = d_mid_ref[rows, :].astype(F32) + norm_back(d_in * scale, norm, spread)
        out_refs[row // depth][row % depth : row % depth + step, :] = value.astype(BF)


def local(
    hidden_in,
    time_embed,
    seg_lengths,
    ada_weight,
    query_weight,
    key_weight,
    value_weight,
    out_weight,
    up_weight,
    down_weight,
    out_cotangent,
):
    count_a, count_b, count_p = (lax.axis_size(name) for name in ("a", "b", "p"))
    at_a, at_b, at_r, at_p = (lax.axis_index(name) for name in ("a", "b", "r", "p"))
    width = hidden_in.shape[2]
    block = hidden_in.shape[1]
    mine = 2 * block
    frames = mine * count_p
    heads_wide = query_weight.shape[1]
    ffn = up_weight.shape[1] * 2 * count_p
    others = range(1, count_p)

    qkv_shard = pack([query_weight, key_weight, value_weight], vmem=60)
    qkv_z = along_line(qkv_shard)
    every = ("a", "b", "r", "p")
    time_vecs = time_embed.astype(F32)
    time_low = jax.nn.silu(time_vecs).astype(BF)
    low_mine = lax.all_to_all(time_low, ("a", "b"), split_axis=1, concat_axis=0, tiled=True)
    low_mine = jnp.repeat(low_mine, count_p, axis=0)
    ada_rows, ada_cols = ada_weight.shape
    devices, blocks = low_mine.shape[0], 2 * count_p
    part = call(
        modulation_part_kernel,
        "modulation_part",
        [sds((devices, ada_cols // PAIR, PAIR), F32)],
        [low_mine, ada_weight],
        vmem=8,
    )[0]
    (hidden_own, hidden_other), (cot_own, cot_other) = exchange_rows(
        [hidden_in, out_cotangent]
    )
    qkv_line = stage("stage1", [[qkv_shard, *qkv_z]], [hidden_other, cot_other, part])[0]

    uo_shard = pack([up_weight, out_weight], [qkv_line])
    qkv_r, qkv_b = sideways(qkv_line)
    uo_z = along_line(uo_shard)
    hidden, cotangent = stage(
        "join", [[hidden_own, hidden_other], [cot_own, cot_other]], [uo_shard]
    )
    hidden, cotangent = hidden.reshape(mine, width), cotangent.reshape(mine, width)
    hidden_parts = [hidden] + [swap(hidden, "p", dp) for dp in others]
    part = lax.all_to_all(part, every, split_axis=0, concat_axis=0, tiled=True)
    modulation = call(
        functools.partial(modulation_sum_kernel, blocks),
        "modulation",
        [sds((6, width), F32)],
        [part],
        vmem=8,
    )[0]

    lengths = lax.dynamic_index_in_dim(seg_lengths, at_r, keepdims=False)
    frame_ids = jnp.concatenate(
        [
            ((at_r ^ dr) * count_p + (at_p ^ dp)) * block + jnp.arange(block, dtype=jnp.int32)
            for dp in range(count_p)
            for dr in range(2)
        ]
    )
    passed = frame_ids[:, None] >= jnp.cumsum(lengths)[None, :]
    seg_ids = jnp.sum(passed.astype(jnp.int32), axis=1)
    positions = frame_ids - jnp.sum(jnp.where(passed, lengths[None, :], 0), axis=1)
    half_dim = HEAD_DIM // 2
    lane = jnp.arange(PAIR, dtype=jnp.int32)
    inverse = 10000.0 ** (-(lane % half_dim).astype(F32) / half_dim)
    angles = positions.astype(F32)[:, None] * inverse[None, :]
    cosine = jnp.cos(angles)
    sine = jnp.where(lane % HEAD_DIM < half_dim, -1.0, 1.0)[None, :] * jnp.sin(angles)
    segs = seg_lengths.shape[1]
    same = seg_ids[:, None] == lane[None, :]
    real = (lane < segs)[None, :]
    extra_q = jnp.where(real & ~same, -1e30, 0.0).astype(BF)
    extra_k = jnp.where((real & same) | ((lane >= 8) & (lane < 11))[None, :], 1.0, 0.0).astype(BF)

    heads = sds((frames, heads_wide), BF)
    whole = sds((mine, width), BF)

    def project(x, weights, after):
        return call(qkv_kernel, "qkv", [heads] * 3, [x, weights, cosine, sine], after=after)

    def attend(three, after):
        pair_block = pl.BlockSpec((frames, PAIR), lambda i: (0, i))
        pair_rows = pl.BlockSpec((mine, PAIR), lambda i: (0, i))
        pair_fixed = pl.BlockSpec((frames, PAIR), lambda i: (0, 0))
        return pl.pallas_call(
            lambda *refs: attend_kernel(min(256, mine), *refs[:5], *refs[5 + len(after) :]),
            name="attend",
            grid=(heads_wide // PAIR,),
            in_specs=[pair_block] * 3 + [pair_fixed] * 2 + [ANY] * len(after),
            out_specs=[pair_rows] * count_p + [pair_block],
            out_shape=[sds((mine, heads_wide), BF)] * count_p + [sds((frames, heads_wide), F32)],
            compiler_params=pltpu.CompilerParams(vmem_limit_bytes=9 * MIB),
            cost_estimate=pl.CostEstimate(flops=1, bytes_accessed=1, transcendentals=0),
        )(*three, extra_q, extra_k, *after)

    *qkv_halves, uo_shard2 = stage(
        "stage2", halves_of(qkv_r, qkv_b) + [uo_shard], [*qkv_b, *uo_z[:-1]]
    )
    uo_z = uo_z[:-1] + [swap(uo_shard2, "a", count_a - 1)]
    qkv_ends = corners(qkv_halves)
    attn_input, hidden_norm = call(
        attn_input_kernel,
        "attn_input",
        [sds((frames, width), BF)] * 2,
        [*hidden_parts, modulation],
        after=[qkv_halves[0]],
    )
    qkv_w = [assemble(left_blocks(qkv_line, qkv_b), "assemble_qkv", [attn_input], False)]
    qkv = [project(attn_input, qkv_w[0], ())]
    qkv_w.append(assemble(right_blocks(qkv_r, qkv_ends), "assemble_qkv", [qkv[0][0]], False))

    uo_line = stage("stage3", [[uo_shard, *uo_z]], [qkv_w[1]])[0]
    down_shard = pack([down_weight], [uo_line])
    uo_r, uo_b = sideways(uo_line)
    down_z = along_line(down_shard)
    attended = [attend(qkv[0], [down_shard])]
    qkv.append(project(attn_input, qkv_w[1], [attended[0][0]]))
    attended.append(attend(qkv[1], ()))

    *uo_halves, down_line = stage(
        "stage4", halves_of(uo_r, uo_b) + [[down_shard, *down_z]], [attended[1][0], *uo_b]
    )
    uo_ends = corners(uo_halves)

    uo_pieces = left_blocks(uo_line, uo_b) + right_blocks(uo_r, uo_ends)
    uo_w = [assemble(uo_pieces, "assemble_uo", [down_line])]
    uo_w += [swap(uo_w[0], "p", dp) for dp in others]
    down_line = stage("stage5", [down_line], [uo_w[0]])[0]
    down_r, down_b = sideways(down_line)
    att = [attended[dr][0] for dr in range(2)]
    for dp in others:
        att += [swap(attended[dr][dp], "p", dp) for dr in range(2)]
    ffn_block = ffn // (2 * count_p)
    branch_attn, mid, ffn_input, att_all = call(
        functools.partial(out_kernel, count_p, ffn_block),
        "attn_out",
        [whole, sds((mine, width), F32), whole, whole],
        [hidden, modulation, *att, *uo_w],
        scratch=[pltpu.VMEM((mine, width), F32)],
        after=[down_line],
    )
    gelu_low, slope, d_branch_ffn = call(
        functools.partial(up_kernel, count_p, ffn_block),
        "ffn_up",
        [sds((mine, ffn), BF)] * 2 + [whole],
        [ffn_input, cotangent, modulation, *uo_w],
    )

    down_halves = stage("stage6", halves_of(down_r, down_b), [gelu_low, *down_b])
    down_ends = corners(down_halves)
    fold = down_weight.shape[0] // up_weight.shape[0]
    down_wide = down_weight.shape[1]
    down_sum = Scatter("down", [(down_wide, fold)], count_a // 2)
    uo_sum = Scatter("uo", [(ffn_block, 1), (heads_wide, 1)], count_a // 2)
    qkv_sum = Scatter("qkv", [(heads_wide, 1)] * 3, count_a // 2)

    def split_grad(name, xs, ys, token, fold=1):
        sent = []
        for dp in others:
            token = weight_grad(name, xs, ys, dp, [token], fold)
            sent.append(swap(token, "p", dp))
        own = weight_grad(name, xs, ys, 0, [token], fold)
        return [own, *sent]

    down_parts = split_grad("down_grad", [gelu_low], [d_branch_ffn], down_halves[0], fold)
    down_sum.add([down_parts], (0, 1))

    down_pieces = left_blocks(down_line, down_b) + right_blocks(down_r, down_ends)
    down_w = [assemble(down_pieces, "assemble_down", [down_parts[0]])]
    down_w += [swap(down_w[0], "p", dp) for dp in others]
    token = down_sum.corner([down_w[0]])
    d_up = call(
        functools.partial(d_up_kernel, count_p),
        "d_up",
        [sds((mine, ffn), BF)],
        [d_branch_ffn, slope, *down_w],
        after=[token],
    )[0]
    token = down_sum.side_b([down_sum.side_r([d_up])])
    up_sums = split_grad("up_grad", [ffn_input], [d_up], token)
    token = up_sums[0]
    d_mid, d_branch_attn, sums_mid, *d_att = call(
        functools.partial(mid_back_kernel, count_p, ffn_block),
        "mid_back",
        [whole, whole, sds((3, width), F32)]
        + [sds((mine, heads_wide), BF)] * (2 * count_p),
        [d_up, mid, cotangent, branch_attn, modulation, *uo_w],
        scratch=[pltpu.VMEM((mine, width), F32)],
        after=[token],
    )
    *out_parts, d_ffn_gate = call(
        functools.partial(down_kernel, count_p),
        "ffn_down",
        [sds((block, width), BF)] * 2 + [sds((1, width), F32)],
        [gelu_low, mid, cotangent, modulation, *down_w],
        scratch=[pltpu.VMEM((mine, width), F32)],
        after=[d_branch_attn],
    )
    token = down_sum.line([out_parts[0]])
    out_sums = split_grad("out_grad", [att_all], [d_branch_attn], token)
    uo_sum.add([up_sums, out_sums], (0, 1))

    pairs = heads_wide // PAIR
    d_heads = [
        [d_att[dr]] + [swap(d_att[2 * dp + dr], "p", dp) for dp in others] for dr in range(2)
    ]

    def attend_back(dr, pair, after):
        return call(
            functools.partial(attend_back_kernel, min(512, frames), count_p, pair * PAIR),
            "attend_back",
            [sds((frames, PAIR), BF)] * 3,
            [
                *qkv[dr],
                extra_q,
                extra_k,
                attended[dr][-1],
                cosine,
                sine,
                *attended[dr][:-1],
                *d_heads[dr],
            ],
            after=after,
        )

    def qkv_parts(dr, after):
        return [[weight_grad("qkv_grad", [attn_input], d_qkv[dr], None, after)]]

    d_pairs = [[None] * pairs, [None] * pairs]
    d_qkv = [None, None]

    token = uo_sum.corner()
    d_pairs[1][0] = attend_back(1, 0, [token])
    token = uo_sum.side_b([uo_sum.side_r([d_pairs[1][0][0]])])
    token = down_sum.line_next([token])
    for pair in range(1, pairs):
        d_pairs[1][pair] = attend_back(1, pair, [token])
        token = d_pairs[1][pair][0]
    d_qkv[1] = [d_pairs[1][pair][t] for t in range(3) for pair in range(pairs)]
    qkv_sum.add(qkv_parts(1, [token]), (1,))
    down_grad = down_sum.final([qkv_sum.parts[(0, 1)][0][0][0], *d_heads[0][1:]])[0]
    token = qkv_sum.corner([down_grad])
    token = uo_sum.line([token])
    d_pairs[0][0] = attend_back(0, 0, [token])
    token = uo_sum.line_next([d_pairs[0][0][0]])
    for pair in range(1, pairs):
        d_pairs[0][pair] = attend_back(0, pair, [token])
        token = d_pairs[0][pair][0]
    d_qkv[0] = [d_pairs[0][pair][t] for t in range(3) for pair in range(pairs)]
    qkv_sum.add(qkv_parts(0, [token]), (0,))
    token = qkv_sum.side_b([qkv_sum.side_r([qkv_sum.parts[(0, 0)][0][0][0]])])

    every_d = [*d_qkv[0], *d_qkv[1]]
    pieces = 4
    piece = sds((mine // pieces, width), BF)
    d_own, *d_sent, sums_in = call(
        functools.partial(d_attn_kernel, count_p, len(every_d)),
        "d_attn",
        [whole] + [piece] * (pieces * (count_p - 1)) + [sds((2, width), F32)],
        [*every_d, *qkv_w, hidden_norm],
        after=[token],
    )
    received = [swap(x, "p", 1 + i // pieces) for i, x in enumerate(d_sent)]
    d_mod = call(
        functools.partial(d_modulation_kernel, blocks),
        "d_modulation",
        [sds((devices, ada_cols // PAIR, PAIR), F32)],
        [sums_in, sums_mid, d_ffn_gate],
        vmem=8,
    )[0]
    d_rows = lax.all_to_all(d_mod, every, split_axis=0, concat_axis=0, tiled=True)
    grad_parts = call(
        functools.partial(hidden_back_kernel, pieces),
        "hidden_back",
        [sds((block, width), BF)] * 2,
        [*received, d_own, hidden, d_mid, modulation],
        after=[d_mod],
    )

    d_rows = stage("modulation_rows", [d_rows], [grad_parts[0]])[0]
    token = qkv_sum.line([d_rows])
    ada_grad, d_low = call(
        functools.partial(ada_back_kernel, blocks),
        "ada_back",
        [sds(ada_weight.shape, F32), sds((devices, blocks, ada_rows), F32)],
        [low_mine, d_rows, ada_weight],
        vmem=16,
        after=[token],
    )
    token = qkv_sum.line_next([d_low])
    up_grad, out_grad = uo_sum.final([token])
    hidden_out = restore_rows(*out_parts, [up_grad])
    d_low = lax.all_to_all(d_low, every, split_axis=0, concat_axis=0, tiled=True)
    hidden_grad = restore_rows(*grad_parts, [hidden_out])
    query_grad, key_grad, value_grad = qkv_sum.final([hidden_grad])

    time_grad = call(
        functools.partial(time_grad_kernel, blocks, count_p),
        "time_grad",
        [sds((2, width), F32)],
        [d_low, time_embed],
        vmem=8,
        after=[query_grad],
    )[0]
    return (
        hidden_out,
        hidden_grad,
        time_grad,
        ada_grad,
        query_grad,
        key_grad,
        value_grad,
        out_grad,
        up_grad,
        down_grad,
    )


def solution(mesh):
    count_dp, count_sp = mesh.shape["dp"], mesh.shape["sp"]
    fine = Mesh(mesh.devices.reshape(4, count_dp // 4, 2, count_sp // 2), ("a", "b", "r", "p"))
    dp, sp = ("a", "b"), ("r", "p")
    in_specs = (
        (P(dp, sp, None), P(dp, None), P(dp, None)) + (P(dp, sp),) * 7 + (P(dp, sp, None),)
    )
    out_specs = (P(dp, sp, None), P(dp, sp, None), P(dp, None)) + (P(dp, sp),) * 7
    return jax.shard_map(local, mesh=fine, in_specs=in_specs, out_specs=out_specs, check_vma=False)
```

```python
import functools

import jax
import jax.numpy as jnp
from jax import lax
from jax.experimental import pallas as pl
from jax.experimental.pallas import tpu as pltpu
from jax.sharding import Mesh
from jax.sharding import PartitionSpec as P

HEAD_DIM = 64
PAIR = 2 * HEAD_DIM
LOG2E = 1.4426950408889634
LN2 = 0.6931471805599453
HIGH = lax.Precision.HIGHEST
F32 = jnp.float32
BF = jnp.bfloat16
NN = (((1,), (0,)), ((), ()))
NT = (((1,), (1,)), ((), ()))
TN = (((0,), (0,)), ((), ()))
ANY = pl.BlockSpec(memory_space=pl.ANY)
HBM = pl.BlockSpec(memory_space=pltpu.HBM)
VM = pl.BlockSpec(memory_space=pltpu.VMEM)
MIB = 1 << 20
TILE = 128


def dot(left, right, dims=NN):
    return lax.dot_general(left, right, dims, preferred_element_type=F32)


def sds(shape, dtype):
    return jax.ShapeDtypeStruct(shape, dtype)


def call(kernel, name, outs, args, scratch=(), vmem=9, after=(), spec=VM, to=VM):
    taken = len(args)

    def body(*refs):
        kernel(*refs[:taken], *refs[taken + len(after) :])

    return pl.pallas_call(
        body,
        name=name,
        in_specs=[spec] * taken + [ANY] * len(after),
        out_specs=[to] * len(outs),
        out_shape=outs,
        scratch_shapes=scratch,
        compiler_params=pltpu.CompilerParams(vmem_limit_bytes=vmem * MIB),
        cost_estimate=pl.CostEstimate(flops=1, bytes_accessed=1, transcendentals=0),
    )(*args, *after)


def swap(value, axis, offset=1):
    count = lax.axis_size(axis)
    return lax.ppermute(value, axis, [(i, i ^ offset) for i in range(count)])


def stage_kernel(plan, *refs):
    count = sum(len(pieces) for pieces in plan)
    ins, outs = iter(refs[:count]), refs[count:]
    for pieces, out in zip(plan, outs):
        at = 0
        for start, size in pieces:
            ref = next(ins)
            if start is not None:
                out[at : at + size] = ref[start : start + size]
            elif len(ref.shape) < len(out.shape):
                out[at] = ref[...]
            else:
                out[...] = ref[...]
            at += size


def stage(name, groups, after=()):
    arrays, plan, outs = [], [], []
    for group in groups:
        if not isinstance(group, list):
            arrays.append(group)
            plan.append(((None, 1),))
            outs.append(sds(group.shape, group.dtype))
            continue
        pieces, total = [], 0
        for piece in group:
            array, start, size = piece if isinstance(piece, tuple) else (piece, None, 1)
            arrays.append(array)
            pieces.append((start, size))
            total += size
        tail = array.shape if start is None else array.shape[1:]
        plan.append(tuple(pieces))
        outs.append(sds((total,) + tail, array.dtype))
    return call(
        functools.partial(stage_kernel, tuple(plan)),
        name,
        outs,
        arrays,
        vmem=12,
        after=after,
    )


def pick_kernel(*refs):
    count = (len(refs) - 1) // 3
    ins, outs, sems = refs[:count], refs[count:-1], refs[-1]
    at_r = lax.axis_index("r")
    copies = []
    for i, ref in enumerate(ins):
        for j, row in enumerate((at_r, 1 - at_r)):
            at = 2 * i + j
            copies.append(pltpu.make_async_copy(ref.at[row], outs[at], sems.at[at]))
    for copy in copies:
        copy.start()
    for copy in copies:
        copy.wait()


def exchange_rows(arrays, after=()):
    outs = [sds(x.shape[1:], x.dtype) for x in arrays for _ in range(2)]
    picked = call(
        pick_kernel,
        "pick_rows",
        outs,
        arrays,
        scratch=[pltpu.SemaphoreType.DMA((len(outs),))],
        vmem=60,
        after=after,
        spec=HBM,
    )
    return [(own, swap(other, "r")) for own, other in zip(picked[::2], picked[1::2])]


def place_kernel(own_ref, other_ref, out_ref, sems):
    at_r = lax.axis_index("r")
    copies = [
        pltpu.make_async_copy(own_ref, out_ref.at[at_r], sems.at[0]),
        pltpu.make_async_copy(other_ref, out_ref.at[1 - at_r], sems.at[1]),
    ]
    for copy in copies:
        copy.start()
    for copy in copies:
        copy.wait()


def restore_rows(own, other, after=()):
    outs = [sds((2,) + own.shape, own.dtype)]
    args = [own, swap(other, "r")]
    sems = [pltpu.SemaphoreType.DMA((2,))]
    return call(
        place_kernel, "place_rows", outs, args, scratch=sems, vmem=8, after=after, to=HBM
    )[0]


def pack_kernel(*refs):
    ins, (out, sems) = refs[:-2], refs[-2:]
    at, copies = 0, []
    for i, ref in enumerate(ins):
        place = out.at[:, pl.ds(at, ref.shape[1])]
        copies.append(pltpu.make_async_copy(ref, place, sems.at[i]))
        at += ref.shape[1]
    for copy in copies:
        copy.start()
    for copy in copies:
        copy.wait()


def pack(shards, after=(), vmem=8):
    width = sum(x.shape[1] for x in shards)
    outs = [sds((shards[0].shape[0], width), BF)]
    return call(
        pack_kernel,
        "pack",
        outs,
        shards,
        scratch=[pltpu.SemaphoreType.DMA((len(shards),))],
        vmem=vmem,
        after=after,
        spec=HBM,
    )[0]


def along_line(shard):
    return [swap(shard, "a", d) for d in range(1, lax.axis_size("a"))]


def sideways(first):
    return swap(first, "r"), [swap(first, "b", dy) for dy in range(1, lax.axis_size("b"))]


def halves_of(side_r, sides_b):
    half = side_r.shape[0] // 2
    return [[(side, 0, half)] for side in sides_b] + [[(side_r, half, half)]]


def corners(halves):
    *sides_b, side_r = halves
    return [
        (swap(side_b, "r"), swap(side_r, "b", dy + 1)) for dy, side_b in enumerate(sides_b)
    ]


def span(dy, dr, start, stop):
    return [(dy, dr, dz) for dz in range(start, stop)]


def left_blocks(first, sides_b):
    line = first.shape[0]
    left = [(first, span(0, 0, 0, line))]
    return left + [(side, span(dy + 1, 0, 0, line)) for dy, side in enumerate(sides_b)]


def right_blocks(side_r, ends):
    line = side_r.shape[0]
    right = [(side_r, span(0, 1, 0, line))]
    for dy, (low, high) in enumerate(ends):
        right.append((low, span(dy + 1, 1, 0, line // 2)))
        right.append((high, span(dy + 1, 1, line // 2, line)))
    return right


def totals(refs, members, t):
    wide, refs = [], iter(refs)
    for member in members:
        wide.append(sum(next(refs)[index + (t,)].astype(F32) for _, index in member))
    return wide[0] if len(wide) == 1 else jnp.concatenate(wide, axis=1)


class Scatter:
    def __init__(self, name, cuts, cut):
        self.name, self.cuts, self.cut = name, cuts, cut
        self.line_count = lax.axis_size("a")
        self.count_b = lax.axis_size("b")
        self.parts = {}
        self.first_r = {dy: [] for dy in range(1, self.count_b)}
        self.first_b = {dy: [] for dy in range(1, self.count_b)}

    def add(self, members, rights):
        for dy in range(self.count_b):
            for at, dr in enumerate(rights):
                index = (dy,) if len(rights) == 1 else (dy, at)
                found = self.parts.setdefault((dy, dr), [])
                found += [[(x, index) for x in member] for member in members]

    def step(self, label, body, shapes, members, extra, after):
        arrays = [array for member in members for array, _ in member]
        return call(body, self.name + label, shapes, arrays + extra, after=after)

    def block(self, members):
        return members[0][0][0].shape[-2], sum(member[0][0].shape[-1] for member in members)

    def corner(self, after=(), some=slice(None)):
        cut, line = self.cut, self.line_count
        for dy in range(1, self.count_b):
            members = self.parts[(dy, 1)][some]
            shape = self.block(members)

            def body(*refs, members=members):
                for t in range(line):
                    out, at = (refs[-2], t) if t < cut else (refs[-1], t - cut)
                    out[at] = totals(refs, members, t).astype(BF)

            shapes = [sds((cut,) + shape, BF), sds((line - cut,) + shape, BF)]
            first, second = self.step("_corner", body, shapes, members, [], after)
            self.first_r[dy].append(swap(first, "r"))
            self.first_b[dy].append(swap(second, "b", dy))
        return first

    def side_r(self, after=()):
        members = self.parts[(0, 1)]
        groups = list(self.first_b.values())
        extra = [x for group in groups for x in group]
        cut, line = self.cut, self.line_count

        def body(*refs):
            more, out = refs[-1 - len(extra) : -1], refs[-1]
            for t in range(line):
                total = totals(refs, members, t)
                if t >= cut:
                    total = total + self.added(more, len(groups), t - cut)
                out[t] = total.astype(BF)

        shapes = [sds((line,) + self.block(members), BF)]
        after = [*after, *[x for group in self.first_r.values() for x in group]]
        side = self.step("_side_r", body, shapes, members, extra, after)[0]
        self.from_r = swap(side, "r")
        return side

    def added(self, refs, groups, t):
        each = len(refs) // groups
        total = 0.0
        for at in range(0, len(refs), each):
            pieces = [ref[t].astype(F32) for ref in refs[at : at + each]]
            total = total + (pieces[0] if each == 1 else jnp.concatenate(pieces, axis=1))
        return total

    def side_b(self, after=()):
        self.from_b = []
        cut, line = self.cut, self.line_count
        for dy in range(1, self.count_b):
            members = self.parts[(dy, 0)]
            extra = self.first_r[dy]

            def body(*refs, members=members, extra=extra):
                more, out = refs[-1 - len(extra) : -1], refs[-1]
                for t in range(line):
                    total = totals(refs, members, t)
                    if t < cut:
                        total = total + self.added(more, 1, t)
                    out[t] = total.astype(BF)

            shapes = [sds((line,) + self.block(members), BF)]
            side = self.step("_side_b", body, shapes, members, extra, after)[0]
            self.from_b.append(swap(side, "b", dy))
        return side

    def line(self, after=()):
        members = self.parts[(0, 0)]
        shape, line = self.block(members), self.line_count
        extra = [self.from_r, *self.from_b]
        kept = line // 2

        def body(*refs):
            more, (keep, sent) = refs[-2 - len(extra) : -2], refs[-2:]
            for t in range(line):
                total = totals(refs, members, t) + sum(ref[t].astype(F32) for ref in more)
                if t % 2:
                    sent[t // 2] = total.astype(BF)
                else:
                    keep[t // 2] = total

        shapes = [sds((kept,) + shape, F32), sds((kept,) + shape, BF)]
        self.keep, sent = self.step("_line", body, shapes, members, extra, after)
        self.step_size, self.from_a = 1, swap(sent, "a", 1)
        return sent

    def line_next(self, after=()):
        kept = self.keep.shape[0] // 2
        shape = self.keep.shape[1:]

        def body(keep_ref, recv_ref, keep, sent):
            for t in range(2 * kept):
                total = keep_ref[t] + recv_ref[t].astype(F32)
                if t % 2:
                    sent[t // 2] = total.astype(BF)
                else:
                    keep[t // 2] = total

        shapes = [sds((kept,) + shape, F32), sds((kept,) + shape, BF)]
        self.keep, sent = self.step("_line_next", body, shapes, [], [self.keep, self.from_a], after)
        self.step_size *= 2
        self.from_a = swap(sent, "a", self.step_size)
        return sent

    def final(self, after=()):
        depth = self.keep.shape[1]
        cuts = self.cuts

        def body(keep_ref, recv_ref, *outs):
            total = keep_ref[0] + recv_ref[0].astype(F32)
            at = 0
            for out, (width, fold) in zip(outs, cuts):
                for i in range(fold):
                    out[i * depth : (i + 1) * depth, :] = total[:, at : at + width]
                    at += width

        shapes = [sds((depth * fold, width), F32) for width, fold in cuts]
        return self.step("_final", body, shapes, [], [self.keep, self.from_a], after)


def assemble_kernel(meta, keep_r, count_b, *refs):
    ins, out = refs[: len(meta)], refs[len(meta)]
    at_a, at_b, at_r = (lax.axis_index(name) for name in ("a", "b", "r"))
    for ref, places in zip(ins, meta):
        depth = ref.shape[1]
        for t, (dy, dr, dz) in enumerate(places):
            row = pl.multiple_of(((at_a ^ dz) * count_b + (at_b ^ dy)) * depth, depth)
            if keep_r:
                out[at_r ^ dr, pl.ds(row, depth), :] = ref[t]
            else:
                out[pl.ds(row, depth), :] = ref[t]


def assemble(pieces, name, after=(), keep_r=True):
    count_a, count_b = lax.axis_size("a"), lax.axis_size("b")
    arrays = [piece for piece, _ in pieces]
    meta = [places for _, places in pieces]
    _, depth, width = arrays[0].shape
    shape = (count_a * count_b * depth, width)
    if keep_r:
        shape = (2,) + shape
    return call(
        functools.partial(assemble_kernel, tuple(meta), keep_r, count_b),
        name,
        [sds(shape, BF)],
        arrays,
        vmem=16,
        after=after,
    )[0]


def normed(values):
    centre = values - jnp.mean(values, axis=-1, keepdims=True)
    spread = lax.rsqrt(jnp.mean(centre * centre, axis=-1, keepdims=True) + 1e-06)
    return centre * spread, spread


def norm_back(grad, norm, spread):
    return spread * (
        grad
        - jnp.mean(grad, axis=-1, keepdims=True)
        - norm * jnp.mean(grad * norm, axis=-1, keepdims=True)
    )


def modulation_part_kernel(low_ref, ada_ref, out_ref):
    low = low_ref[...]
    for i in range(out_ref.shape[1]):
        out_ref[:, i, :] = dot(low, ada_ref[:, i * PAIR : (i + 1) * PAIR])


def modulation_sum_kernel(blocks, in_ref, out_ref):
    groups, slabs = in_ref.shape[0] // blocks, in_ref.shape[1]
    wide = out_ref.shape[1] // PAIR
    for block in range(blocks):
        total = in_ref[block]
        for group in range(1, groups):
            total = total + in_ref[group * blocks + block]
        for i in range(slabs):
            m, c = divmod(block * slabs + i, wide)
            out_ref[m : m + 1, c * PAIR : (c + 1) * PAIR] = total[i : i + 1]


def d_modulation_kernel(blocks, in_ref, mid_ref, gate_ref, out_ref):
    groups, slabs = out_ref.shape[0] // blocks, out_ref.shape[1]
    rows = [in_ref[m : m + 1] for m in range(2)] + [mid_ref[m : m + 1] for m in range(3)]
    rows.append(gate_ref[...])
    wide = gate_ref.shape[1] // PAIR
    for block in range(blocks):
        for i in range(slabs):
            m, c = divmod(block * slabs + i, wide)
            value = rows[m][:, c * PAIR : (c + 1) * PAIR]
            for group in range(groups):
                out_ref[group * blocks + block, i : i + 1, :] = value


def ada_back_kernel(copies, low_ref, rows_ref, ada_ref, grad_ref, out_ref):
    kinds = dict(preferred_element_type=F32, precision=HIGH)
    low, d_low = low_ref[...].astype(F32), 0.0
    for i in range(rows_ref.shape[1]):
        lanes = slice(i * PAIR, (i + 1) * PAIR)
        rows = rows_ref[:, i, :]
        grad_ref[:, lanes] = lax.dot_general(low, rows, TN, **kinds)
        d_low = d_low + lax.dot_general(rows, ada_ref[:, lanes].astype(F32), NT, **kinds)
    for i in range(out_ref.shape[0]):
        start = i // copies * copies
        out_ref[i] = d_low[start : start + copies]


def time_grad_kernel(copies, count_p, in_ref, time_ref, out_ref):
    depth = in_ref.shape[2]
    time = time_ref[...].astype(F32)
    sigmoid = 1.0 / (1.0 + jnp.exp(-time))
    slope = sigmoid * (1.0 + time * (1.0 - sigmoid))
    for group in range(in_ref.shape[0] // copies):
        total = in_ref[group * copies]
        for i in range(1, copies):
            total = total + in_ref[group * copies + i]
        lanes = slice(group * depth, (group + 1) * depth)
        for r in range(2):
            row = jnp.sum(total[r * count_p : (r + 1) * count_p], axis=0, keepdims=True)
            out_ref[r : r + 1, lanes] = row * slope[r : r + 1, lanes]


def attn_input_kernel(*refs):
    x_refs, (mod_ref, out_ref, norm_ref) = refs[:-3], refs[-3:]
    scale, shift = 1.0 + mod_ref[1:2, :], mod_ref[0:1, :]
    at = 0
    for ref in x_refs:
        for row in range(0, ref.shape[0], TILE):
            norm, _ = normed(ref[row : row + TILE, :].astype(F32))
            rows = slice(at + row, at + row + TILE)
            norm_ref[rows, :] = norm.astype(BF)
            out_ref[rows, :] = (norm * scale + shift).astype(BF)
        at += ref.shape[0]


def lane_ids(width=PAIR):
    return lax.broadcasted_iota(jnp.int32, (1, width), 1)


def turn(values, cosine, sine):
    early = lane_ids() % HEAD_DIM < HEAD_DIM // 2
    step = HEAD_DIM // 2
    other = jnp.where(early, pltpu.roll(values, PAIR - step, 1), pltpu.roll(values, step, 1))
    return values * cosine + other * sine


def qkv_kernel(x_ref, w_ref, cos_ref, sin_ref, q_ref, k_ref, v_ref):
    width = q_ref.shape[1]
    weights = w_ref[...]
    step = min(512, x_ref.shape[0])
    for row in range(0, x_ref.shape[0], step):
        rows = slice(row, row + step)
        both = dot(x_ref[rows, :], weights)
        cosine, sine = cos_ref[rows, :], sin_ref[rows, :]
        for lane in range(0, width, PAIR):
            lanes, at = slice(lane, lane + PAIR), width + lane
            query = turn(both[:, lanes], cosine, sine) * (HEAD_DIM**-0.5 * LOG2E)
            q_ref[rows, lanes] = query.astype(BF)
            k_ref[rows, lanes] = turn(both[:, at : at + PAIR], cosine, sine).astype(BF)
        v_ref[rows, :] = both[:, 2 * width :].astype(BF)


def attend_kernel(block, q_ref, k_ref, v_ref, aq_ref, ak_ref, *refs):
    o_refs, lse_ref = refs[:-1], refs[-1]
    depth = o_refs[0].shape[0]
    frames = q_ref.shape[0]
    keys = jnp.concatenate([k_ref[...], ak_ref[...]], axis=1)
    values = v_ref[...]
    low = lane_ids() < HEAD_DIM
    zero, one = jnp.zeros((), BF), jnp.ones((), BF)

    def attend(with_max):
        for start in range(0, frames, block):
            rows = pl.ds(start, block)
            query, extra = q_ref[rows, :], aq_ref[rows, :]
            outs, logs = [], []
            for head in range(2):
                mine = low if head == 0 else jnp.logical_not(low)
                left = jnp.concatenate([jnp.where(mine, query, zero), extra], axis=1)
                scores = dot(left, keys, NT)
                if with_max:
                    top = jnp.max(scores, axis=1, keepdims=True)
                    scores = scores - top
                weights = jnp.exp2(scores).astype(BF)
                mixed = dot(weights, jnp.where(mine, values, one))
                outs.append(mixed / pltpu.roll(mixed, HEAD_DIM, 1))
                log = jnp.log2(jnp.maximum(mixed, 1e-30))
                logs.append(log + top if with_max else log)
            both = jnp.where(low, outs[0], outs[1]).astype(BF)
            o_refs[start // depth][pl.ds(start % depth, block), :] = both
            lse_ref[rows, :] = jnp.where(low, logs[1], logs[0])

    query_all, key_all = q_ref[...].astype(F32), k_ref[...].astype(F32)
    bound = jnp.max(jnp.sum(query_all * query_all, axis=1)) * jnp.max(
        jnp.sum(key_all * key_all, axis=1)
    )
    small = bound < 3600.0

    @pl.when(small)
    def _():
        attend(False)

    @pl.when(jnp.logical_not(small))
    def _():
        attend(True)


def split3(values):
    first = values.astype(BF)
    rest = values - first.astype(F32)
    second = rest.astype(BF)
    return first, second, (rest - second.astype(F32)).astype(BF)


def placed(parts, start, base):
    lanes = lane_ids()
    for i, part in enumerate(parts):
        base = jnp.where(lanes == start + i, part, base)
    return base


def attend_back_kernel(block, parts, lanes_at, q_ref, k_ref, v_ref, aq_ref, ak_ref, lse_ref, cos_ref, sin_ref, *refs):
    o_refs, do_refs, (dq_ref, dk_ref, dv_ref) = refs[:parts], refs[parts : 2 * parts], refs[2 * parts :]
    frames = q_ref.shape[0]
    at = slice(lanes_at, lanes_at + PAIR)
    lanes = lane_ids()
    low = lanes < HEAD_DIM
    zero = jnp.zeros((), BF)
    query, extra, lse = q_ref[:, at], aq_ref[...], lse_ref[:, at]
    grad = jnp.concatenate([ref[:, at] for ref in do_refs], axis=0)
    out = jnp.concatenate([ref[:, at] for ref in o_refs], axis=0)
    product = grad.astype(F32) * out.astype(F32)
    queries, grads, lefts, rights = [], [], [], []
    for head in range(2):
        mine = low if head == 0 else jnp.logical_not(low)
        log = lse[:, HEAD_DIM : HEAD_DIM + 1] if head == 0 else lse[:, 0:1]
        queries.append(jnp.where(mine, query, zero))
        lefts.append(jnp.concatenate([queries[-1], placed(split3(-log), 8, extra)], axis=1))
        inner = -jnp.sum(jnp.where(mine, product, 0.0), axis=1, keepdims=True)
        grads.append(jnp.where(mine, grad, zero))
        tail = placed(split3(inner), 0, jnp.zeros((frames, PAIR), BF))
        rights.append(jnp.concatenate([grads[-1], tail], axis=1))
    ones = jnp.where(lanes < 3, 1.0, 0.0).astype(BF)
    dq_turned = jnp.zeros((PAIR, frames), F32)
    for start in range(0, frames, block):
        rows = pl.ds(start, block)
        key, value = k_ref[rows, at], v_ref[rows, at]
        keys = jnp.concatenate([key, ak_ref[rows, :]], axis=1)
        values = jnp.concatenate([value, jnp.broadcast_to(ones, value.shape)], axis=1)
        dv, dk = 0.0, 0.0
        for head in range(2):
            mine = low if head == 0 else jnp.logical_not(low)
            soft = jnp.exp2(dot(keys, lefts[head], NT))
            d_scores = (soft * dot(values, rights[head], NT)).astype(BF)
            dv = dv + dot(soft.astype(BF), grads[head])
            dk = dk + dot(d_scores, queries[head])
            dq_turned = dq_turned + dot(jnp.where(mine, key, zero), d_scores, TN)
        dv_ref[rows, :] = dv.astype(BF)
        dk_ref[rows, :] = turn(dk * LN2, cos_ref[rows, :], -sin_ref[rows, :]).astype(BF)
    dq = dq_turned.T * HEAD_DIM**-0.5
    dq_ref[...] = turn(dq, cos_ref[...], -sin_ref[...]).astype(BF)


def column(dr, dp):
    at_r, at_p = lax.axis_index("r"), lax.axis_index("p")
    return (at_r ^ dr) * lax.axis_size("p") + (at_p ^ dp)


def lanes_of(index, width):
    return pl.ds(pl.multiple_of(index * width, width), width)


def column_blocks(weight_refs):
    count_r = lax.axis_size("r")
    count_p = lax.axis_size("p")
    at_p = lax.axis_index("p")
    for dp, ref in enumerate(weight_refs):
        for r in range(count_r):
            yield r * count_p + (at_p ^ dp), ref, r


def out_kernel(count_p, at_lane, x_ref, mod_ref, *refs):
    att_refs = refs[: 2 * count_p]
    w_refs = refs[2 * count_p : 3 * count_p]
    branch_ref, mid_ref, ffn_ref, att_ref, sum_ref = refs[3 * count_p :]
    width = att_refs[0].shape[1]
    for dp in range(count_p):
        for dr in range(2):
            att_ref[:, lanes_of(column(dr, dp), width)] = att_refs[2 * dp + dr][...]
    att = att_ref[...]
    for j, ref, r in column_blocks(w_refs):
        sum_ref[:, lanes_of(j, width)] = dot(att, ref[r, :, at_lane : at_lane + width])
    gate, scale, shift = mod_ref[2:3, :], 1.0 + mod_ref[4:5, :], mod_ref[3:4, :]
    for row in range(0, x_ref.shape[0], TILE):
        rows = slice(row, row + TILE)
        branch = sum_ref[rows, :]
        branch_ref[rows, :] = branch.astype(BF)
        mid = x_ref[rows, :].astype(F32) + gate * branch
        mid_ref[rows, :] = mid
        norm, _ = normed(mid)
        ffn_ref[rows, :] = (norm * scale + shift).astype(BF)


def up_kernel(count_p, wide, x_ref, cot_ref, mod_ref, *refs):
    w_refs, (gelu_ref, slope_ref, dbf_ref) = refs[:count_p], refs[count_p:]
    dbf_ref[...] = (cot_ref[...].astype(F32) * mod_ref[5:6, :]).astype(BF)
    x = x_ref[...]
    root = 0.7978845608028654
    for j, ref, r in column_blocks(w_refs):
        up = dot(x, ref[r, :, :wide])
        square = up * up
        tanh = jnp.tanh(up * (root + (root * 0.044715) * square))
        half = 0.5 + 0.5 * tanh
        at = lanes_of(j, wide)
        gelu_ref[:, at] = (up * half).astype(BF)
        slope = half + up * (1.0 - tanh * tanh) * (0.5 * root + (0.5 * root * 0.134145) * square)
        slope_ref[:, at] = slope.astype(BF)


def down_kernel(count_p, gelu_ref, mid_ref, cot_ref, mod_ref, *refs):
    w_refs = refs[:count_p]
    out_refs, (dgate_ref, sum_ref) = refs[count_p:-2], refs[-2:]
    gelu = gelu_ref[...]
    for j, ref, r in column_blocks(w_refs):
        sum_ref[:, lanes_of(j, ref.shape[2])] = dot(gelu, ref[r])
    gate, total, depth = mod_ref[5:6, :], 0.0, out_refs[0].shape[0]
    for row in range(0, mid_ref.shape[0], TILE):
        rows = slice(row, row + TILE)
        branch = sum_ref[rows, :]
        place = out_refs[row // depth]
        place[row % depth : row % depth + TILE, :] = (mid_ref[rows, :] + gate * branch).astype(BF)
        total = total + jnp.sum(cot_ref[rows, :].astype(F32) * branch, axis=0, keepdims=True)
    dgate_ref[...] = total


def turned_dot(x_ref, w_refs, start=0, width=None):
    total = 0.0
    for j, ref, r in column_blocks(w_refs):
        wide = width or ref.shape[2]
        total = total + dot(x_ref[:, lanes_of(j, wide)], ref[r, :, start : start + wide], NT)
    return total


def d_up_kernel(count_p, dbf_ref, slope_ref, *refs):
    w_refs, (out_ref,) = refs[:count_p], refs[count_p:]
    out_ref[...] = (turned_dot(dbf_ref, w_refs) * slope_ref[...].astype(F32)).astype(BF)


def mid_back_kernel(count_p, wide, d_up_ref, mid_ref, cot_ref, branch_ref, mod_ref, *refs):
    w_refs = refs[:count_p]
    d_mid_ref, dba_ref, sums_ref = refs[count_p : count_p + 3]
    att_refs, all_ref = refs[count_p + 3 : -1], refs[-1]
    all_ref[...] = turned_dot(d_up_ref, w_refs, 0, wide)
    scale, gate = 1.0 + mod_ref[4:5, :], mod_ref[2:3, :]
    sums = [0.0, 0.0, 0.0]
    for row in range(0, mid_ref.shape[0], TILE):
        rows = slice(row, row + TILE)
        d_in = all_ref[rows, :]
        norm, spread = normed(mid_ref[rows, :])
        d_mid = cot_ref[rows, :].astype(F32) + norm_back(d_in * scale, norm, spread)
        d_mid_ref[rows, :] = d_mid.astype(BF)
        dba_ref[rows, :] = (d_mid * gate).astype(BF)
        parts = (d_mid * branch_ref[rows, :].astype(F32), d_in, d_in * norm)
        sums = [s + jnp.sum(part, axis=0, keepdims=True) for s, part in zip(sums, parts)]
    for i in range(3):
        sums_ref[i : i + 1, :] = sums[i]
    width = att_refs[0].shape[1]
    all_ref[...] = turned_dot(dba_ref, w_refs, wide, width)
    for dp in range(count_p):
        for dr in range(2):
            att_refs[2 * dp + dr][...] = all_ref[:, lanes_of(column(dr, dp), width)].astype(BF)


def weight_grad_kernel(counts, places, sizes, *refs):
    count_x, count_y = counts
    x_refs, y_refs, out_ref = refs[:count_x], refs[count_x:-1], refs[-1]
    count_a, count_b = sizes
    count_p = lax.axis_size("p")
    at_a, at_b = lax.axis_index("a"), lax.axis_index("b")
    depth = x_refs[0].shape[1] // (count_a * count_b)
    fold = depth // out_ref.shape[-2]
    xs = [ref[...] for ref in x_refs]
    for dp, dr in places:
        if dr is None:
            ys = [jnp.concatenate([ref[...] for ref in y_refs], axis=1)]
        else:
            ys = []
            for ref in y_refs:
                ys.append(ref[:, lanes_of(column(dr, dp), ref.shape[1] // (2 * count_p))])
        at = 0
        for x, y in zip(xs, ys):
            grad = dot(x, y, TN).astype(BF)
            part = depth // fold
            for i in range(count_a * count_b * fold):
                block, piece = divmod(i, fold)
                dz, dy = at_a ^ (block // count_b), at_b ^ (block % count_b)
                rows = grad[i * part : (i + 1) * part]
                lanes = slice(at + piece * y.shape[1], at + (piece + 1) * y.shape[1])
                if dr is None:
                    out_ref[dy, dz, :, lanes] = rows
                else:
                    out_ref[dy, dr, dz, :, lanes] = rows
            at += y.shape[1] * fold


def weight_grad(name, xs, ys, dp=None, after=(), fold=1):
    count_a, count_b = lax.axis_size("a"), lax.axis_size("b")
    depth = xs[0].shape[1] // (count_a * count_b)
    width = sum(y.shape[1] for y in ys)
    if dp is not None:
        width //= 2 * lax.axis_size("p")
        places = [(dp, dr) for dr in reversed(range(2))]
        outs = [sds((count_b, 2, count_a, depth // fold, width * fold), BF)]
    else:
        places = [(0, None)]
        outs = [sds((count_b, count_a, depth, width), BF)]
    return call(
        functools.partial(
            weight_grad_kernel, (len(xs), len(ys)), tuple(places), (count_a, count_b)
        ),
        name,
        outs,
        [*xs, *ys],
        after=after,
    )[0]


def d_attn_kernel(count_p, count_d, *refs):
    d_refs, ws = refs[:count_d], refs[count_d : count_d + 2]
    x_ref, own_ref, outs, sums_ref = refs[count_d + 2], refs[count_d + 3], refs[count_d + 4 : -1], refs[-1]
    depth = x_ref.shape[0] // count_p
    pieces = len(outs) // (count_p - 1) if outs else 0
    sums = [0.0, 0.0]
    for c in reversed(range(count_p)):
        rows = slice(c * depth, (c + 1) * depth)
        d_in = 0.0
        for half, w_ref in enumerate(ws):
            parts = d_refs[half * count_d // 2 : (half + 1) * count_d // 2]
            left = jnp.concatenate([ref[rows, :] for ref in parts], axis=1)
            d_in = d_in + dot(left, w_ref[...], NT)
        norm = x_ref[rows, :].astype(F32)
        sums[0] = sums[0] + jnp.sum(d_in, axis=0, keepdims=True)
        sums[1] = sums[1] + jnp.sum(d_in * norm, axis=0, keepdims=True)
        if c == 0:
            own_ref[...] = d_in.astype(BF)
        for i in range(pieces if c else 0):
            out = outs[(c - 1) * pieces + i]
            out[...] = d_in[i * out.shape[0] : (i + 1) * out.shape[0]].astype(BF)
    for i in range(2):
        sums_ref[i : i + 1, :] = sums[i]


def hidden_back_kernel(pieces, *refs):
    recv, (own_d_ref, x_ref, d_mid_ref, mod_ref, *out_refs) = refs[:-6], refs[-6:]
    scale, depth = 1.0 + mod_ref[1:2, :], out_refs[0].shape[0]
    step = recv[0].shape[0] if recv else depth
    for row in range(0, x_ref.shape[0], step):
        rows = slice(row, row + step)
        d_in = own_d_ref[rows, :].astype(F32)
        for i in range(0, len(recv), pieces):
            d_in = d_in + recv[i + row // step][...].astype(F32)
        norm, spread = normed(x_ref[rows, :].astype(F32))
        value = d_mid_ref[rows, :].astype(F32) + norm_back(d_in * scale, norm, spread)
        out_refs[row // depth][row % depth : row % depth + step, :] = value.astype(BF)


def local(
    hidden_in,
    time_embed,
    seg_lengths,
    ada_weight,
    query_weight,
    key_weight,
    value_weight,
    out_weight,
    up_weight,
    down_weight,
    out_cotangent,
):
    count_a, count_b, count_p = (lax.axis_size(name) for name in ("a", "b", "p"))
    at_a, at_b, at_r, at_p = (lax.axis_index(name) for name in ("a", "b", "r", "p"))
    width = hidden_in.shape[2]
    block = hidden_in.shape[1]
    mine = 2 * block
    frames = mine * count_p
    heads_wide = query_weight.shape[1]
    ffn = up_weight.shape[1] * 2 * count_p
    others = range(1, count_p)

    qkv_shard = pack([query_weight, key_weight, value_weight], vmem=60)
    qkv_z = along_line(qkv_shard)
    every = ("a", "b", "r", "p")
    time_vecs = time_embed.astype(F32)
    time_low = jax.nn.silu(time_vecs).astype(BF)
    low_mine = lax.all_to_all(time_low, ("a", "b"), split_axis=1, concat_axis=0, tiled=True)
    low_mine = jnp.repeat(low_mine, count_p, axis=0)
    ada_rows, ada_cols = ada_weight.shape
    devices, blocks = low_mine.shape[0], 2 * count_p
    part = call(
        modulation_part_kernel,
        "modulation_part",
        [sds((devices, ada_cols // PAIR, PAIR), F32)],
        [low_mine, ada_weight],
        vmem=8,
    )[0]
    (hidden_own, hidden_other), (cot_own, cot_other) = exchange_rows(
        [hidden_in, out_cotangent]
    )
    qkv_line = stage("stage1", [[qkv_shard, *qkv_z]], [hidden_other, cot_other, part])[0]

    uo_shard = pack([up_weight, out_weight], [qkv_line])
    qkv_r, qkv_b = sideways(qkv_line)
    uo_z = along_line(uo_shard)
    hidden, cotangent = stage(
        "join", [[hidden_own, hidden_other], [cot_own, cot_other]], [uo_shard]
    )
    hidden, cotangent = hidden.reshape(mine, width), cotangent.reshape(mine, width)
    hidden_parts = [hidden] + [swap(hidden, "p", dp) for dp in others]
    part = lax.all_to_all(part, every, split_axis=0, concat_axis=0, tiled=True)
    modulation = call(
        functools.partial(modulation_sum_kernel, blocks),
        "modulation",
        [sds((6, width), F32)],
        [part],
        vmem=8,
    )[0]

    lengths = lax.dynamic_index_in_dim(seg_lengths, at_r, keepdims=False)
    frame_ids = jnp.concatenate(
        [
            ((at_r ^ dr) * count_p + (at_p ^ dp)) * block + jnp.arange(block, dtype=jnp.int32)
            for dp in range(count_p)
            for dr in range(2)
        ]
    )
    passed = frame_ids[:, None] >= jnp.cumsum(lengths)[None, :]
    seg_ids = jnp.sum(passed.astype(jnp.int32), axis=1)
    positions = frame_ids - jnp.sum(jnp.where(passed, lengths[None, :], 0), axis=1)
    half_dim = HEAD_DIM // 2
    lane = jnp.arange(PAIR, dtype=jnp.int32)
    inverse = 10000.0 ** (-(lane % half_dim).astype(F32) / half_dim)
    angles = positions.astype(F32)[:, None] * inverse[None, :]
    cosine = jnp.cos(angles)
    sine = jnp.where(lane % HEAD_DIM < half_dim, -1.0, 1.0)[None, :] * jnp.sin(angles)
    segs = seg_lengths.shape[1]
    same = seg_ids[:, None] == lane[None, :]
    real = (lane < segs)[None, :]
    extra_q = jnp.where(real & ~same, -1e30, 0.0).astype(BF)
    extra_k = jnp.where((real & same) | ((lane >= 8) & (lane < 11))[None, :], 1.0, 0.0).astype(BF)

    heads = sds((frames, heads_wide), BF)
    whole = sds((mine, width), BF)

    def project(x, weights, after):
        return call(qkv_kernel, "qkv", [heads] * 3, [x, weights, cosine, sine], after=after)

    def attend(three, after):
        pair_block = pl.BlockSpec((frames, PAIR), lambda i: (0, i))
        pair_rows = pl.BlockSpec((mine, PAIR), lambda i: (0, i))
        pair_fixed = pl.BlockSpec((frames, PAIR), lambda i: (0, 0))
        return pl.pallas_call(
            lambda *refs: attend_kernel(min(256, mine), *refs[:5], *refs[5 + len(after) :]),
            name="attend",
            grid=(heads_wide // PAIR,),
            in_specs=[pair_block] * 3 + [pair_fixed] * 2 + [ANY] * len(after),
            out_specs=[pair_rows] * count_p + [pair_block],
            out_shape=[sds((mine, heads_wide), BF)] * count_p + [sds((frames, heads_wide), F32)],
            compiler_params=pltpu.CompilerParams(vmem_limit_bytes=9 * MIB),
            cost_estimate=pl.CostEstimate(flops=1, bytes_accessed=1, transcendentals=0),
        )(*three, extra_q, extra_k, *after)

    *qkv_halves, uo_shard2 = stage(
        "stage2", halves_of(qkv_r, qkv_b) + [uo_shard], [*qkv_b, *uo_z[:-1]]
    )
    uo_z = uo_z[:-1] + [swap(uo_shard2, "a", count_a - 1)]
    qkv_ends = corners(qkv_halves)
    attn_input, hidden_norm = call(
        attn_input_kernel,
        "attn_input",
        [sds((frames, width), BF)] * 2,
        [*hidden_parts, modulation],
        after=[qkv_halves[0]],
    )
    qkv_w = [assemble(left_blocks(qkv_line, qkv_b), "assemble_qkv", [attn_input], False)]
    qkv = [project(attn_input, qkv_w[0], ())]
    qkv_w.append(assemble(right_blocks(qkv_r, qkv_ends), "assemble_qkv", [qkv[0][0]], False))

    uo_line = stage("stage3", [[uo_shard, *uo_z]], [qkv_w[1]])[0]
    down_shard = pack([down_weight], [uo_line])
    uo_r, uo_b = sideways(uo_line)
    down_z = along_line(down_shard)
    attended = [attend(qkv[0], [down_shard])]
    qkv.append(project(attn_input, qkv_w[1], [attended[0][0]]))
    attended.append(attend(qkv[1], ()))

    *uo_halves, down_line = stage(
        "stage4", halves_of(uo_r, uo_b) + [[down_shard, *down_z]], [attended[1][0], *uo_b]
    )
    uo_ends = corners(uo_halves)

    uo_pieces = left_blocks(uo_line, uo_b) + right_blocks(uo_r, uo_ends)
    uo_w = [assemble(uo_pieces, "assemble_uo", [down_line])]
    uo_w += [swap(uo_w[0], "p", dp) for dp in others]
    down_line = stage("stage5", [down_line], [uo_w[0]])[0]
    down_r, down_b = sideways(down_line)
    att = [attended[dr][0] for dr in range(2)]
    for dp in others:
        att += [swap(attended[dr][dp], "p", dp) for dr in range(2)]
    ffn_block = ffn // (2 * count_p)
    branch_attn, mid, ffn_input, att_all = call(
        functools.partial(out_kernel, count_p, ffn_block),
        "attn_out",
        [whole, sds((mine, width), F32), whole, whole],
        [hidden, modulation, *att, *uo_w],
        scratch=[pltpu.VMEM((mine, width), F32)],
        after=[down_line],
    )
    gelu_low, slope, d_branch_ffn = call(
        functools.partial(up_kernel, count_p, ffn_block),
        "ffn_up",
        [sds((mine, ffn), BF)] * 2 + [whole],
        [ffn_input, cotangent, modulation, *uo_w],
    )

    down_halves = stage("stage6", halves_of(down_r, down_b), [gelu_low, *down_b])
    down_ends = corners(down_halves)
    fold = down_weight.shape[0] // up_weight.shape[0]
    down_wide = down_weight.shape[1]
    down_sum = Scatter("down", [(down_wide, fold)], count_a // 2)
    uo_sum = Scatter("uo", [(ffn_block, 1), (heads_wide, 1)], count_a // 2)
    qkv_sum = Scatter("qkv", [(heads_wide, 1)] * 3, count_a // 2)

    def split_grad(name, xs, ys, token, fold=1):
        sent = []
        for dp in others:
            token = weight_grad(name, xs, ys, dp, [token], fold)
            sent.append(swap(token, "p", dp))
        own = weight_grad(name, xs, ys, 0, [token], fold)
        return [own, *sent]

    down_parts = split_grad("down_grad", [gelu_low], [d_branch_ffn], down_halves[0], fold)
    down_sum.add([down_parts], (0, 1))

    down_pieces = left_blocks(down_line, down_b) + right_blocks(down_r, down_ends)
    down_w = [assemble(down_pieces, "assemble_down", [down_parts[0]])]
    down_w += [swap(down_w[0], "p", dp) for dp in others]
    token = down_sum.corner([down_w[0]])
    d_up = call(
        functools.partial(d_up_kernel, count_p),
        "d_up",
        [sds((mine, ffn), BF)],
        [d_branch_ffn, slope, *down_w],
        after=[token],
    )[0]
    token = down_sum.side_r([down_sum.side_b([d_up])])
    up_sums = split_grad("up_grad", [ffn_input], [d_up], token)
    token = up_sums[0]
    d_mid, d_branch_attn, sums_mid, *d_att = call(
        functools.partial(mid_back_kernel, count_p, ffn_block),
        "mid_back",
        [whole, whole, sds((3, width), F32)]
        + [sds((mine, heads_wide), BF)] * (2 * count_p),
        [d_up, mid, cotangent, branch_attn, modulation, *uo_w],
        scratch=[pltpu.VMEM((mine, width), F32)],
        after=[token],
    )
    *out_parts, d_ffn_gate = call(
        functools.partial(down_kernel, count_p),
        "ffn_down",
        [sds((block, width), BF)] * 2 + [sds((1, width), F32)],
        [gelu_low, mid, cotangent, modulation, *down_w],
        scratch=[pltpu.VMEM((mine, width), F32)],
        after=[d_branch_attn],
    )
    token = down_sum.line([out_parts[0]])
    out_sums = split_grad("out_grad", [att_all], [d_branch_attn], token)
    uo_sum.add([up_sums, out_sums], (0, 1))

    pairs = heads_wide // PAIR
    d_heads = [
        [d_att[dr]] + [swap(d_att[2 * dp + dr], "p", dp) for dp in others] for dr in range(2)
    ]

    def attend_back(dr, pair, after):
        return call(
            functools.partial(attend_back_kernel, min(512, frames), count_p, pair * PAIR),
            "attend_back",
            [sds((frames, PAIR), BF)] * 3,
            [
                *qkv[dr],
                extra_q,
                extra_k,
                attended[dr][-1],
                cosine,
                sine,
                *attended[dr][:-1],
                *d_heads[dr],
            ],
            after=after,
        )

    def qkv_parts(dr, after):
        return [[weight_grad("qkv_grad", [attn_input], d_qkv[dr], None, after)]]

    d_pairs = [[None] * pairs, [None] * pairs]
    d_qkv = [None, None]

    token = uo_sum.corner()
    d_pairs[1][0] = attend_back(1, 0, [token])
    token = uo_sum.side_b([uo_sum.side_r([d_pairs[1][0][0]])])
    token = down_sum.line_next([token])
    for pair in range(1, pairs):
        d_pairs[1][pair] = attend_back(1, pair, [token])
        token = d_pairs[1][pair][0]
    d_qkv[1] = [d_pairs[1][pair][t] for t in range(3) for pair in range(pairs)]
    qkv_sum.add(qkv_parts(1, [token]), (1,))
    down_grad = down_sum.final([qkv_sum.parts[(0, 1)][0][0][0], *d_heads[0][1:]])[0]
    token = qkv_sum.corner([down_grad])
    token = uo_sum.line([token])
    d_pairs[0][0] = attend_back(0, 0, [token])
    token = uo_sum.line_next([d_pairs[0][0][0]])
    for pair in range(1, pairs):
        d_pairs[0][pair] = attend_back(0, pair, [token])
        token = d_pairs[0][pair][0]
    d_qkv[0] = [d_pairs[0][pair][t] for t in range(3) for pair in range(pairs)]
    qkv_sum.add(qkv_parts(0, [token]), (0,))
    token = qkv_sum.side_b([qkv_sum.side_r([qkv_sum.parts[(0, 0)][0][0][0]])])

    every_d = [*d_qkv[0], *d_qkv[1]]
    pieces = 4
    piece = sds((mine // pieces, width), BF)
    d_own, *d_sent, sums_in = call(
        functools.partial(d_attn_kernel, count_p, len(every_d)),
        "d_attn",
        [whole] + [piece] * (pieces * (count_p - 1)) + [sds((2, width), F32)],
        [*every_d, *qkv_w, hidden_norm],
        after=[token],
    )
    received = [swap(x, "p", 1 + i // pieces) for i, x in enumerate(d_sent)]
    d_mod = call(
        functools.partial(d_modulation_kernel, blocks),
        "d_modulation",
        [sds((devices, ada_cols // PAIR, PAIR), F32)],
        [sums_in, sums_mid, d_ffn_gate],
        vmem=8,
    )[0]
    d_rows = lax.all_to_all(d_mod, every, split_axis=0, concat_axis=0, tiled=True)
    grad_parts = call(
        functools.partial(hidden_back_kernel, pieces),
        "hidden_back",
        [sds((block, width), BF)] * 2,
        [*received, d_own, hidden, d_mid, modulation],
    )

    d_rows = stage("modulation_rows", [d_rows], [grad_parts[0]])[0]
    token = qkv_sum.line([d_rows])
    ada_grad, d_low = call(
        functools.partial(ada_back_kernel, blocks),
        "ada_back",
        [sds(ada_weight.shape, F32), sds((devices, blocks, ada_rows), F32)],
        [low_mine, d_rows, ada_weight],
        vmem=16,
        after=[token],
    )
    token = qkv_sum.line_next([d_low])
    up_grad, out_grad = uo_sum.final([token])
    hidden_out = restore_rows(*out_parts, [up_grad])
    d_low = lax.all_to_all(d_low, every, split_axis=0, concat_axis=0, tiled=True)
    hidden_grad = restore_rows(*grad_parts, [hidden_out])
    query_grad, key_grad, value_grad = qkv_sum.final([hidden_grad])

    time_grad = call(
        functools.partial(time_grad_kernel, blocks, count_p),
        "time_grad",
        [sds((2, width), F32)],
        [d_low, time_embed],
        vmem=8,
        after=[query_grad],
    )[0]
    return (
        hidden_out,
        hidden_grad,
        time_grad,
        ada_grad,
        query_grad,
        key_grad,
        value_grad,
        out_grad,
        up_grad,
        down_grad,
    )


def solution(mesh):
    count_dp, count_sp = mesh.shape["dp"], mesh.shape["sp"]
    fine = Mesh(mesh.devices.reshape(4, count_dp // 4, 2, count_sp // 2), ("a", "b", "r", "p"))
    dp, sp = ("a", "b"), ("r", "p")
    in_specs = (
        (P(dp, sp, None), P(dp, None), P(dp, None)) + (P(dp, sp),) * 7 + (P(dp, sp, None),)
    )
    out_specs = (P(dp, sp, None), P(dp, sp, None), P(dp, None)) + (P(dp, sp),) * 7
    return jax.shard_map(local, mesh=fine, in_specs=in_specs, out_specs=out_specs, check_vma=False)
```
